256 devices in a mesh: seq: 32 (over z, y), tp: 8 (over x, core).
Axes of the slice: x: 4, y: 4, z: 8, core: 2. Of those that a mesh axis runs over, the one named last changes fastest.
Arguments:
- inner_x: bfloat16 [8192, 8192], P('seq', 'tp'), may hold values from -6 to 6
- in_b: bfloat16 [8192, 1024], P('seq', 'tp'), may hold values from -6 to 6
- in_c: bfloat16 [8192, 1024], P('seq', 'tp'), may hold values from -6 to 6
- log_decay: float32 [128, 8192], P('tp', 'seq'), may hold values from -2 to 0
- doc_lengths: int32 [4], replicated, may hold values from 1 to 4096, 8192 in all
- out_grad: bfloat16 [8192, 8192], P('seq', 'tp'), may hold values from -0.0016937256 to 0.0016937256
- w_b: bfloat16 [8192, 1024], P(None, 'tp'), may hold values from -0.09375 to 0.09375
- w_c: bfloat16 [8192, 1024], P(None, 'tp'), may hold values from -0.0625 to 0.0625
Outputs:
- grad_x: bfloat16 [8192, 8192], P('seq', 'tp')
- grad_input: bfloat16 [8192, 8192], P('seq', 'tp')
The draws below stay inside these ranges and needn't reach their ends.
Inputs may be any that keep to these rules, and one draw needn't show every extreme that they name: `doc_lengths`: the lengths sum to 8192; the longest is exactly half of 8192.
All inputs are finite; a program needn't handle non-finite values.
Results may differ from the reference program's by a relative error of at most 0.023.
Values may be sent and summed in bfloat16 or wider, within the bound.
No kernel may reach another device: no remote copies, remote signals or barrier semaphores. Data moves between devices by JAX's collectives and lax.ppermute only.
A program may use at most 128 MiB of HBM per device.

```python
import math
import jax
import jax.numpy as jnp
import numpy as np
from jax import lax

D = 8192
SPACE_HEADS = 128
HEAD_DIM = 64
STATE = 128
GROUPS = 8
SPAN = 128
TOK_DEV = 256
DOCS = 4
SEQUENCE_TOKENS = 8192
INNER = 8192
BC_WIDTH = 1024
N_TP = 8


def draw_log_decay(key, part):
    random_key_series = jax.random.split(jax.random.fold_in(key, 7), 8)
    mixed_share = 0.5
    mixed_heads = jax.random.bernoulli(random_key_series[0], mixed_share, (SPACE_HEADS,))
    device_fast = jax.random.bernoulli(random_key_series[7], 0.5, (SPACE_HEADS, SEQUENCE_TOKENS // TOK_DEV))
    device_fast = jnp.repeat(device_fast, TOK_DEV, axis=1)
    fast_tokens = jnp.logical_and(mixed_heads[:, None], device_fast)
    fast_rate = jnp.exp(jax.random.uniform(random_key_series[1], (SPACE_HEADS,), jnp.float32, math.log(1.0 / 50.0), math.log(1.0 / 30.0)))
    slow_rate = jnp.exp(jax.random.uniform(random_key_series[2], (SPACE_HEADS,), jnp.float32, math.log(0.02), math.log(0.12))) / SEQUENCE_TOKENS
    token_rate = jnp.where(fast_tokens, fast_rate[:, None], slow_rate[:, None])
    block_multiplier = jnp.exp(jax.random.uniform(random_key_series[3], (SPACE_HEADS, SEQUENCE_TOKENS // SPAN), jnp.float32, math.log(0.5), math.log(2.0)))
    block_multiplier = jnp.repeat(block_multiplier, SPAN, axis=1)
    position_multiplier = jax.random.uniform(random_key_series[4], (SPACE_HEADS, SEQUENCE_TOKENS), jnp.float32, 0.5, 2.0)
    surge_position = jax.random.randint(random_key_series[5], (3,), 0, SEQUENCE_TOKENS)
    surge_length = jax.random.uniform(random_key_series[6], (SPACE_HEADS, 1), jnp.float32, 0.22, 0.69)
    surge_matches = jnp.sum((jnp.arange(SEQUENCE_TOKENS)[None, :] == surge_position[:, None]).astype(jnp.float32), axis=0)
    return -(token_rate * block_multiplier * position_multiplier) - surge_length * surge_matches[None, :]


def strengthened(result, rng, source, target, parts, factor):
    owner, partner = [(jnp.arange(result.shape[axis_at]) // (result.shape[axis_at] // parts)).reshape([-1 if axis == axis_at else 1 for axis in range(result.ndim)]) for axis_at in (source, target)]
    chosen = jax.random.permutation(rng, parts)[partner]
    strong = (owner == chosen) | (owner == (partner + parts // 2) % parts)
    return jnp.where(strong, factor * result, result)


def levels(stream_key, dims, cuts, low, top_value):
    loudness, own = 1.0, jax.random.fold_in(stream_key, 6)
    for dim, parts in cuts:
        draws = jnp.exp(jax.random.uniform(jax.random.fold_in(own, dim), (parts,), jnp.float32, low / len(cuts), top_value / len(cuts)))
        loudness = loudness * jnp.repeat(draws, dims[dim] // parts).reshape([-1 if axis == dim else 1 for axis in range(len(dims))])
    return loudness


def profile(number_of, total, limit, skew):
    loads = [(1 << 20) // math.isqrt(rank ** skew) + 1 for rank in range(2, number_of + 1)]
    surplus, given = total - limit - (number_of - 1), [1] * (number_of - 1)
    while surplus > 0:
        movable = [i for i in range(number_of - 1) if given[i] < limit]
        pool, budget = sum([loads[i] for i in movable]), surplus
        for i in movable:
            extra = min(limit - given[i], max(1, budget * loads[i] // pool), surplus)
            given[i] = given[i] + extra
            surplus = surplus - extra
    return np.array([limit] + given)


def ragged_sizes(key, number_of, total, bound, skew):
    if number_of == 2:
        one = jax.random.randint(key, (), max(1, total - bound), min(bound, total - 1) + 1)
        return jnp.stack([one, total - one])
    sizes = jnp.asarray(profile(number_of, total, bound, skew), jnp.int32)
    pairs = (number_of - 1) // 2
    giver, taker = sizes[1:1 + 2 * pairs:2], sizes[2:2 + 2 * pairs:2]
    margin = jnp.minimum(giver - 1, bound - taker)
    passed = jax.random.randint(jax.random.fold_in(key, 1), (pairs,), 0, 1 << 20) % (margin + 1)
    sizes = sizes.at[1:1 + 2 * pairs:2].set(giver - passed).at[2:2 + 2 * pairs:2].set(taker + passed)
    return sizes[jax.random.permutation(jax.random.fold_in(key, 2), number_of)]


def normal_values(rng, shape, width, limit, pieces=(), kind=jnp.bfloat16):
    result = width * jax.random.normal(rng, shape, jnp.float32)
    if pieces:
        result = result * levels(rng, shape, pieces, -0.22, 0.18)
    return jnp.clip(result, -limit, limit).astype(kind)


def bell_draw_with(rng, dims, width, bound, shards, heavy, held_as=jnp.bfloat16):
    array = width * jax.random.normal(rng, dims, jnp.float32)
    if shards:
        array = array * levels(rng, dims, shards, -0.22, 0.18)
    return jnp.clip(strengthened(array, jax.random.fold_in(rng, 3), *heavy), -bound, bound).astype(held_as)


def setup_inputs(seed: int = 0) -> dict:
    key_of = jax.random.split(jax.random.key(seed), 9)
    return {
        "inner_x": normal_values(key_of[0], (SEQUENCE_TOKENS, INNER), 1.0, 6.0, ((0, 32), (1, 8))),
        "in_b": normal_values(key_of[1], (SEQUENCE_TOKENS, BC_WIDTH), 1.0, 6.0, ((0, 32), (1, 8))),
        "in_c": normal_values(key_of[2], (SEQUENCE_TOKENS, BC_WIDTH), 1.0, 6.0, ((0, 32), (1, 8))),
        "log_decay": draw_log_decay(jax.random.fold_in(key_of[8], 71), 0),
        "doc_lengths": ragged_sizes(key_of[4], DOCS, SEQUENCE_TOKENS, SEQUENCE_TOKENS // 2, 2).astype(jnp.int32),
        "out_grad": jnp.clip(jax.random.uniform(key_of[5], (SEQUENCE_TOKENS, INNER), jnp.float32, -0.0016937256, 0.0016937256) * levels(key_of[5], (SEQUENCE_TOKENS, INNER), ((0, 32), (1, 8)), -0.4, 0.0), -0.0016937256, 0.0016937256).astype(jnp.bfloat16),
        "w_b": bell_draw_with(key_of[6], (D, BC_WIDTH), D ** -0.5, 0.09375, ((1, 8),), (1, 0, 8, 2.0)),
        "w_c": normal_values(key_of[7], (D, BC_WIDTH), D ** -0.5, 0.0625, ((1, 8),)),
    }


def doc_ids(doc_lengths, positions):
    doc_ends = jnp.cumsum(doc_lengths)[:-1]
    return jnp.sum((positions[:, None] >= doc_ends[None, :]).astype(jnp.int32), axis=1).astype(jnp.int32)


def span_vectors(log_part, doc_part, doc_prior):
    cumulative = jnp.cumsum(log_part, axis=-1)
    decay_enter = jnp.where(doc_part == doc_prior, jnp.exp(cumulative), 0.0)
    decay_leave = jnp.where(doc_part == doc_part[-1], jnp.exp(cumulative[..., -1:] - cumulative), 0.0)
    decay_total = jnp.where(doc_part[-1] == doc_prior, jnp.exp(cumulative[..., -1]), 0.0)
    return decay_enter, decay_leave, decay_total


def span_within(log_part, doc_part):
    cumulative = jnp.cumsum(log_part, axis=-1)
    span_len = doc_part.shape[0]
    row_ids = jnp.arange(span_len)
    same_doc = (doc_part[:, None] == doc_part[None, :]) & (row_ids[:, None] >= row_ids[None, :])
    log_gaps = cumulative[..., :, None] - cumulative[..., None, :]
    return jnp.where(same_doc, jnp.exp(jnp.where(same_doc, log_gaps, 0.0)), 0.0)


def weigh_rows(x_part, dy_part, decay_enter, decay_leave):
    leave_rows = jnp.transpose(decay_leave, (2, 0, 1))[..., None]
    enter_rows = jnp.transpose(decay_enter, (2, 0, 1))[..., None]
    x_weighted = (x_part.astype(jnp.float32) * leave_rows).astype(jnp.bfloat16)
    dy_weighted = (dy_part.astype(jnp.float32) * enter_rows).astype(jnp.bfloat16)
    return x_weighted, dy_weighted


def span_summary(x_weighted, dy_weighted, b_part, c_part):
    local_state = jnp.einsum("lghp,lgn->ghpn", x_weighted, b_part, preferred_element_type=jnp.float32)
    local_grad = jnp.einsum("lghp,lgn->ghpn", dy_weighted, c_part, preferred_element_type=jnp.float32)
    return local_state, local_grad


def span_grads(x_part, dy_part, b_part, c_part, x_weighted, dy_weighted, within, decay_leave, start_state, end_grad):
    pair_scores = jnp.einsum("ign,jgn->gij", c_part, b_part, preferred_element_type=jnp.float32)
    inner_dots = jnp.einsum("ighp,jghp->ghij", dy_part, x_part, preferred_element_type=jnp.float32)
    score_low = (within * pair_scores[:, None]).astype(jnp.bfloat16)
    leave_rows = jnp.transpose(decay_leave, (2, 0, 1))[..., None]
    end_low = end_grad.astype(jnp.bfloat16)
    start_low = start_state.astype(jnp.bfloat16)
    grad_x = jnp.einsum("ghij,ighp->jghp", score_low, dy_part, preferred_element_type=jnp.float32)
    grad_x = grad_x + jnp.einsum("jgn,ghpn->jghp", b_part, end_low, preferred_element_type=jnp.float32) * leave_rows
    mixed_low = jnp.sum(within * inner_dots, axis=1).astype(jnp.bfloat16)
    grad_c = jnp.einsum("gij,jgn->ign", mixed_low, b_part, preferred_element_type=jnp.float32)
    grad_c = grad_c + jnp.einsum("ighp,ghpn->ign", dy_weighted, start_low, preferred_element_type=jnp.float32)
    grad_b = jnp.einsum("gij,ign->jgn", mixed_low, c_part, preferred_element_type=jnp.float32)
    grad_b = grad_b + jnp.einsum("jghp,ghpn->jgn", x_weighted, end_low, preferred_element_type=jnp.float32)
    return grad_x, grad_b, grad_c


def reference(inner_x, in_b, in_c, log_decay, doc_lengths, out_grad, w_b, w_c):
    per_group = SPACE_HEADS // GROUPS
    span_count = SEQUENCE_TOKENS // SPAN
    x_parts = inner_x.reshape(span_count, SPAN, GROUPS, per_group, HEAD_DIM)
    dy_parts = out_grad.reshape(span_count, SPAN, GROUPS, per_group, HEAD_DIM)
    b_parts = in_b.reshape(span_count, SPAN, GROUPS, STATE)
    c_parts = in_c.reshape(span_count, SPAN, GROUPS, STATE)
    log_parts = jnp.transpose(log_decay.reshape(GROUPS, per_group, span_count, SPAN), (2, 0, 1, 3))
    doc_all = doc_ids(doc_lengths, jnp.arange(SEQUENCE_TOKENS, dtype=jnp.int32))
    doc_parts = doc_all.reshape(span_count, SPAN)
    doc_priors = jnp.concatenate([jnp.full((1,), -1, jnp.int32), doc_parts[:-1, -1].astype(jnp.int32)])
    zero_state = jnp.zeros((GROUPS, per_group, HEAD_DIM, STATE), jnp.float32)

    def forward(carried, span_item):
        x_part, dy_part, b_part, c_part, log_part, doc_part, doc_prior = span_item
        decay_enter, decay_leave, decay_total = span_vectors(log_part, doc_part, doc_prior)
        x_weighted, dy_weighted = weigh_rows(x_part, dy_part, decay_enter, decay_leave)
        local_state, local_grad = span_summary(x_weighted, dy_weighted, b_part, c_part)
        updated = decay_total[..., None, None] * carried + local_state
        return updated, carried

    items = (x_parts, dy_parts, b_parts, c_parts, log_parts, doc_parts, doc_priors)
    unused, start_states = lax.scan(forward, zero_state, items)

    def backward(carried, span_item):
        x_part, dy_part, b_part, c_part, log_part, doc_part, doc_prior, start_state = span_item
        decay_enter, decay_leave, decay_total = span_vectors(log_part, doc_part, doc_prior)
        x_weighted, dy_weighted = weigh_rows(x_part, dy_part, decay_enter, decay_leave)
        within = span_within(log_part, doc_part)
        grads = span_grads(x_part, dy_part, b_part, c_part, x_weighted, dy_weighted, within, decay_leave, start_state, carried)
        local_state, local_grad = span_summary(x_weighted, dy_weighted, b_part, c_part)
        updated = decay_total[..., None, None] * carried + local_grad
        return updated, grads

    unused_grad, outputs = lax.scan(backward, zero_state, items + (start_states,), reverse=True)
    grad_x = outputs[0].reshape(SEQUENCE_TOKENS, SPACE_HEADS * HEAD_DIM).astype(jnp.bfloat16)
    grad_b = outputs[1].reshape(SEQUENCE_TOKENS, GROUPS * STATE).astype(jnp.bfloat16)
    grad_c = outputs[2].reshape(SEQUENCE_TOKENS, GROUPS * STATE).astype(jnp.bfloat16)
    block_width = GROUPS * STATE // N_TP
    summed = jnp.zeros((SEQUENCE_TOKENS, D), jnp.float32)
    for number in range(N_TP):
        low = number * block_width
        high = low + block_width
        partial_value = lax.dot_general(grad_b[:, low:high], w_b[:, low:high], (((1,), (1,)), ((), ())), preferred_element_type=jnp.float32)
        partial_value = partial_value + lax.dot_general(grad_c[:, low:high], w_c[:, low:high], (((1,), (1,)), ((), ())), preferred_element_type=jnp.float32)
        summed = summed + lax.optimization_barrier(partial_value.astype(jnp.bfloat16)).astype(jnp.float32)
    return grad_x, summed.astype(jnp.bfloat16)
```

```python
import functools

import jax
import jax.numpy as jnp
from jax import lax
from jax.experimental import pallas as pl
from jax.experimental.pallas import tpu as pltpu
from jax.sharding import PartitionSpec as P

HEAD_DIM = 64
STATE = 128
SPAN = 128
HEADS = 16
LANES = 128
WIDE = HEADS * HEAD_DIM
PAIRS = WIDE // LANES
LOW = jnp.bfloat16
FULL = jnp.float32
NN = (((1,), (0,)), ((), ()))
NT = (((1,), (1,)), ((), ()))
TN = (((0,), (0,)), ((), ()))
VMEM_BYTES = 48 * 1024 * 1024


def mul(a, b, dims=NN):
    return lax.dot_general(a, b, dims, preferred_element_type=FULL)


def iota(shape, axis):
    return lax.broadcasted_iota(jnp.int32, shape, axis)


def doc_of(positions, ends):
    return sum((positions >= end).astype(jnp.int32) for end in ends)


def doc_ends(lengths_ref):
    first = lengths_ref[0]
    second = first + lengths_ref[1]
    return (first, second, second + lengths_ref[2])


def token_vectors(log_ref, lengths_ref):
    tokens = log_ref.shape[1]
    first_row = lax.axis_index("seq") * tokens
    ends = doc_ends(lengths_ref)
    upper = (iota((tokens, tokens), 0) <= iota((tokens, tokens), 1)).astype(FULL)
    cumulative = lax.dot_general(
        log_ref[...], upper, NN, precision=lax.Precision.HIGHEST, preferred_element_type=FULL
    )
    docs = doc_of(first_row + iota((HEADS, tokens), 1), ends)
    prior = jnp.where(first_row > 0, doc_of(first_row - 1, ends), -1)
    last = doc_of(first_row + tokens - 1, ends)
    cum_last = cumulative[:, tokens - 1 :]
    enter = jnp.where(docs == prior, jnp.exp(cumulative), 0.0)
    leave = jnp.where(docs == last, jnp.exp(cum_last - cumulative), 0.0)
    total = jnp.where(last == prior, jnp.exp(cum_last), 0.0)
    return first_row, ends, cumulative, docs, enter, leave, total


def split_columns(rows):
    high = rows.astype(LOW).astype(FULL)
    both = jnp.concatenate([high, rows - high], axis=0)
    return both.T.astype(LOW)


def spread(columns, low, width):
    head = (low + iota((2 * HEADS, width), 1)) // HEAD_DIM
    pick = (head == iota((2 * HEADS, width), 0) % HEADS).astype(FULL).astype(LOW)
    return mul(columns, pick)


def summary_kernel(lengths_ref, x_ref, dy_ref, b_ref, c_ref, log_ref, out_ref):
    slices = out_ref.shape[0]
    rows = WIDE // slices
    _, _, _, _, enter, leave, total = token_vectors(log_ref, lengths_ref)
    enter_cols = split_columns(enter)
    leave_cols = split_columns(leave)
    b, c = b_ref[...], c_ref[...]
    width = 2 * LANES
    for chunk in range(WIDE // width):
        low = chunk * width
        span = slice(low, low + width)
        at = slice(low // rows, (low + width) // rows)
        weighted = (x_ref[:, span].astype(FULL) * spread(leave_cols, low, width)).astype(LOW)
        out_ref[at, 0:rows, :] = mul(weighted, b, TN).astype(LOW).reshape(width // rows, rows, STATE)
        weighted = (dy_ref[:, span].astype(FULL) * spread(enter_cols, low, width)).astype(LOW)
        out_ref[at, rows : 2 * rows, :] = (
            mul(weighted, c, TN).astype(LOW).reshape(width // rows, rows, STATE)
        )
    total = jnp.broadcast_to(total, (HEADS, STATE))
    high = total.astype(LOW).astype(FULL)
    per_head = slices // HEADS
    for head in range(HEADS):
        rest = jnp.broadcast_to((total - high)[head : head + 1], (8, STATE))
        tile = jnp.where(iota((8, STATE), 0) == 0, high[head : head + 1], rest).astype(LOW)
        for part in range(per_head):
            out_ref[head * per_head + part, 2 * rows : 2 * rows + 8, :] = tile


def scan_kernel(in_ref, out_ref):
    devices, rows = out_ref.shape[0], out_ref.shape[1] // 2
    decays = []
    for at in range(devices):
        pair = in_ref[at, 2 * rows : 2 * rows + 8, :].astype(FULL)
        decays.append(pair[0:1] + pair[1:2])
    state = jnp.zeros((rows, STATE), FULL)
    for at in range(devices):
        out_ref[at, 0:rows, :] = state.astype(LOW)
        state = decays[at] * state + in_ref[at, 0:rows, :].astype(FULL)
    state = jnp.zeros((rows, STATE), FULL)
    for at in reversed(range(devices)):
        out_ref[at, rows : 2 * rows, :] = state.astype(LOW)
        state = decays[at] * state + in_ref[at, rows : 2 * rows, :].astype(FULL)


def grads_kernel(
    lengths_ref, x_ref, dy_ref, b_ref, c_ref, log_ref, edge_ref, grad_x_ref, grad_bc_ref
):
    slices, rows = edge_ref.shape[0], edge_ref.shape[1] // 2
    first_row, ends, cumulative, docs, enter, leave, _ = token_vectors(log_ref, lengths_ref)
    cum_cols = cumulative.T
    enter_cols, leave_cols = split_columns(enter), split_columns(leave)
    middle = doc_of(first_row + SPAN - 1, ends)
    cum_middle = cumulative[:, SPAN - 1 : SPAN]
    leave_first = jnp.where(
        docs[:, :SPAN] == middle, jnp.exp(cum_middle - cumulative[:, :SPAN]), 0.0
    )
    enter_second = jnp.where(
        docs[:, SPAN:] == middle, jnp.exp(cumulative[:, SPAN:] - cum_middle), 0.0
    )
    leave_first, enter_second = split_columns(leave_first), split_columns(enter_second)
    b, c = b_ref[...], c_ref[...]
    scores = mul(b, c, NT)
    cross_scores = scores[:SPAN, SPAN:].astype(LOW)
    is_left = iota((SPAN, LANES), 1) < HEAD_DIM
    masks = []
    for number in range(2):
        base = first_row + number * SPAN
        same = doc_of(base + iota((SPAN, SPAN), 0), ends) == doc_of(
            base + iota((SPAN, SPAN), 1), ends
        )
        masks.append(same & (iota((SPAN, SPAN), 0) <= iota((SPAN, SPAN), 1)))

    def halves(value):
        zero = jnp.zeros_like(value)
        return jnp.concatenate(
            [jnp.where(is_left, value, zero), jnp.where(is_left, zero, value)], axis=0
        )

    mixed = [jnp.zeros((SPAN, SPAN), FULL), jnp.zeros((SPAN, SPAN), FULL)]
    mixed_cross = jnp.zeros((SPAN, SPAN), FULL)
    grad_b = jnp.zeros((2 * SPAN, STATE), FULL)
    grad_c = jnp.zeros((2 * SPAN, STATE), FULL)
    for pair in range(PAIRS):
        low = pair * LANES
        x, dy = x_ref[:, low : low + LANES], dy_ref[:, low : low + LANES]
        at = slice(low // rows, (low + LANES) // rows)
        start = edge_ref[at, 0:rows, :].reshape(LANES, STATE)
        end = edge_ref[at, rows : 2 * rows, :].reshape(LANES, STATE)
        leave_wide = spread(leave_cols, low, LANES)
        weighted = (x.astype(FULL) * leave_wide).astype(LOW)
        grad_b += mul(weighted, end)
        weighted = (dy.astype(FULL) * spread(enter_cols, low, LANES)).astype(LOW)
        grad_c += mul(weighted, start)
        grad_x = leave_wide * mul(b, end, NT)
        first_wide = spread(leave_first, low, LANES)
        x_first = (x[:SPAN].astype(FULL) * first_wide).astype(LOW)
        dy_second = (dy[SPAN:].astype(FULL) * spread(enter_second, low, LANES)).astype(LOW)
        mixed_cross += mul(x_first, dy_second, NT)
        pieces = [first_wide * mul(cross_scores, dy_second), 0.0]
        for number in range(2):
            span = slice(number * SPAN, (number + 1) * SPAN)
            inner = mul(halves(x[span]), dy[span], NT)
            low_scores = []
            for side in range(2):
                head = 2 * pair + side
                gaps = cumulative[head : head + 1, span] - cum_cols[span, head : head + 1]
                within = jnp.exp(jnp.where(masks[number], gaps, -1e30))
                mixed[number] += within * inner[side * SPAN : (side + 1) * SPAN]
                low_scores.append((within * scores[span, span]).astype(LOW))
            pieces[number] += mul(jnp.concatenate(low_scores, axis=1), halves(dy[span]))
            grad_x_ref[span, low : low + LANES] = (grad_x[span] + pieces[number]).astype(LOW)
    nothing = jnp.zeros((SPAN, SPAN), FULL)
    table = jnp.concatenate(
        [
            jnp.concatenate([mixed[0], mixed_cross], axis=1),
            jnp.concatenate([nothing, mixed[1]], axis=1),
        ],
        axis=0,
    )
    grad_bc_ref[:, :STATE] = (grad_b + mul(table.astype(LOW), c)).astype(LOW)
    grad_bc_ref[:, STATE:] = (grad_c + mul(table.T.astype(LOW), b)).astype(LOW)


def call(body, out_shape, specs, flops, moved):
    return pl.pallas_call(
        body,
        out_shape=out_shape,
        in_specs=specs,
        out_specs=jax.tree.map(lambda _: pl.BlockSpec(memory_space=pltpu.VMEM), out_shape),
        compiler_params=pltpu.CompilerParams(vmem_limit_bytes=VMEM_BYTES),
        cost_estimate=pl.CostEstimate(flops=flops, bytes_accessed=moved, transcendentals=0),
    )


def per_device(inner_x, in_b, in_c, log_decay, doc_lengths, out_grad, w_b, w_c):
    tokens = inner_x.shape[0]
    devices = lax.axis_size("seq")
    rows = WIDE // devices
    small = pl.BlockSpec(memory_space=pltpu.SMEM)
    block = pl.BlockSpec(memory_space=pltpu.VMEM)
    local = (doc_lengths, inner_x, out_grad, in_b, in_c, log_decay)
    summary = call(
        summary_kernel,
        jax.ShapeDtypeStruct((devices, 2 * rows + 8, STATE), LOW),
        [small] + [block] * 5,
        2 * 10**8,
        2 * 10**6,
    )(*local)
    summary = lax.all_to_all(summary, "seq", 0, 0)
    edges = call(
        scan_kernel,
        jax.ShapeDtypeStruct((devices, 2 * rows, STATE), LOW),
        [block],
        10**6,
        10**6,
    )(summary)
    edges = lax.all_to_all(edges, "seq", 0, 0)
    grad_x, grad_bc = call(
        grads_kernel,
        (
            jax.ShapeDtypeStruct((tokens, WIDE), LOW),
            jax.ShapeDtypeStruct((tokens, 2 * STATE), LOW),
        ),
        [small] + [block] * 6,
        4 * 10**8,
        3 * 10**6,
    )(*local, edges)
    partial_value = lax.dot_general(grad_bc[:, :STATE], w_b, NT, preferred_element_type=FULL)
    partial_value = partial_value + lax.dot_general(
        grad_bc[:, STATE:], w_c, NT, preferred_element_type=FULL
    )
    grad_input = lax.psum_scatter(
        partial_value.astype(LOW), "tp", scatter_dimension=1, tiled=True
    )
    return grad_x, grad_input


def solution(mesh):
    placed = (
        P("seq", "tp"),
        P("seq", "tp"),
        P("seq", "tp"),
        P("tp", "seq"),
        P(),
        P("seq", "tp"),
        P(None, "tp"),
        P(None, "tp"),
    )
    return jax.shard_map(
        per_device,
        mesh=mesh,
        in_specs=placed,
        out_specs=(P("seq", "tp"), P("seq", "tp")),
        check_vma=False,
    )
```

```python
import functools

import jax
import jax.numpy as jnp
from jax import lax
from jax.experimental import pallas as pl
from jax.experimental.pallas import tpu as pltpu
from jax.sharding import PartitionSpec as P

HEAD_DIM = 64
STATE = 128
SPAN = 128
HEADS = 16
LANES = 128
WIDE = HEADS * HEAD_DIM
PAIRS = WIDE // LANES
CORES = 2
LOW = jnp.bfloat16
FULL = jnp.float32
NN = (((1,), (0,)), ((), ()))
NT = (((1,), (1,)), ((), ()))
TN = (((0,), (0,)), ((), ()))
MIB = 1024 * 1024
LARGE_VMEM = 56 * MIB


def mul(a, b, dims=NN):
    return lax.dot_general(a, b, dims, preferred_element_type=FULL)


def iota(shape, axis):
    return lax.broadcasted_iota(jnp.int32, shape, axis)


def doc_of(positions, ends):
    return sum((positions >= end).astype(jnp.int32) for end in ends)


def doc_ends(lengths_ref):
    first = lengths_ref[0]
    second = first + lengths_ref[1]
    return (first, second, second + lengths_ref[2])


def token_vectors(log_ref, lengths_ref):
    tokens = log_ref.shape[1]
    first_row = lax.axis_index("seq") * tokens
    ends = doc_ends(lengths_ref)
    upper = (iota((tokens, tokens), 0) <= iota((tokens, tokens), 1)).astype(FULL)
    cumulative = lax.dot_general(
        log_ref[...], upper, NN, precision=lax.Precision.HIGHEST, preferred_element_type=FULL
    )
    docs = doc_of(first_row + iota((HEADS, tokens), 1), ends)
    prior = jnp.where(first_row > 0, doc_of(first_row - 1, ends), -1)
    last = doc_of(first_row + tokens - 1, ends)
    cum_last = cumulative[:, tokens - 1 :]
    enter = jnp.where(docs == prior, jnp.exp(cumulative), 0.0)
    leave = jnp.where(docs == last, jnp.exp(cum_last - cumulative), 0.0)
    total = jnp.where(last == prior, jnp.exp(cum_last), 0.0)
    return first_row, ends, cumulative, docs, enter, leave, total


def split_columns(rows):
    high = rows.astype(LOW).astype(FULL)
    both = jnp.concatenate([high, rows - high], axis=0)
    return both.T.astype(LOW)


def spread(columns, low, width):
    head = (low + iota((2 * HEADS, width), 1)) // HEAD_DIM
    pick = (head == iota((2 * HEADS, width), 0) % HEADS).astype(FULL).astype(LOW)
    return mul(columns, pick)


def fetch(pairs, sems):
    copies = [
        pltpu.make_async_copy(source, target, sems.at[at])
        for at, (source, target) in enumerate(pairs)
    ]
    for copy in copies:
        copy.start()
    return copies


def summary_kernel(
    lengths_hbm,
    log_hbm,
    x_hbm,
    b_hbm,
    dy_hbm,
    c_hbm,
    w_b_hbm,
    w_c_hbm,
    out_ref,
    *refs,
):
    sent_refs = refs[:-8]
    lengths_ref, log_ref, x_ref, b_ref, dy_ref, c_ref, sems, sent_sems = refs[-8:]
    loads = fetch(
        [
            (lengths_hbm, lengths_ref),
            (log_hbm, log_ref),
            (x_hbm, x_ref),
            (b_hbm, b_ref),
            (dy_hbm, dy_ref),
            (c_hbm, c_ref),
        ],
        sems,
    )
    columns = sent_refs[0].shape[0]
    steps = len(sent_refs) // CORES
    me = lax.axis_index("tp")
    core = lax.rem(me, CORES)
    pairs = []
    for at, sent_ref in enumerate(sent_refs):
        half = 1 - core if at < steps else core
        target = lax.rem(me // CORES + at % steps + 1, steps + 1)
        from_row = pl.ds(pl.multiple_of((target * CORES + half) * columns, columns), columns)
        pairs.append((w_b_hbm.at[from_row, :], sent_ref.at[:, pl.ds(0, STATE)]))
        pairs.append((w_c_hbm.at[from_row, :], sent_ref.at[:, pl.ds(STATE, STATE)]))
    sends = fetch(pairs, sent_sems)
    slices = out_ref.shape[0]
    rows = WIDE // slices
    loads[0].wait()
    loads[1].wait()
    _, _, _, _, enter, leave, total = token_vectors(log_ref, lengths_ref)
    enter_cols = split_columns(enter)
    leave_cols = split_columns(leave)
    width = 2 * LANES
    for side, (wide_ref, narrow_ref, cols) in enumerate(
        ((x_ref, b_ref, leave_cols), (dy_ref, c_ref, enter_cols))
    ):
        loads[2 + 2 * side].wait()
        loads[3 + 2 * side].wait()
        narrow = narrow_ref[...]
        for chunk in range(WIDE // width):
            low = chunk * width
            at = slice(low // rows, (low + width) // rows)
            weighted = wide_ref[:, low : low + width].astype(FULL) * spread(cols, low, width)
            product = mul(weighted.astype(LOW), narrow, TN).astype(LOW)
            out_ref[at, side * rows : (side + 1) * rows, :] = product.reshape(
                width // rows, rows, STATE
            )
    total = jnp.broadcast_to(total, (HEADS, STATE))
    high = total.astype(LOW).astype(FULL)
    per_head = slices // HEADS
    for head in range(HEADS):
        rest = jnp.broadcast_to((total - high)[head : head + 1], (8, STATE))
        tile = jnp.where(iota((8, STATE), 0) == 0, high[head : head + 1], rest).astype(LOW)
        for part in range(per_head):
            out_ref[head * per_head + part, 2 * rows : 2 * rows + 8, :] = tile
    for send in sends:
        send.wait()


def scan_kernel(in_ref, *refs):
    out_ref = refs[-1]
    devices, rows = out_ref.shape[0], out_ref.shape[1] // 2
    decays = []
    for at in range(devices):
        pair = in_ref[at, 2 * rows : 2 * rows + 8, :].astype(FULL)
        decays.append(pair[0:1] + pair[1:2])
    state = jnp.zeros((rows, STATE), FULL)
    for at in range(devices):
        out_ref[at, 0:rows, :] = state.astype(LOW)
        state = decays[at] * state + in_ref[at, 0:rows, :].astype(FULL)
    state = jnp.zeros((rows, STATE), FULL)
    for at in reversed(range(devices)):
        out_ref[at, rows : 2 * rows, :] = state.astype(LOW)
        state = decays[at] * state + in_ref[at, rows : 2 * rows, :].astype(FULL)


def local_kernel(
    lengths_hbm,
    log_hbm,
    x_hbm,
    b_hbm,
    dy_hbm,
    c_hbm,
    grad_x_ref,
    grad_bc_ref,
    x_weighted_ref,
    dy_weighted_ref,
    leave_ref,
    lengths_ref,
    log_ref,
    x_ref,
    b_ref,
    dy_ref,
    c_ref,
    sems,
):
    loads = fetch(
        [
            (lengths_hbm, lengths_ref),
            (log_hbm, log_ref),
            (x_hbm, x_ref),
            (b_hbm, b_ref),
            (dy_hbm, dy_ref),
            (c_hbm, c_ref),
        ],
        sems,
    )
    for load in loads:
        load.wait()
    first_row, ends, cumulative, docs, enter, leave, _ = token_vectors(log_ref, lengths_ref)
    enter_cols, leave_cols = split_columns(enter), split_columns(leave)
    leave_ref[...] = leave_cols
    cum_cols = cumulative.T
    middle = doc_of(first_row + SPAN - 1, ends)
    cum_middle = cumulative[:, SPAN - 1 : SPAN]
    leave_first = jnp.where(
        docs[:, :SPAN] == middle, jnp.exp(cum_middle - cumulative[:, :SPAN]), 0.0
    )
    enter_second = jnp.where(
        docs[:, SPAN:] == middle, jnp.exp(cumulative[:, SPAN:] - cum_middle), 0.0
    )
    leave_first, enter_second = split_columns(leave_first), split_columns(enter_second)
    b, c = b_ref[...], c_ref[...]
    scores = mul(b, c, NT)
    cross_scores = scores[:SPAN, SPAN:].astype(LOW)
    is_left = iota((SPAN, LANES), 1) < HEAD_DIM
    masks = []
    for number in range(2):
        base = first_row + number * SPAN
        same = doc_of(base + iota((SPAN, SPAN), 0), ends) == doc_of(
            base + iota((SPAN, SPAN), 1), ends
        )
        masks.append(same & (iota((SPAN, SPAN), 0) <= iota((SPAN, SPAN), 1)))

    def halves(value):
        zero = jnp.zeros_like(value)
        return jnp.concatenate(
            [jnp.where(is_left, value, zero), jnp.where(is_left, zero, value)], axis=0
        )

    mixed = [jnp.zeros((SPAN, SPAN), FULL), jnp.zeros((SPAN, SPAN), FULL)]
    mixed_cross = jnp.zeros((SPAN, SPAN), FULL)
    for pair in range(PAIRS):
        low = pair * LANES
        x, dy = x_ref[:, low : low + LANES], dy_ref[:, low : low + LANES]
        for wide, cols, weighted_ref in (
            (x, leave_cols, x_weighted_ref),
            (dy, enter_cols, dy_weighted_ref),
        ):
            weighted = (wide.astype(FULL) * spread(cols, low, LANES)).astype(LOW)
            weighted_ref[:, low : low + LANES] = weighted
        first_wide = spread(leave_first, low, LANES)
        x_first = (x[:SPAN].astype(FULL) * first_wide).astype(LOW)
        dy_second = (dy[SPAN:].astype(FULL) * spread(enter_second, low, LANES)).astype(LOW)
        mixed_cross += mul(x_first, dy_second, NT)
        pieces = [first_wide * mul(cross_scores, dy_second), 0.0]
        for number in range(2):
            span = slice(number * SPAN, (number + 1) * SPAN)
            inner = mul(halves(x[span]), dy[span], NT)
            low_scores = []
            for side in range(2):
                head = 2 * pair + side
                gaps = cumulative[head : head + 1, span] - cum_cols[span, head : head + 1]
                within = jnp.exp(jnp.where(masks[number], gaps, -1e30))
                mixed[number] += within * inner[side * SPAN : (side + 1) * SPAN]
                low_scores.append((within * scores[span, span]).astype(LOW))
            grad_x_ref[span, low : low + LANES] = pieces[number] + mul(
                jnp.concatenate(low_scores, axis=1), halves(dy[span])
            )
    nothing = jnp.zeros((SPAN, SPAN), FULL)
    table = jnp.concatenate(
        [
            jnp.concatenate([mixed[0], mixed_cross], axis=1),
            jnp.concatenate([nothing, mixed[1]], axis=1),
        ],
        axis=0,
    )
    grad_bc_ref[:, :STATE] = mul(table.astype(LOW), c)
    grad_bc_ref[:, STATE:] = mul(table.T.astype(LOW), b)


def grad_bc_kernel(x_weighted_ref, dy_weighted_ref, local_ref, edge_ref, *refs):
    out_ref = refs[-1]
    rows = edge_ref.shape[1] // 2
    start = edge_ref[:, 0:rows, :].reshape(WIDE, STATE)
    end = edge_ref[:, rows : 2 * rows, :].reshape(WIDE, STATE)
    out_ref[:, :STATE] = (local_ref[:, :STATE] + mul(x_weighted_ref[...], end)).astype(LOW)
    out_ref[:, STATE:] = (local_ref[:, STATE:] + mul(dy_weighted_ref[...], start)).astype(LOW)


def grad_x_kernel(b_ref, leave_ref, local_ref, edge_ref, out_ref):
    rows = edge_ref.shape[1] // 2
    width = 2 * LANES
    for chunk in range(WIDE // width):
        low = chunk * width
        at = slice(low // rows, (low + width) // rows)
        end = edge_ref[at, rows : 2 * rows, :].reshape(width, STATE)
        later = spread(leave_ref[...], low, width) * mul(b_ref[...], end, NT)
        out_ref[:, low : low + width] = (local_ref[:, low : low + width] + later).astype(LOW)


def project_kernel(w_b_hbm, w_c_hbm, *refs, sibling):
    terms = (len(refs) - 3) // 2
    grads, weights = refs[:terms], refs[terms : 2 * terms - 1]
    out_ref, grads_ref, weights_ref, sems = refs[-4:]
    columns = out_ref.shape[1]
    me = lax.axis_index("tp")
    core = lax.rem(me, CORES)
    half = 1 - core if sibling else core
    from_row = pl.ds(pl.multiple_of((me - core + half) * columns, columns), columns)
    pairs = [
        (w_b_hbm.at[from_row, :], weights_ref.at[0, :, pl.ds(0, STATE)]),
        (w_c_hbm.at[from_row, :], weights_ref.at[0, :, pl.ds(STATE, STATE)]),
    ]
    for at in range(terms):
        pairs.append((grads[at], grads_ref.at[at]))
        if at:
            pairs.append((weights[at - 1], weights_ref.at[at]))
    loads = fetch(pairs, sems)
    total = 0.0
    for at in range(terms):
        for load in loads[:3] if at == 0 else loads[1 + 2 * at : 3 + 2 * at]:
            load.wait()
        total += mul(grads_ref[at], weights_ref[at], NT)
    out_ref[...] = total.astype(out_ref.dtype)


BLOCK = pl.BlockSpec(memory_space=pltpu.VMEM)
WHERE = pl.BlockSpec(memory_space=pl.ANY)
HBM = pl.BlockSpec(memory_space=pltpu.HBM)


def call(body, out_shape, specs, vmem, flops, moved, out_specs=BLOCK, scratch=()):
    return pl.pallas_call(
        body,
        out_shape=out_shape,
        in_specs=specs,
        out_specs=out_specs,
        scratch_shapes=scratch,
        compiler_params=pltpu.CompilerParams(vmem_limit_bytes=vmem),
        cost_estimate=pl.CostEstimate(flops=flops, bytes_accessed=moved, transcendentals=0),
    )


def along_x(value, step):
    devices = lax.axis_size("tp")
    return lax.ppermute(
        value, "tp", [(at, (at + CORES * step) % devices) for at in range(devices)]
    )


def per_device(inner_x, in_b, in_c, log_decay, doc_lengths, out_grad, w_b, w_c):
    tokens = inner_x.shape[0]
    devices = lax.axis_size("seq")
    steps = lax.axis_size("tp") // CORES - 1
    rows = WIDE // devices
    columns = w_b.shape[0] // lax.axis_size("tp")
    local = (doc_lengths, log_decay, inner_x, in_b, out_grad, in_c)
    dma = pltpu.SemaphoreType.DMA
    shape = jax.ShapeDtypeStruct
    held = [pltpu.SMEM(doc_lengths.shape, doc_lengths.dtype)] + [
        pltpu.VMEM(a.shape, a.dtype) for a in local[1:]
    ]
    sends = CORES * steps
    summary, *sent = call(
        summary_kernel,
        [shape((devices, 2 * rows + 8, STATE), LOW)]
        + [shape((columns, 2 * STATE), LOW)] * sends,
        [HBM] * 8,
        LARGE_VMEM,
        2 * 10**8,
        8 * 10**6,
        [BLOCK] + [HBM] * sends,
        held + [dma((6,)), dma((2 * sends,))],
    )(*local, w_b, w_c)
    weights = [along_x(value, at % steps + 1) for at, value in enumerate(sent)]
    summary = lax.all_to_all(summary, "seq", 0, 0)
    edges = call(
        scan_kernel,
        shape((devices, 2 * rows, STATE), LOW),
        [BLOCK] + [WHERE] * steps,
        4 * MIB,
        10**6,
        10**6,
    )(summary, *weights[:steps])
    edges = lax.all_to_all(edges, "seq", 0, 0)
    grad_x, grad_bc, x_weighted, dy_weighted, leave_cols = call(
        local_kernel,
        [
            shape((tokens, WIDE), FULL),
            shape((tokens, 2 * STATE), FULL),
            shape((tokens, WIDE), LOW),
            shape((tokens, WIDE), LOW),
            shape((tokens, 2 * HEADS), LOW),
        ],
        [HBM] * 6,
        16 * MIB,
        4 * 10**8,
        3 * 10**6,
        [BLOCK] * 5,
        held + [dma((6,))],
    )(*local)
    grad_bc = call(
        grad_bc_kernel,
        shape((tokens, 2 * STATE), LOW),
        [BLOCK] * 4 + [WHERE] * steps,
        8 * MIB,
        2 * 10**8,
        10**6,
    )(x_weighted, dy_weighted, grad_bc, edges, *weights[steps:])
    others = [along_x(grad_bc, step + 1) for step in range(steps)]
    grad_x = call(
        grad_x_kernel, shape((tokens, WIDE), LOW), [BLOCK] * 4, 8 * MIB, 10**8, 3 * 10**6
    )(in_b, leave_cols, grad_x, edges)

    def project(sibling, kind):
        terms = steps + 1
        return call(
            functools.partial(project_kernel, sibling=sibling),
            shape((tokens, columns), kind),
            [HBM] * (2 * terms + 1),
            LARGE_VMEM,
            6 * 10**8,
            3 * 10**6,
            BLOCK,
            [
                pltpu.VMEM((terms, tokens, 2 * STATE), LOW),
                pltpu.VMEM((terms, columns, 2 * STATE), LOW),
                dma((2 * terms + 1,)),
            ],
        )(w_b, w_c, grad_bc, *others, *(weights[:steps] if sibling else weights[steps:]))

    partner = [(at, at ^ 1) for at in range(lax.axis_size("tp"))]
    received = lax.ppermute(project(True, LOW), "tp", partner)
    grad_input = (project(False, FULL) + received.astype(FULL)).astype(LOW)
    return grad_x, grad_input


def solution(mesh):
    placed = (
        P("seq", "tp"),
        P("seq", "tp"),
        P("seq", "tp"),
        P("tp", "seq"),
        P(),
        P("seq", "tp"),
        P(None, "tp"),
        P(None, "tp"),
    )
    return jax.shard_map(
        per_device,
        mesh=mesh,
        in_specs=placed,
        out_specs=(P("seq", "tp"), P("seq", "tp")),
        check_vma=False,
    )
```

```python
import functools

import jax
import jax.numpy as jnp
from jax import lax
from jax.experimental import pallas as pl
from jax.experimental.pallas import tpu as pltpu
from jax.sharding import PartitionSpec as P

HEAD_DIM = 64
STATE = 128
SPAN = 128
HEADS = 16
LANES = 128
WIDE = HEADS * HEAD_DIM
PAIRS = WIDE // LANES
CORES = 2
ROUTE = ((1, True), (1, False), (2, True), (3, True), (3, False), (2, False))
LOW = jnp.bfloat16
FULL = jnp.float32
NN = (((1,), (0,)), ((), ()))
NT = (((1,), (1,)), ((), ()))
TN = (((0,), (0,)), ((), ()))
MIB = 1024 * 1024
LARGE_VMEM = 56 * MIB


def mul(a, b, dims=NN):
    return lax.dot_general(a, b, dims, preferred_element_type=FULL)


def iota(shape, axis):
    return lax.broadcasted_iota(jnp.int32, shape, axis)


def doc_of(positions, ends):
    return sum((positions >= end).astype(jnp.int32) for end in ends)


def doc_ends(lengths_ref):
    first = lengths_ref[0]
    second = first + lengths_ref[1]
    return (first, second, second + lengths_ref[2])


def token_vectors(log_ref, lengths_ref):
    tokens = log_ref.shape[1]
    first_row = lax.axis_index("seq") * tokens
    ends = doc_ends(lengths_ref)
    upper = (iota((tokens, tokens), 0) <= iota((tokens, tokens), 1)).astype(FULL)
    cumulative = lax.dot_general(
        log_ref[...], upper, NN, precision=lax.Precision.HIGHEST, preferred_element_type=FULL
    )
    docs = doc_of(first_row + iota((HEADS, tokens), 1), ends)
    prior = jnp.where(first_row > 0, doc_of(first_row - 1, ends), -1)
    last = doc_of(first_row + tokens - 1, ends)
    cum_last = cumulative[:, tokens - 1 :]
    enter = jnp.where(docs == prior, jnp.exp(cumulative), 0.0)
    leave = jnp.where(docs == last, jnp.exp(cum_last - cumulative), 0.0)
    total = jnp.where(last == prior, jnp.exp(cum_last), 0.0)
    return first_row, ends, cumulative, docs, enter, leave, total


def split_columns(rows):
    high = rows.astype(LOW).astype(FULL)
    both = jnp.concatenate([high, rows - high], axis=0)
    return both.T.astype(LOW)


def spread(columns, low, width):
    head = (low + iota((2 * HEADS, width), 1)) // HEAD_DIM
    pick = (head == iota((2 * HEADS, width), 0) % HEADS).astype(FULL).astype(LOW)
    return mul(columns, pick)


def fetch(pairs, sems):
    copies = [
        pltpu.make_async_copy(source, target, sems.at[at])
        for at, (source, target) in enumerate(pairs)
    ]
    for copy in copies:
        copy.start()
    return copies


def summary_kernel(
    lengths_hbm,
    log_hbm,
    x_hbm,
    b_hbm,
    dy_hbm,
    c_hbm,
    w_b_hbm,
    w_c_hbm,
    out_ref,
    *refs,
):
    sent_refs = refs[:-10]
    lengths_ref, log_ref, x_ref, b_ref, dy_ref, c_ref, passing_ref = refs[-10:-3]
    sems, passing_sems, sent_sems = refs[-3:]
    loads = fetch(
        [
            (lengths_hbm, lengths_ref),
            (log_hbm, log_ref),
            (x_hbm, x_ref),
            (b_hbm, b_ref),
            (dy_hbm, dy_ref),
            (c_hbm, c_ref),
        ],
        sems,
    )
    columns = passing_ref.shape[1]
    me = lax.axis_index("tp")
    core, chips = lax.rem(me, CORES), lax.axis_size("tp") // CORES
    pairs = []
    for at, (step, sibling) in enumerate(ROUTE):
        half = 1 - core if sibling else core
        target = lax.rem(me // CORES + step, chips)
        from_row = pl.ds(pl.multiple_of((target * CORES + half) * columns, columns), columns)
        pairs.append((w_b_hbm.at[from_row, :], passing_ref.at[at, :, pl.ds(0, STATE)]))
        pairs.append((w_c_hbm.at[from_row, :], passing_ref.at[at, :, pl.ds(STATE, STATE)]))
    passing = fetch(pairs, passing_sems)
    slices = out_ref.shape[0]
    rows = WIDE // slices
    loads[0].wait()
    loads[1].wait()
    _, _, _, _, enter, leave, total = token_vectors(log_ref, lengths_ref)
    enter_cols = split_columns(enter)
    leave_cols = split_columns(leave)
    sends = []
    width = 2 * LANES
    for side, (wide_ref, narrow_ref, cols) in enumerate(
        ((x_ref, b_ref, leave_cols), (dy_ref, c_ref, enter_cols))
    ):
        loads[2 + 2 * side].wait()
        loads[3 + 2 * side].wait()
        if side:
            for copy in passing:
                copy.wait()
            sends = fetch(
                [
                    (passing_ref.at[at], sent_refs[at // 3].at[pl.ds(at % 3 * columns, columns), :])
                    for at in range(len(ROUTE))
                ],
                sent_sems,
            )
        narrow = narrow_ref[...]
        for chunk in range(WIDE // width):
            low = chunk * width
            at = slice(low // rows, (low + width) // rows)
            weighted = wide_ref[:, low : low + width].astype(FULL) * spread(cols, low, width)
            product = mul(weighted.astype(LOW), narrow, TN).astype(LOW)
            out_ref[at, side * rows : (side + 1) * rows, :] = product.reshape(
                width // rows, rows, STATE
            )
    total = jnp.broadcast_to(total, (HEADS, STATE))
    high = total.astype(LOW).astype(FULL)
    per_head = slices // HEADS
    for head in range(HEADS):
        rest = jnp.broadcast_to((total - high)[head : head + 1], (8, STATE))
        tile = jnp.where(iota((8, STATE), 0) == 0, high[head : head + 1], rest).astype(LOW)
        for part in range(per_head):
            out_ref[head * per_head + part, 2 * rows : 2 * rows + 8, :] = tile
    for send in sends:
        send.wait()


def scan_kernel(in_ref, out_ref):
    devices, rows = out_ref.shape[0], out_ref.shape[1] // 2
    decays = []
    for at in range(devices):
        pair = in_ref[at, 2 * rows : 2 * rows + 8, :].astype(FULL)
        decays.append(pair[0:1] + pair[1:2])
    state = jnp.zeros((rows, STATE), FULL)
    for at in range(devices):
        out_ref[at, 0:rows, :] = state.astype(LOW)
        state = decays[at] * state + in_ref[at, 0:rows, :].astype(FULL)
    state = jnp.zeros((rows, STATE), FULL)
    for at in reversed(range(devices)):
        out_ref[at, rows : 2 * rows, :] = state.astype(LOW)
        state = decays[at] * state + in_ref[at, rows : 2 * rows, :].astype(FULL)


def local_kernel(
    lengths_hbm,
    log_hbm,
    x_hbm,
    b_hbm,
    dy_hbm,
    c_hbm,
    grad_x_ref,
    grad_bc_ref,
    x_weighted_ref,
    dy_weighted_ref,
    leave_ref,
    lengths_ref,
    log_ref,
    x_ref,
    b_ref,
    dy_ref,
    c_ref,
    sems,
):
    loads = fetch(
        [
            (lengths_hbm, lengths_ref),
            (log_hbm, log_ref),
            (x_hbm, x_ref),
            (b_hbm, b_ref),
            (dy_hbm, dy_ref),
            (c_hbm, c_ref),
        ],
        sems,
    )
    for load in loads:
        load.wait()
    first_row, ends, cumulative, docs, enter, leave, _ = token_vectors(log_ref, lengths_ref)
    enter_cols, leave_cols = split_columns(enter), split_columns(leave)
    leave_ref[...] = leave_cols
    cum_cols = cumulative.T
    middle = doc_of(first_row + SPAN - 1, ends)
    cum_middle = cumulative[:, SPAN - 1 : SPAN]
    leave_first = jnp.where(
        docs[:, :SPAN] == middle, jnp.exp(cum_middle - cumulative[:, :SPAN]), 0.0
    )
    enter_second = jnp.where(
        docs[:, SPAN:] == middle, jnp.exp(cumulative[:, SPAN:] - cum_middle), 0.0
    )
    leave_first, enter_second = split_columns(leave_first), split_columns(enter_second)
    b, c = b_ref[...], c_ref[...]
    scores = mul(b, c, NT)
    cross_scores = scores[:SPAN, SPAN:].astype(LOW)
    is_left = iota((SPAN, LANES), 1) < HEAD_DIM
    masks = []
    for number in range(2):
        base = first_row + number * SPAN
        same = doc_of(base + iota((SPAN, SPAN), 0), ends) == doc_of(
            base + iota((SPAN, SPAN), 1), ends
        )
        masks.append(same & (iota((SPAN, SPAN), 0) <= iota((SPAN, SPAN), 1)))

    def halves(value):
        zero = jnp.zeros_like(value)
        return jnp.concatenate(
            [jnp.where(is_left, value, zero), jnp.where(is_left, zero, value)], axis=0
        )

    mixed = [jnp.zeros((SPAN, SPAN), FULL), jnp.zeros((SPAN, SPAN), FULL)]
    mixed_cross = jnp.zeros((SPAN, SPAN), FULL)
    for pair in range(PAIRS):
        low = pair * LANES
        x, dy = x_ref[:, low : low + LANES], dy_ref[:, low : low + LANES]
        for wide, cols, weighted_ref in (
            (x, leave_cols, x_weighted_ref),
            (dy, enter_cols, dy_weighted_ref),
        ):
            weighted = (wide.astype(FULL) * spread(cols, low, LANES)).astype(LOW)
            weighted_ref[:, low : low + LANES] = weighted
        first_wide = spread(leave_first, low, LANES)
        x_first = (x[:SPAN].astype(FULL) * first_wide).astype(LOW)
        dy_second = (dy[SPAN:].astype(FULL) * spread(enter_second, low, LANES)).astype(LOW)
        mixed_cross += mul(x_first, dy_second, NT)
        pieces = [first_wide * mul(cross_scores, dy_second), 0.0]
        for number in range(2):
            span = slice(number * SPAN, (number + 1) * SPAN)
            inner = mul(halves(x[span]), dy[span], NT)
            low_scores = []
            for side in range(2):
                head = 2 * pair + side
                gaps = cumulative[head : head + 1, span] - cum_cols[span, head : head + 1]
                within = jnp.exp(jnp.where(masks[number], gaps, -1e30))
                mixed[number] += within * inner[side * SPAN : (side + 1) * SPAN]
                low_scores.append((within * scores[span, span]).astype(LOW))
            grad_x_ref[span, low : low + LANES] = pieces[number] + mul(
                jnp.concatenate(low_scores, axis=1), halves(dy[span])
            )
    nothing = jnp.zeros((SPAN, SPAN), FULL)
    table = jnp.concatenate(
        [
            jnp.concatenate([mixed[0], mixed_cross], axis=1),
            jnp.concatenate([nothing, mixed[1]], axis=1),
        ],
        axis=0,
    )
    grad_bc_ref[:, :STATE] = mul(table.astype(LOW), c)
    grad_bc_ref[:, STATE:] = mul(table.T.astype(LOW), b)


def grad_bc_kernel(x_weighted_ref, dy_weighted_ref, local_ref, edge_ref, out_ref):
    rows = edge_ref.shape[1] // 2
    start = edge_ref[:, 0:rows, :].reshape(WIDE, STATE)
    end = edge_ref[:, rows : 2 * rows, :].reshape(WIDE, STATE)
    out_ref[:, :STATE] = (local_ref[:, :STATE] + mul(x_weighted_ref[...], end)).astype(LOW)
    out_ref[:, STATE:] = (local_ref[:, STATE:] + mul(dy_weighted_ref[...], start)).astype(LOW)


def grad_x_kernel(b_ref, leave_ref, local_ref, edge_ref, out_ref):
    rows = edge_ref.shape[1] // 2
    width = 2 * LANES
    for chunk in range(WIDE // width):
        low = chunk * width
        at = slice(low // rows, (low + width) // rows)
        end = edge_ref[at, rows : 2 * rows, :].reshape(width, STATE)
        later = spread(leave_ref[...], low, width) * mul(b_ref[...], end, NT)
        out_ref[:, low : low + width] = (local_ref[:, low : low + width] + later).astype(LOW)


def project_kernel(w_b_hbm, w_c_hbm, *refs, sibling):
    grads, (up, twice, down), (out_ref, grads_ref, weights_ref, sems) = refs[:4], refs[4:7], refs[7:]
    columns = out_ref.shape[1]
    me = lax.axis_index("tp")
    core = lax.rem(me, CORES)
    half = 1 - core if sibling else core
    from_row = pl.ds(pl.multiple_of((me - core + half) * columns, columns), columns)
    of_half = pl.ds(0 if sibling else columns, columns)
    pairs = [
        (w_b_hbm.at[from_row, :], weights_ref.at[0, :, pl.ds(0, STATE)]),
        (w_c_hbm.at[from_row, :], weights_ref.at[0, :, pl.ds(STATE, STATE)]),
        (grads[0], grads_ref.at[0]),
    ]
    for at, weight in enumerate((up.at[of_half, :], twice, down.at[of_half, :])):
        pairs.append((grads[at + 1], grads_ref.at[at + 1]))
        pairs.append((weight, weights_ref.at[at + 1]))
    loads = fetch(pairs, sems)
    total = 0.0
    for at in range(4):
        for load in loads[:3] if at == 0 else loads[1 + 2 * at : 3 + 2 * at]:
            load.wait()
        total += mul(grads_ref[at], weights_ref[at], NT)
    out_ref[...] = total.astype(out_ref.dtype)


BLOCK = pl.BlockSpec(memory_space=pltpu.VMEM)
HBM = pl.BlockSpec(memory_space=pltpu.HBM)


def call(body, out_shape, specs, vmem, out_specs=BLOCK, scratch=()):
    return pl.pallas_call(
        body,
        out_shape=out_shape,
        in_specs=specs,
        out_specs=out_specs,
        scratch_shapes=scratch,
        compiler_params=pltpu.CompilerParams(vmem_limit_bytes=vmem),
        cost_estimate=pl.CostEstimate(flops=1000, bytes_accessed=1000, transcendentals=0),
    )


def along_x(value, step):
    devices = lax.axis_size("tp")
    return lax.ppermute(
        value, "tp", [(at, (at + CORES * step) % devices) for at in range(devices)]
    )


def per_device(inner_x, in_b, in_c, log_decay, doc_lengths, out_grad, w_b, w_c):
    tokens = inner_x.shape[0]
    devices = lax.axis_size("seq")
    rows = WIDE // devices
    columns = w_b.shape[0] // lax.axis_size("tp")
    local = (doc_lengths, log_decay, inner_x, in_b, out_grad, in_c)
    dma = pltpu.SemaphoreType.DMA
    shape = jax.ShapeDtypeStruct
    held = [pltpu.SMEM(doc_lengths.shape, doc_lengths.dtype)] + [
        pltpu.VMEM(a.shape, a.dtype) for a in local[1:]
    ]
    blocks = len(ROUTE)
    summary, *sent = call(
        summary_kernel,
        [shape((devices, 2 * rows + 8, STATE), LOW)]
        + [shape((blocks // 2 * columns, 2 * STATE), LOW)] * 2,
        [HBM] * 8,
        LARGE_VMEM,
        [BLOCK, HBM, HBM],
        held
        + [pltpu.VMEM((blocks, columns, 2 * STATE), LOW)]
        + [dma((6,)), dma((2 * blocks,)), dma((blocks,))],
    )(*local, w_b, w_c)
    up, down = along_x(sent[0], 1), along_x(sent[1], 3)
    up_twice = along_x(up[2 * columns :], 1)
    down_twice = along_x(down[2 * columns :], 3)
    summary = lax.all_to_all(summary, "seq", 0, 0)
    edges = call(
        scan_kernel,
        shape((devices, 2 * rows, STATE), LOW),
        [BLOCK],
        4 * MIB,
    )(summary)
    edges = lax.all_to_all(edges, "seq", 0, 0)
    grad_x, grad_bc, x_weighted, dy_weighted, leave_cols = call(
        local_kernel,
        [
            shape((tokens, WIDE), FULL),
            shape((tokens, 2 * STATE), FULL),
            shape((tokens, WIDE), LOW),
            shape((tokens, WIDE), LOW),
            shape((tokens, 2 * HEADS), LOW),
        ],
        [HBM] * 6,
        16 * MIB,
        [BLOCK] * 5,
        held + [dma((6,))],
    )(*local)
    grad_bc = call(
        grad_bc_kernel,
        shape((tokens, 2 * STATE), LOW),
        [BLOCK] * 4,
        8 * MIB,
    )(x_weighted, dy_weighted, grad_bc, edges)
    others = [along_x(grad_bc, step) for step in (1, 2, 3)]
    grad_x = call(
        grad_x_kernel, shape((tokens, WIDE), LOW), [BLOCK] * 4, 8 * MIB
    )(in_b, leave_cols, grad_x, edges)

    def project(sibling, kind):
        return call(
            functools.partial(project_kernel, sibling=sibling),
            shape((tokens, columns), kind),
            [HBM] * 9,
            LARGE_VMEM,
            BLOCK,
            [
                pltpu.VMEM((4, tokens, 2 * STATE), LOW),
                pltpu.VMEM((4, columns, 2 * STATE), LOW),
                dma((9,)),
            ],
        )(w_b, w_c, grad_bc, *others, up, up_twice if sibling else down_twice, down)

    partner = [(at, at ^ 1) for at in range(lax.axis_size("tp"))]
    received = lax.ppermute(project(True, LOW), "tp", partner)
    grad_input = (project(False, FULL) + received.astype(FULL)).astype(LOW)
    return grad_x, grad_input


def solution(mesh):
    placed = (
        P("seq", "tp"),
        P("seq", "tp"),
        P("seq", "tp"),
        P("tp", "seq"),
        P(),
        P("seq", "tp"),
        P(None, "tp"),
        P(None, "tp"),
    )
    return jax.shard_map(
        per_device,
        mesh=mesh,
        in_specs=placed,
        out_specs=(P("seq", "tp"), P("seq", "tp")),
        check_vma=False,
    )
```

```python
import functools

import jax
import jax.numpy as jnp
from jax import lax
from jax.experimental import pallas as pl
from jax.experimental.pallas import tpu as pltpu
from jax.sharding import PartitionSpec as P

HEAD_DIM = 64
STATE = 128
SPAN = 128
HEADS = 16
LANES = 128
WIDE = HEADS * HEAD_DIM
PAIRS = WIDE // LANES
CORES = 2
ROUTE = ((1, True), (1, False), (2, True), (3, True), (3, False), (2, False))
LOW = jnp.bfloat16
FULL = jnp.float32
NN = (((1,), (0,)), ((), ()))
NT = (((1,), (1,)), ((), ()))
TN = (((0,), (0,)), ((), ()))
MIB = 1024 * 1024
LARGE_VMEM = 56 * MIB


def mul(a, b, dims=NN):
    return lax.dot_general(a, b, dims, preferred_element_type=FULL)


def iota(shape, axis):
    return lax.broadcasted_iota(jnp.int32, shape, axis)


def doc_of(positions, ends):
    return sum((positions >= end).astype(jnp.int32) for end in ends)


def doc_ends(lengths_ref):
    first = lengths_ref[0]
    second = first + lengths_ref[1]
    return (first, second, second + lengths_ref[2])


def token_vectors(log_ref, lengths_ref):
    tokens = log_ref.shape[1]
    first_row = lax.axis_index("seq") * tokens
    ends = doc_ends(lengths_ref)
    upper = (iota((tokens, tokens), 0) <= iota((tokens, tokens), 1)).astype(FULL)
    cumulative = lax.dot_general(
        log_ref[...], upper, NN, precision=lax.Precision.HIGHEST, preferred_element_type=FULL
    )
    docs = doc_of(first_row + iota((HEADS, tokens), 1), ends)
    prior = jnp.where(first_row > 0, doc_of(first_row - 1, ends), -1)
    last = doc_of(first_row + tokens - 1, ends)
    cum_last = cumulative[:, tokens - 1 :]
    enter = jnp.where(docs == prior, jnp.exp(cumulative), 0.0)
    leave = jnp.where(docs == last, jnp.exp(cum_last - cumulative), 0.0)
    total = jnp.where(last == prior, jnp.exp(cum_last), 0.0)
    return first_row, ends, cumulative, docs, enter, leave, total


def split_columns(rows):
    high = rows.astype(LOW).astype(FULL)
    both = jnp.concatenate([high, rows - high], axis=0)
    return both.T.astype(LOW)


def spread(columns, low, width):
    head = (low + iota((2 * HEADS, width), 1)) // HEAD_DIM
    pick = (head == iota((2 * HEADS, width), 0) % HEADS).astype(FULL).astype(LOW)
    return mul(columns, pick)


def fetch(pairs, sems):
    copies = [
        pltpu.make_async_copy(source, target, sems.at[at])
        for at, (source, target) in enumerate(pairs)
    ]
    for copy in copies:
        copy.start()
    return copies


def summary_kernel(
    lengths_hbm,
    log_hbm,
    x_hbm,
    b_hbm,
    dy_hbm,
    c_hbm,
    out_ref,
    lengths_ref,
    log_ref,
    x_ref,
    b_ref,
    dy_ref,
    c_ref,
    sems,
):
    loads = fetch(
        [
            (lengths_hbm, lengths_ref),
            (log_hbm, log_ref),
            (x_hbm, x_ref),
            (b_hbm, b_ref),
            (dy_hbm, dy_ref),
            (c_hbm, c_ref),
        ],
        sems,
    )
    slices = out_ref.shape[0]
    rows = WIDE // slices
    loads[0].wait()
    loads[1].wait()
    _, _, _, _, enter, leave, total = token_vectors(log_ref, lengths_ref)
    enter_cols = split_columns(enter)
    leave_cols = split_columns(leave)
    width = 2 * LANES
    for side, (wide_ref, narrow_ref, cols) in enumerate(
        ((x_ref, b_ref, leave_cols), (dy_ref, c_ref, enter_cols))
    ):
        loads[2 + 2 * side].wait()
        loads[3 + 2 * side].wait()
        narrow = narrow_ref[...]
        for chunk in range(WIDE // width):
            low = chunk * width
            at = slice(low // rows, (low + width) // rows)
            weighted = wide_ref[:, low : low + width].astype(FULL) * spread(cols, low, width)
            product = mul(weighted.astype(LOW), narrow, TN).astype(LOW)
            out_ref[at, side * rows : (side + 1) * rows, :] = product.reshape(
                width // rows, rows, STATE
            )
    total = jnp.broadcast_to(total, (HEADS, STATE))
    high = total.astype(LOW).astype(FULL)
    per_head = slices // HEADS
    for head in range(HEADS):
        rest = jnp.broadcast_to((total - high)[head : head + 1], (8, STATE))
        tile = jnp.where(iota((8, STATE), 0) == 0, high[head : head + 1], rest).astype(LOW)
        for part in range(per_head):
            out_ref[head * per_head + part, 2 * rows : 2 * rows + 8, :] = tile


def stage_kernel(_, w_b_hbm, w_c_hbm, up_hbm, down_hbm, passing_ref, passing_sems, sent_sems):
    columns = passing_ref.shape[1]
    me = lax.axis_index("tp")
    core, chips = lax.rem(me, CORES), lax.axis_size("tp") // CORES
    pairs = []
    for at, (step, sibling) in enumerate(ROUTE):
        half = 1 - core if sibling else core
        target = lax.rem(me // CORES + step, chips)
        from_row = pl.ds(pl.multiple_of((target * CORES + half) * columns, columns), columns)
        pairs.append((w_b_hbm.at[from_row, :], passing_ref.at[at, :, pl.ds(0, STATE)]))
        pairs.append((w_c_hbm.at[from_row, :], passing_ref.at[at, :, pl.ds(STATE, STATE)]))
    loads = fetch(pairs, passing_sems)
    sends = []
    for at in range(len(ROUTE)):
        target = (up_hbm, down_hbm)[at // 3].at[pl.ds(at % 3 * columns, columns), :]
        loads[2 * at].wait()
        loads[2 * at + 1].wait()
        sends.append(pltpu.make_async_copy(passing_ref.at[at], target, sent_sems.at[at]))
        sends[-1].start()
    for send in sends:
        send.wait()


def scan_kernel(in_ref, _, out_ref):
    devices, rows = out_ref.shape[0], out_ref.shape[1] // 2
    decays = []
    for at in range(devices):
        pair = in_ref[at, 2 * rows : 2 * rows + 8, :].astype(FULL)
        decays.append(pair[0:1] + pair[1:2])
    state = jnp.zeros((rows, STATE), FULL)
    for at in range(devices):
        out_ref[at, 0:rows, :] = state.astype(LOW)
        state = decays[at] * state + in_ref[at, 0:rows, :].astype(FULL)
    state = jnp.zeros((rows, STATE), FULL)
    for at in reversed(range(devices)):
        out_ref[at, rows : 2 * rows, :] = state.astype(LOW)
        state = decays[at] * state + in_ref[at, rows : 2 * rows, :].astype(FULL)


def local_kernel(
    lengths_hbm,
    log_hbm,
    x_hbm,
    b_hbm,
    dy_hbm,
    c_hbm,
    grad_x_ref,
    grad_bc_ref,
    x_weighted_ref,
    dy_weighted_ref,
    leave_ref,
    lengths_ref,
    log_ref,
    x_ref,
    b_ref,
    dy_ref,
    c_ref,
    sems,
):
    loads = fetch(
        [
            (lengths_hbm, lengths_ref),
            (log_hbm, log_ref),
            (x_hbm, x_ref),
            (b_hbm, b_ref),
            (dy_hbm, dy_ref),
            (c_hbm, c_ref),
        ],
        sems,
    )
    for load in loads:
        load.wait()
    first_row, ends, cumulative, docs, enter, leave, _ = token_vectors(log_ref, lengths_ref)
    enter_cols, leave_cols = split_columns(enter), split_columns(leave)
    leave_ref[...] = leave_cols
    cum_cols = cumulative.T
    middle = doc_of(first_row + SPAN - 1, ends)
    cum_middle = cumulative[:, SPAN - 1 : SPAN]
    leave_first = jnp.where(
        docs[:, :SPAN] == middle, jnp.exp(cum_middle - cumulative[:, :SPAN]), 0.0
    )
    enter_second = jnp.where(
        docs[:, SPAN:] == middle, jnp.exp(cumulative[:, SPAN:] - cum_middle), 0.0
    )
    leave_first, enter_second = split_columns(leave_first), split_columns(enter_second)
    b, c = b_ref[...], c_ref[...]
    scores = mul(b, c, NT)
    cross_scores = scores[:SPAN, SPAN:].astype(LOW)
    is_left = iota((SPAN, LANES), 1) < HEAD_DIM
    masks = []
    for number in range(2):
        base = first_row + number * SPAN
        same = doc_of(base + iota((SPAN, SPAN), 0), ends) == doc_of(
            base + iota((SPAN, SPAN), 1), ends
        )
        masks.append(same & (iota((SPAN, SPAN), 0) <= iota((SPAN, SPAN), 1)))

    def halves(value):
        zero = jnp.zeros_like(value)
        return jnp.concatenate(
            [jnp.where(is_left, value, zero), jnp.where(is_left, zero, value)], axis=0
        )

    mixed = [jnp.zeros((SPAN, SPAN), FULL), jnp.zeros((SPAN, SPAN), FULL)]
    mixed_cross = jnp.zeros((SPAN, SPAN), FULL)
    for pair in range(PAIRS):
        low = pair * LANES
        x, dy = x_ref[:, low : low + LANES], dy_ref[:, low : low + LANES]
        for wide, cols, weighted_ref in (
            (x, leave_cols, x_weighted_ref),
            (dy, enter_cols, dy_weighted_ref),
        ):
            weighted = (wide.astype(FULL) * spread(cols, low, LANES)).astype(LOW)
            weighted_ref[:, low : low + LANES] = weighted
        first_wide = spread(leave_first, low, LANES)
        x_first = (x[:SPAN].astype(FULL) * first_wide).astype(LOW)
        dy_second = (dy[SPAN:].astype(FULL) * spread(enter_second, low, LANES)).astype(LOW)
        mixed_cross += mul(x_first, dy_second, NT)
        pieces = [first_wide * mul(cross_scores, dy_second), 0.0]
        for number in range(2):
            span = slice(number * SPAN, (number + 1) * SPAN)
            inner = mul(halves(x[span]), dy[span], NT)
            low_scores = []
            for side in range(2):
                head = 2 * pair + side
                gaps = cumulative[head : head + 1, span] - cum_cols[span, head : head + 1]
                within = jnp.exp(jnp.where(masks[number], gaps, -1e30))
                mixed[number] += within * inner[side * SPAN : (side + 1) * SPAN]
                low_scores.append((within * scores[span, span]).astype(LOW))
            grad_x_ref[span, low : low + LANES] = pieces[number] + mul(
                jnp.concatenate(low_scores, axis=1), halves(dy[span])
            )
    nothing = jnp.zeros((SPAN, SPAN), FULL)
    table = jnp.concatenate(
        [
            jnp.concatenate([mixed[0], mixed_cross], axis=1),
            jnp.concatenate([nothing, mixed[1]], axis=1),
        ],
        axis=0,
    )
    grad_bc_ref[:, :STATE] = mul(table.astype(LOW), c)
    grad_bc_ref[:, STATE:] = mul(table.T.astype(LOW), b)


def grad_bc_kernel(x_weighted_ref, dy_weighted_ref, local_ref, edge_ref, out_ref):
    rows = edge_ref.shape[1] // 2
    start = edge_ref[:, 0:rows, :].reshape(WIDE, STATE)
    end = edge_ref[:, rows : 2 * rows, :].reshape(WIDE, STATE)
    out_ref[:, :STATE] = (local_ref[:, :STATE] + mul(x_weighted_ref[...], end)).astype(LOW)
    out_ref[:, STATE:] = (local_ref[:, STATE:] + mul(dy_weighted_ref[...], start)).astype(LOW)


def grad_x_kernel(b_ref, leave_ref, local_ref, edge_ref, out_ref):
    rows = edge_ref.shape[1] // 2
    width = 2 * LANES
    for chunk in range(WIDE // width):
        low = chunk * width
        at = slice(low // rows, (low + width) // rows)
        end = edge_ref[at, rows : 2 * rows, :].reshape(width, STATE)
        later = spread(leave_ref[...], low, width) * mul(b_ref[...], end, NT)
        out_ref[:, low : low + width] = (local_ref[:, low : low + width] + later).astype(LOW)


def project_kernel(w_b_hbm, w_c_hbm, *refs, sibling):
    grads, (up, up_twice, down, down_twice) = refs[:4], refs[4:8]
    received, (out_ref, grads_ref, weights_ref, received_ref, sems) = refs[8:-5], refs[-5:]
    columns = out_ref.shape[1]
    me = lax.axis_index("tp")
    core = lax.rem(me, CORES)
    half = 1 - core if sibling else core
    from_row = pl.ds(pl.multiple_of((me - core + half) * columns, columns), columns)
    of_half = pl.ds(0 if sibling else columns, columns)
    pairs = [
        (w_b_hbm.at[from_row, :], weights_ref.at[0, :, pl.ds(0, STATE)]),
        (w_c_hbm.at[from_row, :], weights_ref.at[0, :, pl.ds(STATE, STATE)]),
        (grads[0], grads_ref.at[0]),
    ]
    twice = up_twice if sibling else down_twice
    for at, weight in enumerate((up.at[of_half, :], twice, down.at[of_half, :])):
        pairs.append((grads[at + 1], grads_ref.at[at + 1]))
        pairs.append((weight, weights_ref.at[at + 1]))
    pairs += [(ref, received_ref) for ref in received]
    loads = fetch(pairs, sems)
    total = 0.0
    for at in range(4):
        for load in loads[:3] if at == 0 else loads[1 + 2 * at : 3 + 2 * at]:
            load.wait()
        total += mul(grads_ref[at], weights_ref[at], NT)
    for load in loads[9:]:
        load.wait()
        total += received_ref[...].astype(FULL)
    out_ref[...] = total.astype(LOW)


BLOCK = pl.BlockSpec(memory_space=pltpu.VMEM)
HBM = pl.BlockSpec(memory_space=pltpu.HBM)


def call(body, out_shape, specs, vmem, out_specs=BLOCK, scratch=()):
    return pl.pallas_call(
        body,
        out_shape=out_shape,
        in_specs=specs,
        out_specs=out_specs,
        scratch_shapes=scratch,
        compiler_params=pltpu.CompilerParams(vmem_limit_bytes=vmem),
        cost_estimate=pl.CostEstimate(flops=1000, bytes_accessed=1000, transcendentals=0),
    )


def along_x(value, step):
    devices = lax.axis_size("tp")
    return lax.ppermute(
        value, "tp", [(at, (at + CORES * step) % devices) for at in range(devices)]
    )


def per_device(inner_x, in_b, in_c, log_decay, doc_lengths, out_grad, w_b, w_c):
    tokens = inner_x.shape[0]
    devices = lax.axis_size("seq")
    rows = WIDE // devices
    columns = w_b.shape[0] // lax.axis_size("tp")
    local = (doc_lengths, log_decay, inner_x, in_b, out_grad, in_c)
    dma = pltpu.SemaphoreType.DMA
    shape = jax.ShapeDtypeStruct
    held = [pltpu.SMEM(doc_lengths.shape, doc_lengths.dtype)] + [
        pltpu.VMEM(a.shape, a.dtype) for a in local[1:]
    ]
    blocks = len(ROUTE)
    summary = call(
        summary_kernel,
        shape((devices, 2 * rows + 8, STATE), LOW),
        [HBM] * 6,
        LARGE_VMEM,
        BLOCK,
        held + [dma((6,))],
    )(*local)
    sent = call(
        stage_kernel,
        [shape((blocks // 2 * columns, 2 * STATE), LOW)] * 2,
        [HBM] * 3,
        LARGE_VMEM,
        [HBM, HBM],
        [pltpu.VMEM((blocks, columns, 2 * STATE), LOW), dma((2 * blocks,)), dma((blocks,))],
    )(summary, w_b, w_c)
    up, down = along_x(sent[0], 1), along_x(sent[1], 3)
    up_twice = along_x(up[2 * columns :], 1)
    down_twice = along_x(down[2 * columns :], 3)
    summary = lax.all_to_all(summary, "seq", 0, 0)
    grad_x, grad_bc, x_weighted, dy_weighted, leave_cols = call(
        local_kernel,
        [
            shape((tokens, WIDE), FULL),
            shape((tokens, 2 * STATE), FULL),
            shape((tokens, WIDE), LOW),
            shape((tokens, WIDE), LOW),
            shape((tokens, 2 * HEADS), LOW),
        ],
        [HBM] * 6,
        16 * MIB,
        [BLOCK] * 5,
        held + [dma((6,))],
    )(*local)
    edges = call(
        scan_kernel,
        shape((devices, 2 * rows, STATE), LOW),
        [BLOCK, HBM],
        4 * MIB,
    )(summary, leave_cols)
    edges = lax.all_to_all(edges, "seq", 0, 0)
    grad_bc = call(
        grad_bc_kernel,
        shape((tokens, 2 * STATE), LOW),
        [BLOCK] * 4,
        8 * MIB,
    )(x_weighted, dy_weighted, grad_bc, edges)
    others = [along_x(grad_bc, step) for step in (1, 2, 3)]
    grad_x = call(
        grad_x_kernel, shape((tokens, WIDE), LOW), [BLOCK] * 4, 8 * MIB
    )(in_b, leave_cols, grad_x, edges)

    def project(*received):
        return call(
            functools.partial(project_kernel, sibling=not received),
            shape((tokens, columns), LOW),
            [HBM] * (10 + len(received)),
            LARGE_VMEM,
            BLOCK,
            [
                pltpu.VMEM((4, tokens, 2 * STATE), LOW),
                pltpu.VMEM((4, columns, 2 * STATE), LOW),
                pltpu.VMEM((tokens, columns), LOW),
                dma((9 + len(received),)),
            ],
        )(w_b, w_c, grad_bc, *others, up, up_twice, down, down_twice, *received)

    partner = [(at, at ^ 1) for at in range(lax.axis_size("tp"))]
    grad_input = project(lax.ppermute(project(), "tp", partner))
    return grad_x, grad_input


def solution(mesh):
    placed = (
        P("seq", "tp"),
        P("seq", "tp"),
        P("seq", "tp"),
        P("tp", "seq"),
        P(),
        P("seq", "tp"),
        P(None, "tp"),
        P(None, "tp"),
    )
    return jax.shard_map(
        per_device,
        mesh=mesh,
        in_specs=placed,
        out_specs=(P("seq", "tp"), P("seq", "tp")),
        check_vma=False,
    )
```

```python
import functools

import jax
import jax.numpy as jnp
from jax import lax
from jax.experimental import pallas as pl
from jax.experimental.pallas import tpu as pltpu
from jax.sharding import PartitionSpec as P

HEAD_DIM = 64
STATE = 128
SPAN = 128
HEADS = 16
LANES = 128
WIDE = HEADS * HEAD_DIM
PAIRS = WIDE // LANES
CORES = 2
ROUTE = ((2, True), (2, False), (1, True), (1, False), (3, True), (3, False), (0, True), (0, False))
LOW = jnp.bfloat16
FULL = jnp.float32
NN = (((1,), (0,)), ((), ()))
NT = (((1,), (1,)), ((), ()))
TN = (((0,), (0,)), ((), ()))
MIB = 1024 * 1024
LARGE_VMEM = 56 * MIB


def mul(a, b, dims=NN):
    return lax.dot_general(a, b, dims, preferred_element_type=FULL)


def iota(shape, axis):
    return lax.broadcasted_iota(jnp.int32, shape, axis)


def doc_of(positions, ends):
    return sum((positions >= end).astype(jnp.int32) for end in ends)


def doc_ends(lengths_ref):
    first = lengths_ref[0]
    second = first + lengths_ref[1]
    return (first, second, second + lengths_ref[2])


def token_vectors(log_ref, lengths_ref):
    tokens = log_ref.shape[1]
    first_row = lax.axis_index("seq") * tokens
    ends = doc_ends(lengths_ref)
    upper = (iota((tokens, tokens), 0) <= iota((tokens, tokens), 1)).astype(FULL)
    cumulative = lax.dot_general(
        log_ref[...], upper, NN, precision=lax.Precision.HIGHEST, preferred_element_type=FULL
    )
    docs = doc_of(first_row + iota((HEADS, tokens), 1), ends)
    prior = jnp.where(first_row > 0, doc_of(first_row - 1, ends), -1)
    last = doc_of(first_row + tokens - 1, ends)
    cum_last = cumulative[:, tokens - 1 :]
    enter = jnp.where(docs == prior, jnp.exp(cumulative), 0.0)
    leave = jnp.where(docs == last, jnp.exp(cum_last - cumulative), 0.0)
    total = jnp.where(last == prior, jnp.exp(cum_last), 0.0)
    return first_row, ends, cumulative, docs, enter, leave, total


def split_columns(rows):
    high = rows.astype(LOW).astype(FULL)
    both = jnp.concatenate([high, rows - high], axis=0)
    return both.T.astype(LOW)


def spread(columns, low, width):
    head = (low + iota((2 * HEADS, width), 1)) // HEAD_DIM
    pick = (head == iota((2 * HEADS, width), 0) % HEADS).astype(FULL).astype(LOW)
    return mul(columns, pick)


def fetch(pairs, sems):
    copies = [
        pltpu.make_async_copy(source, target, sems.at[at])
        for at, (source, target) in enumerate(pairs)
    ]
    for copy in copies:
        copy.start()
    return copies


def summary_kernel(
    lengths_hbm,
    log_hbm,
    x_hbm,
    b_hbm,
    dy_hbm,
    c_hbm,
    out_ref,
    lengths_ref,
    log_ref,
    x_ref,
    b_ref,
    dy_ref,
    c_ref,
    sems,
):
    loads = fetch(
        [
            (lengths_hbm, lengths_ref),
            (log_hbm, log_ref),
            (x_hbm, x_ref),
            (b_hbm, b_ref),
            (dy_hbm, dy_ref),
            (c_hbm, c_ref),
        ],
        sems,
    )
    slices = out_ref.shape[0]
    rows = WIDE // slices
    loads[0].wait()
    loads[1].wait()
    _, _, _, _, enter, leave, total = token_vectors(log_ref, lengths_ref)
    enter_cols = split_columns(enter)
    leave_cols = split_columns(leave)
    width = 2 * LANES
    for side, (wide_ref, narrow_ref, cols) in enumerate(
        ((x_ref, b_ref, leave_cols), (dy_ref, c_ref, enter_cols))
    ):
        loads[2 + 2 * side].wait()
        loads[3 + 2 * side].wait()
        narrow = narrow_ref[...]
        for chunk in range(WIDE // width):
            low = chunk * width
            at = slice(low // rows, (low + width) // rows)
            weighted = wide_ref[:, low : low + width].astype(FULL) * spread(cols, low, width)
            product = mul(weighted.astype(LOW), narrow, TN).astype(LOW)
            out_ref[at, side * rows : (side + 1) * rows, :] = product.reshape(
                width // rows, rows, STATE
            )
    total = jnp.broadcast_to(total, (HEADS, STATE))
    high = total.astype(LOW).astype(FULL)
    per_head = slices // HEADS
    for head in range(HEADS):
        rest = jnp.broadcast_to((total - high)[head : head + 1], (8, STATE))
        tile = jnp.where(iota((8, STATE), 0) == 0, high[head : head + 1], rest).astype(LOW)
        for part in range(per_head):
            out_ref[head * per_head + part, 2 * rows : 2 * rows + 8, :] = tile


def stage_kernel(_, w_b_hbm, w_c_hbm, *refs):
    up_twice_hbm, down_twice_hbm, up_hbm, down_hbm, own_hbm = refs[:5]
    passing_ref, passing_sems, sent_sems = refs[5:]
    columns = passing_ref.shape[1]
    me = lax.axis_index("tp")
    core, chips = lax.rem(me, CORES), lax.axis_size("tp") // CORES
    pairs = []
    for at, (step, sibling) in enumerate(ROUTE):
        half = 1 - core if sibling else core
        target = lax.rem(me // CORES + step, chips)
        from_row = pl.ds(pl.multiple_of((target * CORES + half) * columns, columns), columns)
        pairs.append((w_b_hbm.at[from_row, :], passing_ref.at[at, :, pl.ds(0, STATE)]))
        pairs.append((w_c_hbm.at[from_row, :], passing_ref.at[at, :, pl.ds(STATE, STATE)]))
    loads = fetch(pairs, passing_sems)
    sends = []
    targets = [up_twice_hbm, down_twice_hbm]
    for whole in (up_hbm, down_hbm, own_hbm):
        targets += [whole.at[pl.ds(0, columns), :], whole.at[pl.ds(columns, columns), :]]
    for at, target in enumerate(targets):
        loads[2 * at].wait()
        loads[2 * at + 1].wait()
        sends.append(pltpu.make_async_copy(passing_ref.at[at], target, sent_sems.at[at]))
        sends[-1].start()
    for send in sends:
        send.wait()


def scan_kernel(in_ref, _, out_ref):
    devices, rows = out_ref.shape[0], out_ref.shape[1] // 2
    decays = []
    for at in range(devices):
        pair = in_ref[at, 2 * rows : 2 * rows + 8, :].astype(FULL)
        decays.append(pair[0:1] + pair[1:2])
    state = jnp.zeros((rows, STATE), FULL)
    for at in range(devices):
        out_ref[at, 0:rows, :] = state.astype(LOW)
        state = decays[at] * state + in_ref[at, 0:rows, :].astype(FULL)
    state = jnp.zeros((rows, STATE), FULL)
    for at in reversed(range(devices)):
        out_ref[at, rows : 2 * rows, :] = state.astype(LOW)
        state = decays[at] * state + in_ref[at, rows : 2 * rows, :].astype(FULL)


def local_kernel(
    lengths_hbm,
    log_hbm,
    x_hbm,
    b_hbm,
    dy_hbm,
    c_hbm,
    grad_x_ref,
    grad_bc_ref,
    weighted_ref,
    leave_ref,
    lengths_ref,
    log_ref,
    x_ref,
    b_ref,
    dy_ref,
    c_ref,
    sems,
):
    loads = fetch(
        [
            (lengths_hbm, lengths_ref),
            (log_hbm, log_ref),
            (x_hbm, x_ref),
            (b_hbm, b_ref),
            (dy_hbm, dy_ref),
            (c_hbm, c_ref),
        ],
        sems,
    )
    for load in loads:
        load.wait()
    first_row, ends, cumulative, docs, enter, leave, _ = token_vectors(log_ref, lengths_ref)
    enter_cols, leave_cols = split_columns(enter), split_columns(leave)
    leave_ref[...] = leave_cols
    cum_cols = cumulative.T
    middle = doc_of(first_row + SPAN - 1, ends)
    cum_middle = cumulative[:, SPAN - 1 : SPAN]
    leave_first = jnp.where(
        docs[:, :SPAN] == middle, jnp.exp(cum_middle - cumulative[:, :SPAN]), 0.0
    )
    enter_second = jnp.where(
        docs[:, SPAN:] == middle, jnp.exp(cumulative[:, SPAN:] - cum_middle), 0.0
    )
    leave_first, enter_second = split_columns(leave_first), split_columns(enter_second)
    b, c = b_ref[...], c_ref[...]
    scores = mul(b, c, NT)
    cross_scores = scores[:SPAN, SPAN:].astype(LOW)
    is_left = iota((SPAN, LANES), 1) < HEAD_DIM
    masks = []
    for number in range(2):
        base = first_row + number * SPAN
        same = doc_of(base + iota((SPAN, SPAN), 0), ends) == doc_of(
            base + iota((SPAN, SPAN), 1), ends
        )
        masks.append(same & (iota((SPAN, SPAN), 0) <= iota((SPAN, SPAN), 1)))

    def halves(value):
        zero = jnp.zeros_like(value)
        return jnp.concatenate(
            [jnp.where(is_left, value, zero), jnp.where(is_left, zero, value)], axis=0
        )

    mixed = [jnp.zeros((SPAN, SPAN), FULL), jnp.zeros((SPAN, SPAN), FULL)]
    mixed_cross = jnp.zeros((SPAN, SPAN), FULL)
    for pair in range(PAIRS):
        low = pair * LANES
        x, dy = x_ref[:, low : low + LANES], dy_ref[:, low : low + LANES]
        for side, (wide, cols) in enumerate(((x, leave_cols), (dy, enter_cols))):
            weighted = (wide.astype(FULL) * spread(cols, low, LANES)).astype(LOW)
            weighted_ref[side, :, low : low + LANES] = weighted
        first_wide = spread(leave_first, low, LANES)
        x_first = (x[:SPAN].astype(FULL) * first_wide).astype(LOW)
        dy_second = (dy[SPAN:].astype(FULL) * spread(enter_second, low, LANES)).astype(LOW)
        mixed_cross += mul(x_first, dy_second, NT)
        pieces = [first_wide * mul(cross_scores, dy_second), 0.0]
        for number in range(2):
            span = slice(number * SPAN, (number + 1) * SPAN)
            inner = mul(halves(x[span]), dy[span], NT)
            low_scores = []
            for side in range(2):
                head = 2 * pair + side
                gaps = cumulative[head : head + 1, span] - cum_cols[span, head : head + 1]
                within = jnp.exp(jnp.where(masks[number], gaps, -1e30))
                mixed[number] += within * inner[side * SPAN : (side + 1) * SPAN]
                low_scores.append((within * scores[span, span]).astype(LOW))
            grad_x_ref[span, low : low + LANES] = pieces[number] + mul(
                jnp.concatenate(low_scores, axis=1), halves(dy[span])
            )
    nothing = jnp.zeros((SPAN, SPAN), FULL)
    table = jnp.concatenate(
        [
            jnp.concatenate([mixed[0], mixed_cross], axis=1),
            jnp.concatenate([nothing, mixed[1]], axis=1),
        ],
        axis=0,
    )
    grad_bc_ref[:, :STATE] = mul(table.astype(LOW), c)
    grad_bc_ref[:, STATE:] = mul(table.T.astype(LOW), b)


def grad_bc_kernel(weighted_ref, local_ref, edge_ref, *refs):
    out_ref = refs[-1]
    rows = edge_ref.shape[1] // 2
    start = edge_ref[:, 0:rows, :].reshape(WIDE, STATE)
    end = edge_ref[:, rows : 2 * rows, :].reshape(WIDE, STATE)
    out_ref[:, :STATE] = (local_ref[:, :STATE] + mul(weighted_ref[0], end)).astype(LOW)
    out_ref[:, STATE:] = (local_ref[:, STATE:] + mul(weighted_ref[1], start)).astype(LOW)


def grad_x_kernel(b_ref, leave_ref, local_ref, edge_ref, out_ref):
    rows = edge_ref.shape[1] // 2
    width = 2 * LANES
    for chunk in range(WIDE // width):
        low = chunk * width
        at = slice(low // rows, (low + width) // rows)
        end = edge_ref[at, rows : 2 * rows, :].reshape(width, STATE)
        later = spread(leave_ref[...], low, width) * mul(b_ref[...], end, NT)
        out_ref[:, low : low + width] = (local_ref[:, low : low + width] + later).astype(LOW)


def project_kernel(*refs, sibling):
    grads, (own, up, down), relayed = refs[:4], refs[4:7], refs[7:9]
    received, out_ref = refs[9:-1], refs[-1]
    columns = out_ref.shape[1]
    half = slice(0, columns) if sibling else slice(columns, 2 * columns)
    total = mul(grads[0][...], own[half, :], NT)
    total += mul(grads[1][...], up[half, :], NT)
    total += mul(grads[2][...], relayed[0 if sibling else 1][...], NT)
    total += mul(grads[3][...], down[half, :], NT)
    for ref in received:
        total += ref[...].astype(FULL)
    out_ref[...] = total.astype(LOW)


BLOCK = pl.BlockSpec(memory_space=pltpu.VMEM)
HBM = pl.BlockSpec(memory_space=pltpu.HBM)


def call(body, out_shape, specs, vmem, out_specs=BLOCK, scratch=()):
    return pl.pallas_call(
        body,
        out_shape=out_shape,
        in_specs=specs,
        out_specs=out_specs,
        scratch_shapes=scratch,
        compiler_params=pltpu.CompilerParams(vmem_limit_bytes=vmem),
        cost_estimate=pl.CostEstimate(flops=1000, bytes_accessed=1000, transcendentals=0),
    )


def along_x(value, step):
    devices = lax.axis_size("tp")
    return lax.ppermute(
        value, "tp", [(at, (at + CORES * step) % devices) for at in range(devices)]
    )


def per_device(inner_x, in_b, in_c, log_decay, doc_lengths, out_grad, w_b, w_c):
    tokens = inner_x.shape[0]
    devices = lax.axis_size("seq")
    rows = WIDE // devices
    columns = w_b.shape[0] // lax.axis_size("tp")
    local = (doc_lengths, log_decay, inner_x, in_b, out_grad, in_c)
    dma = pltpu.SemaphoreType.DMA
    shape = jax.ShapeDtypeStruct
    held = [pltpu.SMEM(doc_lengths.shape, doc_lengths.dtype)] + [
        pltpu.VMEM(a.shape, a.dtype) for a in local[1:]
    ]
    blocks = len(ROUTE)
    summary = call(
        summary_kernel,
        shape((devices, 2 * rows + 8, STATE), LOW),
        [HBM] * 6,
        LARGE_VMEM,
        BLOCK,
        held + [dma((6,))],
    )(*local)
    sent = call(
        stage_kernel,
        [shape((columns, 2 * STATE), LOW)] * 2 + [shape((2 * columns, 2 * STATE), LOW)] * 3,
        [HBM] * 3,
        LARGE_VMEM,
        [HBM] * 5,
        [pltpu.VMEM((blocks, columns, 2 * STATE), LOW), dma((2 * blocks,)), dma((blocks,))],
    )(summary, w_b, w_c)
    up_twice, down_twice = along_x(sent[0], 1), along_x(sent[1], 3)
    up, down = along_x(sent[2], 1), along_x(sent[3], 3)
    up_twice, down_twice = along_x(up_twice, 1), along_x(down_twice, 3)
    summary = lax.all_to_all(summary, "seq", 0, 0)
    grad_x, grad_bc, weighted, leave_cols = call(
        local_kernel,
        [
            shape((tokens, WIDE), FULL),
            shape((tokens, 2 * STATE), FULL),
            shape((2, tokens, WIDE), LOW),
            shape((tokens, 2 * HEADS), LOW),
        ],
        [HBM] * 6,
        16 * MIB,
        [BLOCK] * 4,
        held + [dma((6,))],
    )(*local)
    edges = call(
        scan_kernel,
        shape((devices, 2 * rows, STATE), LOW),
        [BLOCK, HBM],
        4 * MIB,
    )(summary, leave_cols)
    edges = lax.all_to_all(edges, "seq", 0, 0)
    grad_bc = call(
        grad_bc_kernel,
        shape((tokens, 2 * STATE), LOW),
        [BLOCK] * 3 + [HBM] * 2,
        8 * MIB,
    )(weighted, grad_bc, edges, up, down)
    others = [along_x(grad_bc, step) for step in (1, 2, 3)]
    grad_x = call(
        grad_x_kernel, shape((tokens, WIDE), LOW), [BLOCK] * 4, 8 * MIB
    )(in_b, leave_cols, grad_x, edges)

    def project(*received):
        return call(
            functools.partial(project_kernel, sibling=not received),
            shape((tokens, columns), LOW),
            [BLOCK] * (9 + len(received)),
            16 * MIB,
        )(grad_bc, *others, sent[4], up, down, up_twice, down_twice, *received)

    partner = [(at, at ^ 1) for at in range(lax.axis_size("tp"))]
    grad_input = project(lax.ppermute(project(), "tp", partner))
    return grad_x, grad_input


def solution(mesh):
    placed = (
        P("seq", "tp"),
        P("seq", "tp"),
        P("seq", "tp"),
        P("tp", "seq"),
        P(),
        P("seq", "tp"),
        P(None, "tp"),
        P(None, "tp"),
    )
    return jax.shard_map(
        per_device,
        mesh=mesh,
        in_specs=placed,
        out_specs=(P("seq", "tp"), P("seq", "tp")),
        check_vma=False,
    )
```

```python
import functools

import jax
import jax.numpy as jnp
from jax import lax
from jax.experimental import pallas as pl
from jax.experimental.pallas import tpu as pltpu
from jax.sharding import PartitionSpec as P

HEAD_DIM = 64
STATE = 128
SPAN = 128
HEADS = 16
LANES = 128
WIDE = HEADS * HEAD_DIM
PAIRS = WIDE // LANES
CORES = 2
ALONG_Y = 4
ROUTE = ((2, 0, 1), (2, 1, 1), (1, 0, 2), (3, 0, 2))
LOW = jnp.bfloat16
FULL = jnp.float32
NN = (((1,), (0,)), ((), ()))
NT = (((1,), (1,)), ((), ()))
TN = (((0,), (0,)), ((), ()))
MIB = 1024 * 1024
LARGE_VMEM = 56 * MIB


def mul(a, b, dims=NN):
    return lax.dot_general(a, b, dims, preferred_element_type=FULL)


def iota(shape, axis):
    return lax.broadcasted_iota(jnp.int32, shape, axis)


def doc_of(positions, ends):
    return sum((positions >= end).astype(jnp.int32) for end in ends)


def doc_ends(lengths_ref):
    first = lengths_ref[0]
    second = first + lengths_ref[1]
    return (first, second, second + lengths_ref[2])


def token_vectors(log_ref, lengths_ref):
    tokens = log_ref.shape[1]
    first_row = lax.axis_index("seq") * tokens
    ends = doc_ends(lengths_ref)
    upper = (iota((tokens, tokens), 0) <= iota((tokens, tokens), 1)).astype(FULL)
    cumulative = lax.dot_general(
        log_ref[...], upper, NN, precision=lax.Precision.HIGHEST, preferred_element_type=FULL
    )
    docs = doc_of(first_row + iota((HEADS, tokens), 1), ends)
    prior = jnp.where(first_row > 0, doc_of(first_row - 1, ends), -1)
    last = doc_of(first_row + tokens - 1, ends)
    cum_last = cumulative[:, tokens - 1 :]
    enter = jnp.where(docs == prior, jnp.exp(cumulative), 0.0)
    leave = jnp.where(docs == last, jnp.exp(cum_last - cumulative), 0.0)
    total = jnp.where(last == prior, jnp.exp(cum_last), 0.0)
    return first_row, ends, cumulative, docs, enter, leave, total


def split_columns(rows):
    high = rows.astype(LOW).astype(FULL)
    both = jnp.concatenate([high, rows - high], axis=0)
    return both.T.astype(LOW)


def spread(columns, low, width):
    head = (low + iota((2 * HEADS, width), 1)) // HEAD_DIM
    pick = (head == iota((2 * HEADS, width), 0) % HEADS).astype(FULL).astype(LOW)
    return mul(columns, pick)


def fetch(pairs, sems):
    copies = [
        pltpu.make_async_copy(source, target, sems.at[at])
        for at, (source, target) in enumerate(pairs)
    ]
    for copy in copies:
        copy.start()
    return copies


def summary_kernel(
    lengths_hbm,
    log_hbm,
    x_hbm,
    b_hbm,
    dy_hbm,
    c_hbm,
    out_ref,
    lengths_ref,
    log_ref,
    x_ref,
    b_ref,
    dy_ref,
    c_ref,
    sems,
):
    loads = fetch(
        [
            (lengths_hbm, lengths_ref),
            (log_hbm, log_ref),
            (x_hbm, x_ref),
            (b_hbm, b_ref),
            (dy_hbm, dy_ref),
            (c_hbm, c_ref),
        ],
        sems,
    )
    slices = out_ref.shape[0]
    rows = WIDE // slices
    loads[0].wait()
    loads[1].wait()
    _, _, _, _, enter, leave, total = token_vectors(log_ref, lengths_ref)
    enter_cols = split_columns(enter)
    leave_cols = split_columns(leave)
    width = 2 * LANES
    for side, (wide_ref, narrow_ref, cols) in enumerate(
        ((x_ref, b_ref, leave_cols), (dy_ref, c_ref, enter_cols))
    ):
        loads[2 + 2 * side].wait()
        loads[3 + 2 * side].wait()
        narrow = narrow_ref[...]
        for chunk in range(WIDE // width):
            low = chunk * width
            at = slice(low // rows, (low + width) // rows)
            weighted = wide_ref[:, low : low + width].astype(FULL) * spread(cols, low, width)
            product = mul(weighted.astype(LOW), narrow, TN).astype(LOW)
            out_ref[at, side * rows : (side + 1) * rows, :] = product.reshape(
                width // rows, rows, STATE
            )
    total = jnp.broadcast_to(total, (HEADS, STATE))
    high = total.astype(LOW).astype(FULL)
    per_head = slices // HEADS
    for head in range(HEADS):
        rest = jnp.broadcast_to((total - high)[head : head + 1], (8, STATE))
        tile = jnp.where(iota((8, STATE), 0) == 0, high[head : head + 1], rest).astype(LOW)
        for part in range(per_head):
            out_ref[head * per_head + part, 2 * rows : 2 * rows + 8, :] = tile


def fetches_sibling():
    return lax.rem(lax.axis_index("seq"), 2) == 0


def pass_through(pieces, w_b_hbm, w_c_hbm, load_sems, sent_sems):
    pairs = []
    for rows, held_ref, _ in pieces:
        pairs.append((w_b_hbm.at[rows, :], held_ref.at[:, pl.ds(0, STATE)]))
        pairs.append((w_c_hbm.at[rows, :], held_ref.at[:, pl.ds(STATE, STATE)]))
    loads = fetch(pairs, load_sems)
    sends = []
    for at, (_, held_ref, sent_ref) in enumerate(pieces):
        loads[2 * at].wait()
        loads[2 * at + 1].wait()
        sends.append(pltpu.make_async_copy(held_ref, sent_ref, sent_sems.at[at]))
        sends[-1].start()
    for send in sends:
        send.wait()


def stage_kernel(_, w_b_hbm, w_c_hbm, *refs):
    sent_refs, held_refs, sems = refs[: len(ROUTE)], refs[len(ROUTE) : -2], refs[-2:]
    part = sent_refs[0].shape[0]
    me = lax.axis_index("tp")
    core, chips = lax.rem(me, CORES), lax.axis_size("tp") // CORES
    half = lax.rem(core + 1 + lax.rem(lax.axis_index("seq"), 2), CORES)
    pieces = []
    for (step, first, parts), held_ref, sent_ref in zip(ROUTE, held_refs, sent_refs):
        target = lax.rem(me // CORES + step, chips)
        row = (target * CORES + half) * 2 * part + first * part
        pieces.append((pl.ds(pl.multiple_of(row, part), parts * part), held_ref, sent_ref))
    pass_through(pieces, w_b_hbm, w_c_hbm, *sems)


def own_kernel(w_b_hbm, w_c_hbm, out_ref, held_ref, *sems):
    columns = out_ref.shape[0] // CORES
    me = lax.axis_index("tp")
    core = lax.rem(me, CORES)
    pieces = []
    for which, other in enumerate((1 - core, core)):
        row = pl.multiple_of((me - core + other) * columns, columns)
        to = pl.ds(which * columns, columns)
        pieces.append((pl.ds(row, columns), held_ref.at[to, :], out_ref.at[to, :]))
    pass_through(pieces, w_b_hbm, w_c_hbm, *sems)


def scan_kernel(in_ref, *refs):
    out_ref = refs[-1]
    devices, rows = out_ref.shape[0], out_ref.shape[1] // 2
    decays = []
    for at in range(devices):
        pair = in_ref[at, 2 * rows : 2 * rows + 8, :].astype(FULL)
        decays.append(pair[0:1] + pair[1:2])
    state = jnp.zeros((rows, STATE), FULL)
    for at in range(devices):
        out_ref[at, 0:rows, :] = state.astype(LOW)
        state = decays[at] * state + in_ref[at, 0:rows, :].astype(FULL)
    state = jnp.zeros((rows, STATE), FULL)
    for at in reversed(range(devices)):
        out_ref[at, rows : 2 * rows, :] = state.astype(LOW)
        state = decays[at] * state + in_ref[at, rows : 2 * rows, :].astype(FULL)


def local_kernel(
    lengths_hbm,
    log_hbm,
    x_hbm,
    b_hbm,
    dy_hbm,
    c_hbm,
    grad_x_ref,
    terms_ref,
    leave_ref,
    lengths_ref,
    log_ref,
    x_ref,
    b_ref,
    dy_ref,
    c_ref,
    sems,
):
    loads = fetch(
        [
            (lengths_hbm, lengths_ref),
            (log_hbm, log_ref),
            (x_hbm, x_ref),
            (b_hbm, b_ref),
            (dy_hbm, dy_ref),
            (c_hbm, c_ref),
        ],
        sems,
    )
    for load in loads:
        load.wait()
    first_row, ends, cumulative, docs, enter, leave, _ = token_vectors(log_ref, lengths_ref)
    enter_cols, leave_cols = split_columns(enter), split_columns(leave)
    leave_ref[...] = leave_cols
    cum_cols = cumulative.T
    middle = doc_of(first_row + SPAN - 1, ends)
    cum_middle = cumulative[:, SPAN - 1 : SPAN]
    leave_first = jnp.where(
        docs[:, :SPAN] == middle, jnp.exp(cum_middle - cumulative[:, :SPAN]), 0.0
    )
    enter_second = jnp.where(
        docs[:, SPAN:] == middle, jnp.exp(cumulative[:, SPAN:] - cum_middle), 0.0
    )
    leave_first, enter_second = split_columns(leave_first), split_columns(enter_second)
    b, c = b_ref[...], c_ref[...]
    scores = mul(b, c, NT)
    cross_scores = scores[:SPAN, SPAN:].astype(LOW)
    is_left = iota((SPAN, LANES), 1) < HEAD_DIM
    masks = []
    for number in range(2):
        base = first_row + number * SPAN
        same = doc_of(base + iota((SPAN, SPAN), 0), ends) == doc_of(
            base + iota((SPAN, SPAN), 1), ends
        )
        masks.append(same & (iota((SPAN, SPAN), 0) <= iota((SPAN, SPAN), 1)))

    def halves(value):
        zero = jnp.zeros_like(value)
        return jnp.concatenate(
            [jnp.where(is_left, value, zero), jnp.where(is_left, zero, value)], axis=0
        )

    mixed = [jnp.zeros((SPAN, SPAN), FULL), jnp.zeros((SPAN, SPAN), FULL)]
    mixed_cross = jnp.zeros((SPAN, SPAN), FULL)
    for pair in range(PAIRS):
        low = pair * LANES
        x, dy = x_ref[:, low : low + LANES], dy_ref[:, low : low + LANES]
        for side, (wide, cols) in enumerate(((x, leave_cols), (dy, enter_cols))):
            weighted = (wide.astype(FULL) * spread(cols, low, LANES)).astype(LOW)
            terms_ref[:, side * WIDE + low : side * WIDE + low + LANES] = weighted
        first_wide = spread(leave_first, low, LANES)
        x_first = (x[:SPAN].astype(FULL) * first_wide).astype(LOW)
        dy_second = (dy[SPAN:].astype(FULL) * spread(enter_second, low, LANES)).astype(LOW)
        mixed_cross += mul(x_first, dy_second, NT)
        pieces = [first_wide * mul(cross_scores, dy_second), 0.0]
        for number in range(2):
            span = slice(number * SPAN, (number + 1) * SPAN)
            inner = mul(halves(x[span]), dy[span], NT)
            low_scores = []
            for side in range(2):
                head = 2 * pair + side
                gaps = cumulative[head : head + 1, span] - cum_cols[span, head : head + 1]
                within = jnp.exp(jnp.where(masks[number], gaps, -1e30))
                mixed[number] += within * inner[side * SPAN : (side + 1) * SPAN]
                low_scores.append((within * scores[span, span]).astype(LOW))
            grad_x_ref[span, low : low + LANES] = pieces[number] + mul(
                jnp.concatenate(low_scores, axis=1), halves(dy[span])
            )
    nothing = jnp.zeros((SPAN, SPAN), FULL)
    table = jnp.concatenate(
        [
            jnp.concatenate([mixed[0], mixed_cross], axis=1),
            jnp.concatenate([nothing, mixed[1]], axis=1),
        ],
        axis=0,
    )
    for side, part in enumerate((mul(table.astype(LOW), c), mul(table.T.astype(LOW), b))):
        high = part.astype(LOW)
        low = 2 * (WIDE + side * STATE)
        terms_ref[:, low : low + STATE] = high
        terms_ref[:, low + STATE : low + 2 * STATE] = (part - high.astype(FULL)).astype(LOW)


def grad_bc_kernel(terms_ref, edge_ref, out_ref):
    rows = edge_ref.shape[1] // 2
    for side in range(2):
        which = slice(rows, 2 * rows) if side == 0 else slice(0, rows)
        edge = edge_ref[:, which, :].reshape(WIDE, STATE)
        total = mul(terms_ref[:, side * WIDE : (side + 1) * WIDE], edge)
        low = 2 * (WIDE + side * STATE)
        for part in range(2):
            total += terms_ref[:, low + part * STATE : low + (part + 1) * STATE].astype(FULL)
        out_ref[:, side * STATE : (side + 1) * STATE] = total.astype(LOW)


def grad_x_kernel(b_ref, leave_ref, local_ref, edge_ref, out_ref, done_ref):
    done_ref[...] = jnp.zeros_like(done_ref)
    rows = edge_ref.shape[1] // 2
    width = 2 * LANES
    for chunk in range(WIDE // width):
        low = chunk * width
        at = slice(low // rows, (low + width) // rows)
        end = edge_ref[at, rows : 2 * rows, :].reshape(width, STATE)
        later = spread(leave_ref[...], low, width) * mul(b_ref[...], end, NT)
        out_ref[:, low : low + width] = (local_ref[:, low : low + width] + later).astype(LOW)


def project_kernel(*refs, sibling):
    grads, own, fetched, given, (_, out_ref) = refs[:4], refs[4], refs[5:9], refs[9:13], refs[13:]
    columns = out_ref.shape[1]
    half = slice(0, columns) if sibling else slice(columns, 2 * columns)

    def products(weights):
        twice_first, twice_second, up, down = weights
        total = mul(grads[0][...], own[half, :], NT)
        total += mul(grads[1][...], up[...], NT)
        total += mul(grads[3][...], down[...], NT)
        twice = [mul(grads[2][...], part[...], NT) for part in (twice_first, twice_second)]
        out_ref[...] = (total + jnp.concatenate(twice, axis=1)).astype(out_ref.dtype)

    here = fetches_sibling() if sibling else jnp.logical_not(fetches_sibling())
    pl.when(here)(lambda: products(fetched))
    pl.when(jnp.logical_not(here))(lambda: products(given))


def sum_kernel(kept_ref, received_ref, out_ref):
    out_ref[...] = (kept_ref[...] + received_ref[...].astype(FULL)).astype(LOW)


BLOCK = pl.BlockSpec(memory_space=pltpu.VMEM)
HBM = pl.BlockSpec(memory_space=pltpu.HBM)


def call(body, out_shape, specs, vmem, out_specs=BLOCK, scratch=()):
    return pl.pallas_call(
        body,
        out_shape=out_shape,
        in_specs=specs,
        out_specs=out_specs,
        scratch_shapes=scratch,
        compiler_params=pltpu.CompilerParams(vmem_limit_bytes=vmem),
        cost_estimate=pl.CostEstimate(flops=1000, bytes_accessed=1000, transcendentals=0),
    )


def along_x(value, step):
    devices = lax.axis_size("tp")
    return lax.ppermute(
        value, "tp", [(at, (at + CORES * step) % devices) for at in range(devices)]
    )


def along_y(value, step):
    pairs = []
    for at in range(lax.axis_size("seq")):
        y = at % ALONG_Y
        pairs.append((at, at - y + (y + step) % ALONG_Y))
    return lax.ppermute(value, "seq", pairs)


def per_device(inner_x, in_b, in_c, log_decay, doc_lengths, out_grad, w_b, w_c):
    tokens = inner_x.shape[0]
    devices = lax.axis_size("seq")
    rows = WIDE // devices
    columns = w_b.shape[0] // lax.axis_size("tp")
    local = (doc_lengths, log_decay, inner_x, in_b, out_grad, in_c)
    dma = pltpu.SemaphoreType.DMA
    shape = jax.ShapeDtypeStruct
    held = [pltpu.SMEM(doc_lengths.shape, doc_lengths.dtype)] + [
        pltpu.VMEM(a.shape, a.dtype) for a in local[1:]
    ]
    summary = call(
        summary_kernel,
        shape((devices, 2 * rows + 8, STATE), LOW),
        [HBM] * 6,
        LARGE_VMEM,
        BLOCK,
        held + [dma((6,))],
    )(*local)
    pieces = [(parts * columns // 2, 2 * STATE) for _, _, parts in ROUTE]
    own = (CORES * columns, 2 * STATE)
    sent = call(
        stage_kernel,
        [shape(piece, LOW) for piece in pieces],
        [HBM] * 3,
        LARGE_VMEM,
        [HBM] * len(pieces),
        [pltpu.VMEM(piece, LOW) for piece in pieces]
        + [dma((2 * len(pieces),)), dma((len(pieces),))],
    )(summary, w_b, w_c)
    own = call(
        own_kernel,
        shape(own, LOW),
        [HBM] * 2,
        LARGE_VMEM,
        HBM,
        [pltpu.VMEM(own, LOW), dma((4,)), dma((2,))],
    )(w_b, w_c)
    ways = (1, 3, 1, 3)
    fetched = [along_x(piece, way) for piece, way in zip(sent, ways)]
    early = list(fetched)
    fetched[:2] = [along_x(piece, way) for piece, way in zip(fetched[:2], ways)]
    given = [along_y(piece, way) for piece, way in zip(fetched, ways)]
    summary = lax.all_to_all(summary, "seq", 0, 0)
    grad_x, terms, leave_cols = call(
        local_kernel,
        [
            shape((tokens, WIDE), FULL),
            shape((tokens, 2 * WIDE + 4 * STATE), LOW),
            shape((tokens, 2 * HEADS), LOW),
        ],
        [HBM] * 6,
        16 * MIB,
        [BLOCK] * 3,
        held + [dma((6,))],
    )(*local)
    edges = call(
        scan_kernel,
        shape((devices, 2 * rows, STATE), LOW),
        [BLOCK] + [HBM] * (1 + len(early)),
        4 * MIB,
    )(summary, leave_cols, *early)
    edges = lax.all_to_all(edges, "seq", 0, 0)
    grad_bc = call(
        grad_bc_kernel,
        shape((tokens, 2 * STATE), LOW),
        [BLOCK] * 2,
        8 * MIB,
    )(terms, edges)
    others = [along_x(grad_bc, step) for step in (1, 2, 3)]
    grad_x, done = call(
        grad_x_kernel,
        [shape((tokens, WIDE), LOW), shape((8, LANES), FULL)],
        [BLOCK] * 4,
        8 * MIB,
        [BLOCK] * 2,
    )(in_b, leave_cols, grad_x, edges)

    def project(sibling, kind):
        return call(
            functools.partial(project_kernel, sibling=sibling),
            shape((tokens, columns), kind),
            [BLOCK] * 14,
            16 * MIB,
        )(grad_bc, *others, own, *fetched, *given, done)

    partner = [(at, at ^ 1) for at in range(lax.axis_size("tp"))]
    received = lax.ppermute(project(True, LOW), "tp", partner)
    grad_input = call(sum_kernel, shape((tokens, columns), LOW), [BLOCK] * 2, 8 * MIB)(
        project(False, FULL), received
    )
    return grad_x, grad_input


def solution(mesh):
    placed = (
        P("seq", "tp"),
        P("seq", "tp"),
        P("seq", "tp"),
        P("tp", "seq"),
        P(),
        P("seq", "tp"),
        P(None, "tp"),
        P(None, "tp"),
    )
    return jax.shard_map(
        per_device,
        mesh=mesh,
        in_specs=placed,
        out_specs=(P("seq", "tp"), P("seq", "tp")),
        check_vma=False,
    )
```

```python
import functools

import jax
import jax.numpy as jnp
from jax import lax
from jax.experimental import pallas as pl
from jax.experimental.pallas import tpu as pltpu
from jax.sharding import PartitionSpec as P

HEAD_DIM = 64
STATE = 128
SPAN = 128
HEADS = 16
LANES = 128
WIDE = HEADS * HEAD_DIM
PAIRS = WIDE // LANES
CORES = 2
ALONG_Y = 4
ROUTE = ((2, 1), (2, 1), (1, 4), (3, 4))
LOW = jnp.bfloat16
FULL = jnp.float32
NN = (((1,), (0,)), ((), ()))
NT = (((1,), (1,)), ((), ()))
TN = (((0,), (0,)), ((), ()))
MIB = 1024 * 1024
LARGE_VMEM = 56 * MIB


def mul(a, b, dims=NN):
    return lax.dot_general(a, b, dims, preferred_element_type=FULL)


def iota(shape, axis):
    return lax.broadcasted_iota(jnp.int32, shape, axis)


def doc_of(positions, ends):
    return sum((positions >= end).astype(jnp.int32) for end in ends)


def doc_ends(lengths_ref):
    first = lengths_ref[0]
    second = first + lengths_ref[1]
    return (first, second, second + lengths_ref[2])


def token_vectors(log_ref, lengths_ref):
    tokens = log_ref.shape[1]
    first_row = lax.axis_index("seq") * tokens
    ends = doc_ends(lengths_ref)
    upper = (iota((tokens, tokens), 0) <= iota((tokens, tokens), 1)).astype(FULL)
    cumulative = lax.dot_general(
        log_ref[...], upper, NN, precision=lax.Precision.HIGHEST, preferred_element_type=FULL
    )
    docs = doc_of(first_row + iota((HEADS, tokens), 1), ends)
    prior = jnp.where(first_row > 0, doc_of(first_row - 1, ends), -1)
    last = doc_of(first_row + tokens - 1, ends)
    cum_last = cumulative[:, tokens - 1 :]
    enter = jnp.where(docs == prior, jnp.exp(cumulative), 0.0)
    leave = jnp.where(docs == last, jnp.exp(cum_last - cumulative), 0.0)
    total = jnp.where(last == prior, jnp.exp(cum_last), 0.0)
    return first_row, ends, cumulative, docs, enter, leave, total


def split_columns(rows):
    high = rows.astype(LOW).astype(FULL)
    both = jnp.concatenate([high, rows - high], axis=0)
    return both.T.astype(LOW)


def spread(columns, low, width):
    head = (low + iota((2 * HEADS, width), 1)) // HEAD_DIM
    pick = (head == iota((2 * HEADS, width), 0) % HEADS).astype(FULL).astype(LOW)
    return mul(columns, pick)


def fetch(pairs, sems):
    copies = [
        pltpu.make_async_copy(source, target, sems.at[at])
        for at, (source, target) in enumerate(pairs)
    ]
    for copy in copies:
        copy.start()
    return copies


def summary_kernel(
    lengths_hbm,
    log_hbm,
    x_hbm,
    b_hbm,
    dy_hbm,
    c_hbm,
    out_ref,
    lengths_ref,
    log_ref,
    x_ref,
    b_ref,
    dy_ref,
    c_ref,
    sems,
):
    loads = fetch(
        [
            (lengths_hbm, lengths_ref),
            (log_hbm, log_ref),
            (x_hbm, x_ref),
            (b_hbm, b_ref),
            (dy_hbm, dy_ref),
            (c_hbm, c_ref),
        ],
        sems,
    )
    slices = out_ref.shape[0]
    rows = WIDE // slices
    loads[0].wait()
    loads[1].wait()
    _, _, _, _, enter, leave, total = token_vectors(log_ref, lengths_ref)
    enter_cols = split_columns(enter)
    leave_cols = split_columns(leave)
    width = 2 * LANES
    for side, (wide_ref, narrow_ref, cols) in enumerate(
        ((x_ref, b_ref, leave_cols), (dy_ref, c_ref, enter_cols))
    ):
        loads[2 + 2 * side].wait()
        loads[3 + 2 * side].wait()
        narrow = narrow_ref[...]
        for chunk in range(WIDE // width):
            low = chunk * width
            at = slice(low // rows, (low + width) // rows)
            weighted = wide_ref[:, low : low + width].astype(FULL) * spread(cols, low, width)
            product = mul(weighted.astype(LOW), narrow, TN).astype(LOW)
            out_ref[at, side * rows : (side + 1) * rows, :] = product.reshape(
                width // rows, rows, STATE
            )
    total = jnp.broadcast_to(total, (HEADS, STATE))
    high = total.astype(LOW).astype(FULL)
    per_head = slices // HEADS
    for head in range(HEADS):
        rest = jnp.broadcast_to((total - high)[head : head + 1], (8, STATE))
        tile = jnp.where(iota((8, STATE), 0) == 0, high[head : head + 1], rest).astype(LOW)
        for part in range(per_head):
            out_ref[head * per_head + part, 2 * rows : 2 * rows + 8, :] = tile


def fetches_sibling():
    return lax.rem(lax.axis_index("seq"), 2) == 0


def pass_through(pieces, w_b_hbm, w_c_hbm, load_sems, sent_sems):
    pairs = []
    for rows, held_ref, _ in pieces:
        pairs.append((w_b_hbm.at[rows, :], held_ref.at[:, pl.ds(0, STATE)]))
        pairs.append((w_c_hbm.at[rows, :], held_ref.at[:, pl.ds(STATE, STATE)]))
    loads = fetch(pairs, load_sems)
    sends = []
    for at, (_, held_ref, sent_ref) in enumerate(pieces):
        loads[2 * at].wait()
        loads[2 * at + 1].wait()
        sends.append(pltpu.make_async_copy(held_ref, sent_ref, sent_sems.at[at]))
        sends[-1].start()
    for send in sends:
        send.wait()


def stage_kernel(_, w_b_hbm, w_c_hbm, *refs):
    sent_refs, held_refs, sems = refs[: len(ROUTE)], refs[len(ROUTE) : -2], refs[-2:]
    part = sent_refs[0].shape[0]
    columns = 2 * part
    me = lax.axis_index("tp")
    core, chips = lax.rem(me, CORES), lax.axis_size("tp") // CORES
    half = lax.rem(core + 1 + lax.rem(lax.axis_index("seq"), 2), CORES)
    pieces = []
    for at, ((step, _), held_ref, sent_ref) in enumerate(zip(ROUTE, held_refs, sent_refs)):
        first = lax.rem(me // CORES + step, chips) * CORES
        if at < 2:
            row = pl.multiple_of((first + half) * columns + at * part, part)
            pieces.append((pl.ds(row, part), held_ref, sent_ref))
        else:
            for which, other in enumerate((1 - core, core)):
                row = pl.multiple_of((first + other) * columns, columns)
                to = pl.ds(which * columns, columns)
                pieces.append((pl.ds(row, columns), held_ref.at[to, :], sent_ref.at[to, :]))
    pass_through(pieces, w_b_hbm, w_c_hbm, *sems)


def own_kernel(w_b_hbm, w_c_hbm, out_ref, held_ref, *sems):
    columns = out_ref.shape[0] // CORES
    me = lax.axis_index("tp")
    core = lax.rem(me, CORES)
    pieces = []
    for which, other in enumerate((1 - core, core)):
        row = pl.multiple_of((me - core + other) * columns, columns)
        to = pl.ds(which * columns, columns)
        pieces.append((pl.ds(row, columns), held_ref.at[to, :], out_ref.at[to, :]))
    pass_through(pieces, w_b_hbm, w_c_hbm, *sems)


def scan_kernel(in_ref, _, out_ref):
    devices, rows = out_ref.shape[0], out_ref.shape[1] // 2
    decays = []
    for at in range(devices):
        pair = in_ref[at, 2 * rows : 2 * rows + 8, :].astype(FULL)
        decays.append(pair[0:1] + pair[1:2])
    state = jnp.zeros((rows, STATE), FULL)
    for at in range(devices):
        out_ref[at, 0:rows, :] = state.astype(LOW)
        state = decays[at] * state + in_ref[at, 0:rows, :].astype(FULL)
    state = jnp.zeros((rows, STATE), FULL)
    for at in reversed(range(devices)):
        out_ref[at, rows : 2 * rows, :] = state.astype(LOW)
        state = decays[at] * state + in_ref[at, rows : 2 * rows, :].astype(FULL)


def local_kernel(
    lengths_hbm,
    log_hbm,
    x_hbm,
    b_hbm,
    dy_hbm,
    c_hbm,
    grad_x_ref,
    terms_ref,
    leave_ref,
    lengths_ref,
    log_ref,
    x_ref,
    b_ref,
    dy_ref,
    c_ref,
    sems,
):
    loads = fetch(
        [
            (lengths_hbm, lengths_ref),
            (log_hbm, log_ref),
            (x_hbm, x_ref),
            (b_hbm, b_ref),
            (dy_hbm, dy_ref),
            (c_hbm, c_ref),
        ],
        sems,
    )
    for load in loads:
        load.wait()
    first_row, ends, cumulative, docs, enter, leave, _ = token_vectors(log_ref, lengths_ref)
    enter_cols, leave_cols = split_columns(enter), split_columns(leave)
    leave_ref[...] = leave_cols
    cum_cols = cumulative.T
    middle = doc_of(first_row + SPAN - 1, ends)
    cum_middle = cumulative[:, SPAN - 1 : SPAN]
    leave_first = jnp.where(
        docs[:, :SPAN] == middle, jnp.exp(cum_middle - cumulative[:, :SPAN]), 0.0
    )
    enter_second = jnp.where(
        docs[:, SPAN:] == middle, jnp.exp(cumulative[:, SPAN:] - cum_middle), 0.0
    )
    leave_first, enter_second = split_columns(leave_first), split_columns(enter_second)
    b, c = b_ref[...], c_ref[...]
    scores = mul(b, c, NT)
    cross_scores = scores[:SPAN, SPAN:].astype(LOW)
    is_left = iota((SPAN, LANES), 1) < HEAD_DIM
    masks = []
    for number in range(2):
        base = first_row + number * SPAN
        same = doc_of(base + iota((SPAN, SPAN), 0), ends) == doc_of(
            base + iota((SPAN, SPAN), 1), ends
        )
        masks.append(same & (iota((SPAN, SPAN), 0) <= iota((SPAN, SPAN), 1)))

    def halves(value):
        zero = jnp.zeros_like(value)
        return jnp.concatenate(
            [jnp.where(is_left, value, zero), jnp.where(is_left, zero, value)], axis=0
        )

    mixed = [jnp.zeros((SPAN, SPAN), FULL), jnp.zeros((SPAN, SPAN), FULL)]
    mixed_cross = jnp.zeros((SPAN, SPAN), FULL)
    for pair in range(PAIRS):
        low = pair * LANES
        x, dy = x_ref[:, low : low + LANES], dy_ref[:, low : low + LANES]
        for side, (wide, cols) in enumerate(((x, leave_cols), (dy, enter_cols))):
            weighted = (wide.astype(FULL) * spread(cols, low, LANES)).astype(LOW)
            terms_ref[:, side * WIDE + low : side * WIDE + low + LANES] = weighted
        first_wide = spread(leave_first, low, LANES)
        x_first = (x[:SPAN].astype(FULL) * first_wide).astype(LOW)
        dy_second = (dy[SPAN:].astype(FULL) * spread(enter_second, low, LANES)).astype(LOW)
        mixed_cross += mul(x_first, dy_second, NT)
        pieces = [first_wide * mul(cross_scores, dy_second), 0.0]
        for number in range(2):
            span = slice(number * SPAN, (number + 1) * SPAN)
            inner = mul(halves(x[span]), dy[span], NT)
            low_scores = []
            for side in range(2):
                head = 2 * pair + side
                gaps = cumulative[head : head + 1, span] - cum_cols[span, head : head + 1]
                within = jnp.exp(jnp.where(masks[number], gaps, -1e30))
                mixed[number] += within * inner[side * SPAN : (side + 1) * SPAN]
                low_scores.append((within * scores[span, span]).astype(LOW))
            grad_x_ref[span, low : low + LANES] = pieces[number] + mul(
                jnp.concatenate(low_scores, axis=1), halves(dy[span])
            )
    nothing = jnp.zeros((SPAN, SPAN), FULL)
    table = jnp.concatenate(
        [
            jnp.concatenate([mixed[0], mixed_cross], axis=1),
            jnp.concatenate([nothing, mixed[1]], axis=1),
        ],
        axis=0,
    )
    for side, part in enumerate((mul(table.astype(LOW), c), mul(table.T.astype(LOW), b))):
        high = part.astype(LOW)
        low = 2 * (WIDE + side * STATE)
        terms_ref[:, low : low + STATE] = high
        terms_ref[:, low + STATE : low + 2 * STATE] = (part - high.astype(FULL)).astype(LOW)


def grad_bc_kernel(terms_ref, edge_ref, *refs):
    out_ref = refs[-1]
    rows = edge_ref.shape[1] // 2
    for side in range(2):
        which = slice(rows, 2 * rows) if side == 0 else slice(0, rows)
        edge = edge_ref[:, which, :].reshape(WIDE, STATE)
        total = mul(terms_ref[:, side * WIDE : (side + 1) * WIDE], edge)
        low = 2 * (WIDE + side * STATE)
        for part in range(2):
            total += terms_ref[:, low + part * STATE : low + (part + 1) * STATE].astype(FULL)
        out_ref[:, side * STATE : (side + 1) * STATE] = total.astype(LOW)


def grad_x_kernel(b_ref, leave_ref, local_ref, edge_ref, out_ref, done_ref):
    done_ref[...] = jnp.zeros_like(done_ref)
    rows = edge_ref.shape[1] // 2
    width = 2 * LANES
    for chunk in range(WIDE // width):
        low = chunk * width
        at = slice(low // rows, (low + width) // rows)
        end = edge_ref[at, rows : 2 * rows, :].reshape(width, STATE)
        later = spread(leave_ref[...], low, width) * mul(b_ref[...], end, NT)
        out_ref[:, low : low + width] = (local_ref[:, low : low + width] + later).astype(LOW)


def project_kernel(*refs, sibling):
    grads, (own, up, down), fetched, given, (_, out_ref) = (
        refs[:4],
        refs[4:7],
        refs[7:9],
        refs[9:11],
        refs[11:],
    )
    columns = out_ref.shape[1]
    half = slice(0, columns) if sibling else slice(columns, 2 * columns)
    total = mul(grads[0][...], own[half, :], NT)
    total += mul(grads[1][...], up[half, :], NT)
    total += mul(grads[3][...], down[half, :], NT)

    def finish(pieces):
        twice = jnp.concatenate([mul(grads[2][...], piece[...], NT) for piece in pieces], axis=1)
        out_ref[...] = (total + twice).astype(out_ref.dtype)

    here = fetches_sibling() if sibling else jnp.logical_not(fetches_sibling())
    pl.when(here)(lambda: finish(fetched))
    pl.when(jnp.logical_not(here))(lambda: finish(given))


def sum_kernel(kept_ref, received_ref, out_ref):
    out_ref[...] = (kept_ref[...] + received_ref[...].astype(FULL)).astype(LOW)


BLOCK = pl.BlockSpec(memory_space=pltpu.VMEM)
HBM = pl.BlockSpec(memory_space=pltpu.HBM)


def call(body, out_shape, specs, vmem, out_specs=BLOCK, scratch=()):
    return pl.pallas_call(
        body,
        out_shape=out_shape,
        in_specs=specs,
        out_specs=out_specs,
        scratch_shapes=scratch,
        compiler_params=pltpu.CompilerParams(vmem_limit_bytes=vmem),
        cost_estimate=pl.CostEstimate(flops=1000, bytes_accessed=1000, transcendentals=0),
    )


def along_x(value, step):
    devices = lax.axis_size("tp")
    return lax.ppermute(
        value, "tp", [(at, (at + CORES * step) % devices) for at in range(devices)]
    )


def along_y(value, step):
    pairs = []
    for at in range(lax.axis_size("seq")):
        y = at % ALONG_Y
        pairs.append((at, at - y + (y + step) % ALONG_Y))
    return lax.ppermute(value, "seq", pairs)


def per_device(inner_x, in_b, in_c, log_decay, doc_lengths, out_grad, w_b, w_c):
    tokens = inner_x.shape[0]
    devices = lax.axis_size("seq")
    rows = WIDE // devices
    columns = w_b.shape[0] // lax.axis_size("tp")
    local = (doc_lengths, log_decay, inner_x, in_b, out_grad, in_c)
    dma = pltpu.SemaphoreType.DMA
    shape = jax.ShapeDtypeStruct
    held = [pltpu.SMEM(doc_lengths.shape, doc_lengths.dtype)] + [
        pltpu.VMEM(a.shape, a.dtype) for a in local[1:]
    ]
    summary = call(
        summary_kernel,
        shape((devices, 2 * rows + 8, STATE), LOW),
        [HBM] * 6,
        LARGE_VMEM,
        BLOCK,
        held + [dma((6,))],
    )(*local)
    pieces = [(parts * columns // 2, 2 * STATE) for _, parts in ROUTE]
    own = (CORES * columns, 2 * STATE)
    sent = call(
        stage_kernel,
        [shape(piece, LOW) for piece in pieces],
        [HBM] * 3,
        LARGE_VMEM,
        [HBM] * len(pieces),
        [pltpu.VMEM(piece, LOW) for piece in pieces]
        + [dma((12,)), dma((6,))],
    )(summary, w_b, w_c)
    own = call(
        own_kernel,
        shape(own, LOW),
        [HBM] * 2,
        LARGE_VMEM,
        HBM,
        [pltpu.VMEM(own, LOW), dma((4,)), dma((2,))],
    )(w_b, w_c)
    ways = (1, 3)
    up, down = [along_x(piece, way) for piece, way in zip(sent[2:], ways)]
    fetched = [along_x(piece, way) for piece, way in zip(sent[:2], ways)]
    fetched = [along_x(piece, way) for piece, way in zip(fetched, ways)]
    given = [along_y(piece, way) for piece, way in zip(fetched, ways)]
    summary = lax.all_to_all(summary, "seq", 0, 0)
    grad_x, terms, leave_cols = call(
        local_kernel,
        [
            shape((tokens, WIDE), FULL),
            shape((tokens, 2 * WIDE + 4 * STATE), LOW),
            shape((tokens, 2 * HEADS), LOW),
        ],
        [HBM] * 6,
        16 * MIB,
        [BLOCK] * 3,
        held + [dma((6,))],
    )(*local)
    edges = call(
        scan_kernel,
        shape((devices, 2 * rows, STATE), LOW),
        [BLOCK, HBM],
        4 * MIB,
    )(summary, leave_cols)
    edges = lax.all_to_all(edges, "seq", 0, 0)
    grad_bc = call(
        grad_bc_kernel,
        shape((tokens, 2 * STATE), LOW),
        [BLOCK, BLOCK, HBM, HBM],
        8 * MIB,
    )(terms, edges, up, down)
    others = [along_x(grad_bc, step) for step in (1, 2, 3)]
    grad_x, done = call(
        grad_x_kernel,
        [shape((tokens, WIDE), LOW), shape((8, LANES), FULL)],
        [BLOCK] * 4,
        8 * MIB,
        [BLOCK] * 2,
    )(in_b, leave_cols, grad_x, edges)

    def project(sibling, kind):
        return call(
            functools.partial(project_kernel, sibling=sibling),
            shape((tokens, columns), kind),
            [BLOCK] * 12,
            16 * MIB,
        )(grad_bc, *others, own, up, down, *fetched, *given, done)

    partner = [(at, at ^ 1) for at in range(lax.axis_size("tp"))]
    received = lax.ppermute(project(True, LOW), "tp", partner)
    grad_input = call(sum_kernel, shape((tokens, columns), LOW), [BLOCK] * 2, 8 * MIB)(
        project(False, FULL), received
    )
    return grad_x, grad_input


def solution(mesh):
    placed = (
        P("seq", "tp"),
        P("seq", "tp"),
        P("seq", "tp"),
        P("tp", "seq"),
        P(),
        P("seq", "tp"),
        P(None, "tp"),
        P(None, "tp"),
    )
    return jax.shard_map(
        per_device,
        mesh=mesh,
        in_specs=placed,
        out_specs=(P("seq", "tp"), P("seq", "tp")),
        check_vma=False,
    )
```

```python
import functools

import jax
import jax.numpy as jnp
from jax import lax
from jax.experimental import pallas as pl
from jax.experimental.pallas import tpu as pltpu
from jax.sharding import PartitionSpec as P

HEAD_DIM = 64
STATE = 128
SPAN = 128
HEADS = 16
LANES = 128
WIDE = HEADS * HEAD_DIM
PAIRS = WIDE // LANES
CORES = 2
ALONG_Y = 4
ROUTE = ((2, 1), (2, 1), (1, 4), (3, 4))
LOW = jnp.bfloat16
FULL = jnp.float32
NN = (((1,), (0,)), ((), ()))
NT = (((1,), (1,)), ((), ()))
TN = (((0,), (0,)), ((), ()))
MIB = 1024 * 1024
LARGE_VMEM = 56 * MIB


def mul(a, b, dims=NN):
    return lax.dot_general(a, b, dims, preferred_element_type=FULL)


def iota(shape, axis):
    return lax.broadcasted_iota(jnp.int32, shape, axis)


def doc_of(positions, ends):
    return sum((positions >= end).astype(jnp.int32) for end in ends)


def doc_ends(lengths_ref):
    first = lengths_ref[0]
    second = first + lengths_ref[1]
    return (first, second, second + lengths_ref[2])


def token_vectors(log_ref, lengths_ref):
    tokens = log_ref.shape[1]
    first_row = lax.axis_index("seq") * tokens
    ends = doc_ends(lengths_ref)
    upper = (iota((tokens, tokens), 0) <= iota((tokens, tokens), 1)).astype(FULL)
    cumulative = lax.dot_general(
        log_ref[...], upper, NN, precision=lax.Precision.HIGHEST, preferred_element_type=FULL
    )
    docs = doc_of(first_row + iota((HEADS, tokens), 1), ends)
    prior = jnp.where(first_row > 0, doc_of(first_row - 1, ends), -1)
    last = doc_of(first_row + tokens - 1, ends)
    cum_last = cumulative[:, tokens - 1 :]
    enter = jnp.where(docs == prior, jnp.exp(cumulative), 0.0)
    leave = jnp.where(docs == last, jnp.exp(cum_last - cumulative), 0.0)
    total = jnp.where(last == prior, jnp.exp(cum_last), 0.0)
    return first_row, ends, cumulative, docs, enter, leave, total


def split_columns(rows):
    high = rows.astype(LOW).astype(FULL)
    both = jnp.concatenate([high, rows - high], axis=0)
    return both.T.astype(LOW)


def spread(columns, low, width):
    head = (low + iota((2 * HEADS, width), 1)) // HEAD_DIM
    pick = (head == iota((2 * HEADS, width), 0) % HEADS).astype(FULL).astype(LOW)
    return mul(columns, pick)


def fetch(pairs, sems):
    copies = [
        pltpu.make_async_copy(source, target, sems.at[at])
        for at, (source, target) in enumerate(pairs)
    ]
    for copy in copies:
        copy.start()
    return copies


def summary_kernel(
    lengths_hbm,
    log_hbm,
    x_hbm,
    b_hbm,
    dy_hbm,
    c_hbm,
    out_ref,
    lengths_ref,
    log_ref,
    x_ref,
    b_ref,
    dy_ref,
    c_ref,
    sems,
):
    loads = fetch(
        [
            (lengths_hbm, lengths_ref),
            (log_hbm, log_ref),
            (x_hbm, x_ref),
            (b_hbm, b_ref),
            (dy_hbm, dy_ref),
            (c_hbm, c_ref),
        ],
        sems,
    )
    slices = out_ref.shape[0]
    rows = WIDE // slices
    loads[0].wait()
    loads[1].wait()
    _, _, _, _, enter, leave, total = token_vectors(log_ref, lengths_ref)
    enter_cols = split_columns(enter)
    leave_cols = split_columns(leave)
    width = 2 * LANES
    for side, (wide_ref, narrow_ref, cols) in enumerate(
        ((x_ref, b_ref, leave_cols), (dy_ref, c_ref, enter_cols))
    ):
        loads[2 + 2 * side].wait()
        loads[3 + 2 * side].wait()
        narrow = narrow_ref[...]
        for chunk in range(WIDE // width):
            low = chunk * width
            at = slice(low // rows, (low + width) // rows)
            weighted = wide_ref[:, low : low + width].astype(FULL) * spread(cols, low, width)
            product = mul(weighted.astype(LOW), narrow, TN).astype(LOW)
            out_ref[at, side * rows : (side + 1) * rows, :] = product.reshape(
                width // rows, rows, STATE
            )
    total = jnp.broadcast_to(total, (HEADS, STATE))
    high = total.astype(LOW).astype(FULL)
    per_head = slices // HEADS
    for head in range(HEADS):
        rest = jnp.broadcast_to((total - high)[head : head + 1], (8, STATE))
        tile = jnp.where(iota((8, STATE), 0) == 0, high[head : head + 1], rest).astype(LOW)
        for part in range(per_head):
            out_ref[head * per_head + part, 2 * rows : 2 * rows + 8, :] = tile


def fetches_sibling():
    return lax.rem(lax.axis_index("seq"), 2) == 0


def pass_through(pieces, w_b_hbm, w_c_hbm, load_sems, sent_sems):
    pairs = []
    for rows, held_ref, _ in pieces:
        pairs.append((w_b_hbm.at[rows, :], held_ref.at[:, pl.ds(0, STATE)]))
        pairs.append((w_c_hbm.at[rows, :], held_ref.at[:, pl.ds(STATE, STATE)]))
    loads = fetch(pairs, load_sems)
    sends = []
    for at, (_, held_ref, sent_ref) in enumerate(pieces):
        loads[2 * at].wait()
        loads[2 * at + 1].wait()
        sends.append(pltpu.make_async_copy(held_ref, sent_ref, sent_sems.at[at]))
        sends[-1].start()
    for send in sends:
        send.wait()


def stage_kernel(_, w_b_hbm, w_c_hbm, *refs):
    sent_refs, held_refs, sems = refs[: len(ROUTE)], refs[len(ROUTE) : -2], refs[-2:]
    part = sent_refs[0].shape[0]
    columns = 2 * part
    me = lax.axis_index("tp")
    core, chips = lax.rem(me, CORES), lax.axis_size("tp") // CORES
    half = lax.rem(core + 1 + lax.rem(lax.axis_index("seq"), 2), CORES)
    pieces = []
    for at, ((step, _), held_ref, sent_ref) in enumerate(zip(ROUTE, held_refs, sent_refs)):
        first = lax.rem(me // CORES + step, chips) * CORES
        if at < 2:
            row = pl.multiple_of((first + half) * columns + at * part, part)
            pieces.append((pl.ds(row, part), held_ref, sent_ref))
        else:
            for which, other in enumerate((1 - core, core)):
                row = pl.multiple_of((first + other) * columns, columns)
                to = pl.ds(which * columns, columns)
                pieces.append((pl.ds(row, columns), held_ref.at[to, :], sent_ref.at[to, :]))
    pass_through(pieces, w_b_hbm, w_c_hbm, *sems)


def own_kernel(w_b_hbm, w_c_hbm, out_ref, held_ref, *sems):
    columns = out_ref.shape[0] // CORES
    me = lax.axis_index("tp")
    core = lax.rem(me, CORES)
    pieces = []
    for which, other in enumerate((1 - core, core)):
        row = pl.multiple_of((me - core + other) * columns, columns)
        to = pl.ds(which * columns, columns)
        pieces.append((pl.ds(row, columns), held_ref.at[to, :], out_ref.at[to, :]))
    pass_through(pieces, w_b_hbm, w_c_hbm, *sems)


def scan_kernel(in_ref, _, out_ref):
    devices, rows = out_ref.shape[0], out_ref.shape[1] // 2
    decays = []
    for at in range(devices):
        pair = in_ref[at, 2 * rows : 2 * rows + 8, :].astype(FULL)
        decays.append(pair[0:1] + pair[1:2])
    state = jnp.zeros((rows, STATE), FULL)
    for at in range(devices):
        out_ref[at, 0:rows, :] = state.astype(LOW)
        state = decays[at] * state + in_ref[at, 0:rows, :].astype(FULL)
    state = jnp.zeros((rows, STATE), FULL)
    for at in reversed(range(devices)):
        out_ref[at, rows : 2 * rows, :] = state.astype(LOW)
        state = decays[at] * state + in_ref[at, rows : 2 * rows, :].astype(FULL)


def local_kernel(
    lengths_hbm,
    log_hbm,
    x_hbm,
    b_hbm,
    dy_hbm,
    c_hbm,
    grad_x_ref,
    terms_ref,
    leave_ref,
    lengths_ref,
    log_ref,
    x_ref,
    b_ref,
    dy_ref,
    c_ref,
    sems,
):
    loads = fetch(
        [
            (lengths_hbm, lengths_ref),
            (log_hbm, log_ref),
            (x_hbm, x_ref),
            (b_hbm, b_ref),
            (dy_hbm, dy_ref),
            (c_hbm, c_ref),
        ],
        sems,
    )
    for load in loads:
        load.wait()
    first_row, ends, cumulative, docs, enter, leave, _ = token_vectors(log_ref, lengths_ref)
    enter_cols, leave_cols = split_columns(enter), split_columns(leave)
    leave_ref[...] = leave_cols
    cum_cols = cumulative.T
    middle = doc_of(first_row + SPAN - 1, ends)
    cum_middle = cumulative[:, SPAN - 1 : SPAN]
    leave_first = jnp.where(
        docs[:, :SPAN] == middle, jnp.exp(cum_middle - cumulative[:, :SPAN]), 0.0
    )
    enter_second = jnp.where(
        docs[:, SPAN:] == middle, jnp.exp(cumulative[:, SPAN:] - cum_middle), 0.0
    )
    leave_first, enter_second = split_columns(leave_first), split_columns(enter_second)
    b, c = b_ref[...], c_ref[...]
    scores = mul(b, c, NT)
    cross_scores = scores[:SPAN, SPAN:].astype(LOW)
    is_left = iota((SPAN, LANES), 1) < HEAD_DIM
    masks = []
    for number in range(2):
        base = first_row + number * SPAN
        same = doc_of(base + iota((SPAN, SPAN), 0), ends) == doc_of(
            base + iota((SPAN, SPAN), 1), ends
        )
        masks.append(same & (iota((SPAN, SPAN), 0) <= iota((SPAN, SPAN), 1)))

    def halves(value):
        zero = jnp.zeros_like(value)
        return jnp.concatenate(
            [jnp.where(is_left, value, zero), jnp.where(is_left, zero, value)], axis=0
        )

    mixed = [jnp.zeros((SPAN, SPAN), FULL), jnp.zeros((SPAN, SPAN), FULL)]
    mixed_cross = jnp.zeros((SPAN, SPAN), FULL)
    for pair in range(PAIRS):
        low = pair * LANES
        x, dy = x_ref[:, low : low + LANES], dy_ref[:, low : low + LANES]
        for side, (wide, cols) in enumerate(((x, leave_cols), (dy, enter_cols))):
            weighted = (wide.astype(FULL) * spread(cols, low, LANES)).astype(LOW)
            terms_ref[:, side * WIDE + low : side * WIDE + low + LANES] = weighted
        first_wide = spread(leave_first, low, LANES)
        x_first = (x[:SPAN].astype(FULL) * first_wide).astype(LOW)
        dy_second = (dy[SPAN:].astype(FULL) * spread(enter_second, low, LANES)).astype(LOW)
        mixed_cross += mul(x_first, dy_second, NT)
        pieces = [first_wide * mul(cross_scores, dy_second), 0.0]
        for number in range(2):
            span = slice(number * SPAN, (number + 1) * SPAN)
            inner = mul(halves(x[span]), dy[span], NT)
            low_scores = []
            for side in range(2):
                head = 2 * pair + side
                gaps = cumulative[head : head + 1, span] - cum_cols[span, head : head + 1]
                within = jnp.exp(jnp.where(masks[number], gaps, -1e30))
                mixed[number] += within * inner[side * SPAN : (side + 1) * SPAN]
                low_scores.append((within * scores[span, span]).astype(LOW))
            grad_x_ref[span, low : low + LANES] = pieces[number] + mul(
                jnp.concatenate(low_scores, axis=1), halves(dy[span])
            )
    nothing = jnp.zeros((SPAN, SPAN), FULL)
    table = jnp.concatenate(
        [
            jnp.concatenate([mixed[0], mixed_cross], axis=1),
            jnp.concatenate([nothing, mixed[1]], axis=1),
        ],
        axis=0,
    )
    for side, part in enumerate((mul(table.astype(LOW), c), mul(table.T.astype(LOW), b))):
        high = part.astype(LOW)
        low = 2 * (WIDE + side * STATE)
        terms_ref[:, low : low + STATE] = high
        terms_ref[:, low + STATE : low + 2 * STATE] = (part - high.astype(FULL)).astype(LOW)


def grad_bc_kernel(terms_ref, edge_ref, *refs):
    out_ref = refs[-1]
    rows = edge_ref.shape[1] // 2
    for side in range(2):
        which = slice(rows, 2 * rows) if side == 0 else slice(0, rows)
        edge = edge_ref[:, which, :].reshape(WIDE, STATE)
        total = mul(terms_ref[:, side * WIDE : (side + 1) * WIDE], edge)
        low = 2 * (WIDE + side * STATE)
        for part in range(2):
            total += terms_ref[:, low + part * STATE : low + (part + 1) * STATE].astype(FULL)
        out_ref[:, side * STATE : (side + 1) * STATE] = total.astype(LOW)


def grad_x_kernel(b_ref, leave_ref, local_ref, edge_ref, out_ref, done_ref):
    done_ref[...] = jnp.zeros_like(done_ref)
    rows = edge_ref.shape[1] // 2
    width = 2 * LANES
    for chunk in range(WIDE // width):
        low = chunk * width
        at = slice(low // rows, (low + width) // rows)
        end = edge_ref[at, rows : 2 * rows, :].reshape(width, STATE)
        later = spread(leave_ref[...], low, width) * mul(b_ref[...], end, NT)
        out_ref[:, low : low + width] = (local_ref[:, low : low + width] + later).astype(LOW)


def project_kernel(*refs, sibling):
    grads, (own, up, down), fetched, given = refs[:4], refs[4:7], refs[7:9], refs[9:11]
    _, out_ref, held_ref, total_ref, sems = refs[11:]
    columns = out_ref.shape[1]
    part = columns // 2
    here = fetches_sibling() if sibling else jnp.logical_not(fetches_sibling())

    def copies(pieces):
        return [
            pltpu.make_async_copy(piece, held_ref.at[pl.ds(at * part, part), :], sems.at[at])
            for at, piece in enumerate(pieces)
        ]

    def start(pieces):
        for copy in copies(pieces):
            copy.start()

    pl.when(here)(lambda: start(fetched))
    pl.when(jnp.logical_not(here))(lambda: start(given))
    width = 2 * LANES
    first = 0 if sibling else columns
    for low in range(0, columns, width):
        half = slice(first + low, first + low + width)
        total = mul(grads[0][...], own[half, :], NT)
        total += mul(grads[1][...], up[half, :], NT)
        total_ref[:, low : low + width] = total + mul(grads[3][...], down[half, :], NT)
    for copy in copies(fetched):
        copy.wait()
    for low in range(0, columns, width):
        to = slice(low, low + width)
        total = total_ref[:, to] + mul(grads[2][...], held_ref[to, :], NT)
        out_ref[:, to] = total.astype(out_ref.dtype)


def sum_kernel(kept_ref, received_ref, out_ref):
    out_ref[...] = (kept_ref[...] + received_ref[...].astype(FULL)).astype(LOW)


BLOCK = pl.BlockSpec(memory_space=pltpu.VMEM)
HBM = pl.BlockSpec(memory_space=pltpu.HBM)


def call(body, out_shape, specs, vmem, out_specs=BLOCK, scratch=()):
    return pl.pallas_call(
        body,
        out_shape=out_shape,
        in_specs=specs,
        out_specs=out_specs,
        scratch_shapes=scratch,
        compiler_params=pltpu.CompilerParams(vmem_limit_bytes=vmem),
        cost_estimate=pl.CostEstimate(flops=1000, bytes_accessed=1000, transcendentals=0),
    )


def along_x(value, step):
    devices = lax.axis_size("tp")
    return lax.ppermute(
        value, "tp", [(at, (at + CORES * step) % devices) for at in range(devices)]
    )


def along_y(value, step):
    pairs = []
    for at in range(lax.axis_size("seq")):
        y = at % ALONG_Y
        pairs.append((at, at - y + (y + step) % ALONG_Y))
    return lax.ppermute(value, "seq", pairs)


def per_device(inner_x, in_b, in_c, log_decay, doc_lengths, out_grad, w_b, w_c):
    tokens = inner_x.shape[0]
    devices = lax.axis_size("seq")
    rows = WIDE // devices
    columns = w_b.shape[0] // lax.axis_size("tp")
    local = (doc_lengths, log_decay, inner_x, in_b, out_grad, in_c)
    dma = pltpu.SemaphoreType.DMA
    shape = jax.ShapeDtypeStruct
    held = [pltpu.SMEM(doc_lengths.shape, doc_lengths.dtype)] + [
        pltpu.VMEM(a.shape, a.dtype) for a in local[1:]
    ]
    summary = call(
        summary_kernel,
        shape((devices, 2 * rows + 8, STATE), LOW),
        [HBM] * 6,
        LARGE_VMEM,
        BLOCK,
        held + [dma((6,))],
    )(*local)
    pieces = [(parts * columns // 2, 2 * STATE) for _, parts in ROUTE]
    own = (CORES * columns, 2 * STATE)
    sent = call(
        stage_kernel,
        [shape(piece, LOW) for piece in pieces],
        [HBM] * 3,
        LARGE_VMEM,
        [HBM] * len(pieces),
        [pltpu.VMEM(piece, LOW) for piece in pieces]
        + [dma((12,)), dma((6,))],
    )(summary, w_b, w_c)
    own = call(
        own_kernel,
        shape(own, LOW),
        [HBM] * 2,
        LARGE_VMEM,
        HBM,
        [pltpu.VMEM(own, LOW), dma((4,)), dma((2,))],
    )(w_b, w_c)
    ways = (1, 3)
    up, down = [along_x(piece, way) for piece, way in zip(sent[2:], ways)]
    fetched = [along_x(piece, way) for piece, way in zip(sent[:2], ways)]
    fetched = [along_x(piece, way) for piece, way in zip(fetched, ways)]
    given = [along_y(piece, way) for piece, way in zip(fetched, ways)]
    summary = lax.all_to_all(summary, "seq", 0, 0)
    grad_x, terms, leave_cols = call(
        local_kernel,
        [
            shape((tokens, WIDE), FULL),
            shape((tokens, 2 * WIDE + 4 * STATE), LOW),
            shape((tokens, 2 * HEADS), LOW),
        ],
        [HBM] * 6,
        16 * MIB,
        [BLOCK] * 3,
        held + [dma((6,))],
    )(*local)
    edges = call(
        scan_kernel,
        shape((devices, 2 * rows, STATE), LOW),
        [BLOCK, HBM],
        54 * MIB,
    )(summary, terms)
    edges = lax.all_to_all(edges, "seq", 0, 0)
    grad_bc = call(
        grad_bc_kernel,
        shape((tokens, 2 * STATE), LOW),
        [BLOCK, BLOCK, HBM, HBM],
        8 * MIB,
    )(terms, edges, up, down)
    others = [along_x(grad_bc, step) for step in (1, 2, 3)]
    grad_x, done = call(
        grad_x_kernel,
        [shape((tokens, WIDE), LOW), shape((8, LANES), FULL)],
        [BLOCK] * 4,
        8 * MIB,
        [BLOCK] * 2,
    )(in_b, leave_cols, grad_x, edges)

    def project(sibling, kind):
        return call(
            functools.partial(project_kernel, sibling=sibling),
            shape((tokens, columns), kind),
            [BLOCK] * 7 + [HBM] * 4 + [BLOCK],
            16 * MIB,
            BLOCK,
            [
                pltpu.VMEM((columns, 2 * STATE), LOW),
                pltpu.VMEM((tokens, columns), FULL),
                dma((2,)),
            ],
        )(grad_bc, *others, own, up, down, *fetched, *given, done)

    partner = [(at, at ^ 1) for at in range(lax.axis_size("tp"))]
    received = lax.ppermute(project(True, LOW), "tp", partner)
    grad_input = call(sum_kernel, shape((tokens, columns), LOW), [BLOCK] * 2, 8 * MIB)(
        project(False, FULL), received
    )
    return grad_x, grad_input


def solution(mesh):
    placed = (
        P("seq", "tp"),
        P("seq", "tp"),
        P("seq", "tp"),
        P("tp", "seq"),
        P(),
        P("seq", "tp"),
        P(None, "tp"),
        P(None, "tp"),
    )
    return jax.shard_map(
        per_device,
        mesh=mesh,
        in_specs=placed,
        out_specs=(P("seq", "tp"), P("seq", "tp")),
        check_vma=False,
    )
```

```python
import functools

import jax
import jax.numpy as jnp
from jax import lax
from jax.experimental import pallas as pl
from jax.experimental.pallas import tpu as pltpu
from jax.sharding import PartitionSpec as P

HEAD_DIM = 64
STATE = 128
SPAN = 128
HEADS = 16
LANES = 128
WIDE = HEADS * HEAD_DIM
PAIRS = WIDE // LANES
CORES = 2
ALONG_Y = 4
LOW = jnp.bfloat16
FULL = jnp.float32
NN = (((1,), (0,)), ((), ()))
NT = (((1,), (1,)), ((), ()))
TN = (((0,), (0,)), ((), ()))
MIB = 1024 * 1024
LARGE_VMEM = 56 * MIB


def mul(a, b, dims=NN):
    return lax.dot_general(a, b, dims, preferred_element_type=FULL)


def iota(shape, axis):
    return lax.broadcasted_iota(jnp.int32, shape, axis)


def doc_of(positions, ends):
    return sum((positions >= end).astype(jnp.int32) for end in ends)


def doc_ends(lengths_ref):
    first = lengths_ref[0]
    second = first + lengths_ref[1]
    return (first, second, second + lengths_ref[2])


def token_vectors(log_ref, lengths_ref):
    tokens = log_ref.shape[1]
    first_row = lax.axis_index("seq") * tokens
    ends = doc_ends(lengths_ref)
    upper = (iota((tokens, tokens), 0) <= iota((tokens, tokens), 1)).astype(FULL)
    cumulative = lax.dot_general(
        log_ref[...], upper, NN, precision=lax.Precision.HIGHEST, preferred_element_type=FULL
    )
    docs = doc_of(first_row + iota((HEADS, tokens), 1), ends)
    prior = jnp.where(first_row > 0, doc_of(first_row - 1, ends), -1)
    last = doc_of(first_row + tokens - 1, ends)
    cum_last = cumulative[:, tokens - 1 :]
    enter = jnp.where(docs == prior, jnp.exp(cumulative), 0.0)
    leave = jnp.where(docs == last, jnp.exp(cum_last - cumulative), 0.0)
    total = jnp.where(last == prior, jnp.exp(cum_last), 0.0)
    return first_row, ends, cumulative, docs, enter, leave, total


def split_columns(rows):
    high = rows.astype(LOW).astype(FULL)
    both = jnp.concatenate([high, rows - high], axis=0)
    return both.T.astype(LOW)


def spread(columns, low, width):
    head = (low + iota((2 * HEADS, width), 1)) // HEAD_DIM
    pick = (head == iota((2 * HEADS, width), 0) % HEADS).astype(FULL).astype(LOW)
    return mul(columns, pick)


def fetch(pairs, sems):
    copies = [
        pltpu.make_async_copy(source, target, sems.at[at])
        for at, (source, target) in enumerate(pairs)
    ]
    for copy in copies:
        copy.start()
    return copies


def summary_kernel(
    lengths_hbm,
    log_hbm,
    x_hbm,
    b_hbm,
    dy_hbm,
    c_hbm,
    out_ref,
    lengths_ref,
    log_ref,
    x_ref,
    b_ref,
    dy_ref,
    c_ref,
    sems,
):
    loads = fetch(
        [
            (lengths_hbm, lengths_ref),
            (log_hbm, log_ref),
            (x_hbm, x_ref),
            (b_hbm, b_ref),
            (dy_hbm, dy_ref),
            (c_hbm, c_ref),
        ],
        sems,
    )
    slices = out_ref.shape[0]
    rows = WIDE // slices
    loads[0].wait()
    loads[1].wait()
    _, _, _, _, enter, leave, total = token_vectors(log_ref, lengths_ref)
    enter_cols = split_columns(enter)
    leave_cols = split_columns(leave)
    width = 2 * LANES
    for side, (wide_ref, narrow_ref, cols) in enumerate(
        ((x_ref, b_ref, leave_cols), (dy_ref, c_ref, enter_cols))
    ):
        loads[2 + 2 * side].wait()
        loads[3 + 2 * side].wait()
        narrow = narrow_ref[...]
        for chunk in range(WIDE // width):
            low = chunk * width
            at = slice(low // rows, (low + width) // rows)
            weighted = wide_ref[:, low : low + width].astype(FULL) * spread(cols, low, width)
            product = mul(weighted.astype(LOW), narrow, TN).astype(LOW)
            out_ref[at, side * rows : (side + 1) * rows, :] = product.reshape(
                width // rows, rows, STATE
            )
    total = jnp.broadcast_to(total, (HEADS, STATE))
    high = total.astype(LOW).astype(FULL)
    per_head = slices // HEADS
    for head in range(HEADS):
        rest = jnp.broadcast_to((total - high)[head : head + 1], (8, STATE))
        tile = jnp.where(iota((8, STATE), 0) == 0, high[head : head + 1], rest).astype(LOW)
        for part in range(per_head):
            out_ref[head * per_head + part, 2 * rows : 2 * rows + 8, :] = tile


def fetches_sibling():
    return lax.rem(lax.axis_index("seq"), 2) == 0


def pass_through(pieces, w_b_hbm, w_c_hbm, load_sems, sent_sems):
    pairs = []
    for rows, held_ref, _ in pieces:
        pairs.append((w_b_hbm.at[rows, :], held_ref.at[:, pl.ds(0, STATE)]))
        pairs.append((w_c_hbm.at[rows, :], held_ref.at[:, pl.ds(STATE, STATE)]))
    loads = fetch(pairs, load_sems)
    sends = []
    for at, (_, held_ref, sent_ref) in enumerate(pieces):
        loads[2 * at].wait()
        loads[2 * at + 1].wait()
        sends.append(pltpu.make_async_copy(held_ref, sent_ref, sent_sems.at[at]))
        sends[-1].start()
    for send in sends:
        send.wait()


def stage_far_kernel(_, w_b_hbm, w_c_hbm, *refs):
    sent_refs, held_refs, sems = refs[:2], refs[2:4], refs[4:]
    part = sent_refs[0].shape[0]
    me = lax.axis_index("tp")
    core, chips = lax.rem(me, CORES), lax.axis_size("tp") // CORES
    half = lax.rem(core + 1 + lax.rem(lax.axis_index("seq"), 2), CORES)
    first = (lax.rem(me // CORES + 2, chips) * CORES + half) * 2 * part
    pieces = []
    for at in range(2):
        row = pl.multiple_of(first + at * part, part)
        pieces.append((pl.ds(row, part), held_refs[at], sent_refs[at]))
    pass_through(pieces, w_b_hbm, w_c_hbm, *sems)


def stage_near_kernel(_, w_b_hbm, w_c_hbm, *refs):
    sent_refs, held_refs, sems = refs[:2], refs[2:4], refs[4:]
    columns = sent_refs[0].shape[0] // CORES
    me = lax.axis_index("tp")
    core, chips = lax.rem(me, CORES), lax.axis_size("tp") // CORES
    pieces = []
    for step, held_ref, sent_ref in zip((1, 3), held_refs, sent_refs):
        first = lax.rem(me // CORES + step, chips) * CORES
        for which, other in enumerate((1 - core, core)):
            row = pl.multiple_of((first + other) * columns, columns)
            to = pl.ds(which * columns, columns)
            pieces.append((pl.ds(row, columns), held_ref.at[to, :], sent_ref.at[to, :]))
    pass_through(pieces, w_b_hbm, w_c_hbm, *sems)


def own_kernel(w_b_hbm, w_c_hbm, out_ref, held_ref, *sems):
    columns = out_ref.shape[0] // CORES
    me = lax.axis_index("tp")
    core = lax.rem(me, CORES)
    pieces = []
    for which, other in enumerate((1 - core, core)):
        row = pl.multiple_of((me - core + other) * columns, columns)
        to = pl.ds(which * columns, columns)
        pieces.append((pl.ds(row, columns), held_ref.at[to, :], out_ref.at[to, :]))
    pass_through(pieces, w_b_hbm, w_c_hbm, *sems)


def scan_kernel(in_ref, *refs):
    out_ref = refs[-1]
    devices, rows = out_ref.shape[0], out_ref.shape[1] // 2
    decays = []
    for at in range(devices):
        pair = in_ref[at, 2 * rows : 2 * rows + 8, :].astype(FULL)
        decays.append(pair[0:1] + pair[1:2])
    state = jnp.zeros((rows, STATE), FULL)
    for at in range(devices):
        out_ref[at, 0:rows, :] = state.astype(LOW)
        state = decays[at] * state + in_ref[at, 0:rows, :].astype(FULL)
    state = jnp.zeros((rows, STATE), FULL)
    for at in reversed(range(devices)):
        out_ref[at, rows : 2 * rows, :] = state.astype(LOW)
        state = decays[at] * state + in_ref[at, rows : 2 * rows, :].astype(FULL)


def local_kernel(
    lengths_hbm,
    log_hbm,
    x_hbm,
    b_hbm,
    dy_hbm,
    c_hbm,
    grad_x_ref,
    terms_ref,
    leave_ref,
    lengths_ref,
    log_ref,
    x_ref,
    b_ref,
    dy_ref,
    c_ref,
    sems,
):
    loads = fetch(
        [
            (lengths_hbm, lengths_ref),
            (log_hbm, log_ref),
            (x_hbm, x_ref),
            (b_hbm, b_ref),
            (dy_hbm, dy_ref),
            (c_hbm, c_ref),
        ],
        sems,
    )
    for load in loads:
        load.wait()
    first_row, ends, cumulative, docs, enter, leave, _ = token_vectors(log_ref, lengths_ref)
    enter_cols, leave_cols = split_columns(enter), split_columns(leave)
    leave_ref[...] = leave_cols
    cum_cols = cumulative.T
    middle = doc_of(first_row + SPAN - 1, ends)
    cum_middle = cumulative[:, SPAN - 1 : SPAN]
    leave_first = jnp.where(
        docs[:, :SPAN] == middle, jnp.exp(cum_middle - cumulative[:, :SPAN]), 0.0
    )
    enter_second = jnp.where(
        docs[:, SPAN:] == middle, jnp.exp(cumulative[:, SPAN:] - cum_middle), 0.0
    )
    leave_first, enter_second = split_columns(leave_first), split_columns(enter_second)
    b, c = b_ref[...], c_ref[...]
    scores = mul(b, c, NT)
    cross_scores = scores[:SPAN, SPAN:].astype(LOW)
    is_left = iota((SPAN, LANES), 1) < HEAD_DIM
    masks = []
    for number in range(2):
        base = first_row + number * SPAN
        same = doc_of(base + iota((SPAN, SPAN), 0), ends) == doc_of(
            base + iota((SPAN, SPAN), 1), ends
        )
        masks.append(same & (iota((SPAN, SPAN), 0) <= iota((SPAN, SPAN), 1)))

    def halves(value):
        zero = jnp.zeros_like(value)
        return jnp.concatenate(
            [jnp.where(is_left, value, zero), jnp.where(is_left, zero, value)], axis=0
        )

    mixed = [jnp.zeros((SPAN, SPAN), FULL), jnp.zeros((SPAN, SPAN), FULL)]
    mixed_cross = jnp.zeros((SPAN, SPAN), FULL)
    for pair in range(PAIRS):
        low = pair * LANES
        x, dy = x_ref[:, low : low + LANES], dy_ref[:, low : low + LANES]
        for side, (wide, cols) in enumerate(((x, leave_cols), (dy, enter_cols))):
            weighted = (wide.astype(FULL) * spread(cols, low, LANES)).astype(LOW)
            terms_ref[:, side * WIDE + low : side * WIDE + low + LANES] = weighted
        first_wide = spread(leave_first, low, LANES)
        x_first = (x[:SPAN].astype(FULL) * first_wide).astype(LOW)
        dy_second = (dy[SPAN:].astype(FULL) * spread(enter_second, low, LANES)).astype(LOW)
        mixed_cross += mul(x_first, dy_second, NT)
        pieces = [first_wide * mul(cross_scores, dy_second), 0.0]
        for number in range(2):
            span = slice(number * SPAN, (number + 1) * SPAN)
            inner = mul(halves(x[span]), dy[span], NT)
            low_scores = []
            for side in range(2):
                head = 2 * pair + side
                gaps = cumulative[head : head + 1, span] - cum_cols[span, head : head + 1]
                within = jnp.exp(jnp.where(masks[number], gaps, -1e30))
                mixed[number] += within * inner[side * SPAN : (side + 1) * SPAN]
                low_scores.append((within * scores[span, span]).astype(LOW))
            grad_x_ref[span, low : low + LANES] = pieces[number] + mul(
                jnp.concatenate(low_scores, axis=1), halves(dy[span])
            )
    nothing = jnp.zeros((SPAN, SPAN), FULL)
    table = jnp.concatenate(
        [
            jnp.concatenate([mixed[0], mixed_cross], axis=1),
            jnp.concatenate([nothing, mixed[1]], axis=1),
        ],
        axis=0,
    )
    for side, part in enumerate((mul(table.astype(LOW), c), mul(table.T.astype(LOW), b))):
        high = part.astype(LOW)
        low = 2 * (WIDE + side * STATE)
        terms_ref[:, low : low + STATE] = high
        terms_ref[:, low + STATE : low + 2 * STATE] = (part - high.astype(FULL)).astype(LOW)


def grad_bc_kernel(terms_ref, edge_ref, *refs):
    out_ref = refs[-1]
    rows = edge_ref.shape[1] // 2
    for side in range(2):
        which = slice(rows, 2 * rows) if side == 0 else slice(0, rows)
        edge = edge_ref[:, which, :].reshape(WIDE, STATE)
        total = mul(terms_ref[:, side * WIDE : (side + 1) * WIDE], edge)
        low = 2 * (WIDE + side * STATE)
        for part in range(2):
            total += terms_ref[:, low + part * STATE : low + (part + 1) * STATE].astype(FULL)
        out_ref[:, side * STATE : (side + 1) * STATE] = total.astype(LOW)


def grad_x_kernel(b_ref, leave_ref, local_ref, edge_ref, out_ref, done_ref):
    done_ref[...] = jnp.zeros_like(done_ref)
    rows = edge_ref.shape[1] // 2
    width = 2 * LANES
    for chunk in range(WIDE // width):
        low = chunk * width
        at = slice(low // rows, (low + width) // rows)
        end = edge_ref[at, rows : 2 * rows, :].reshape(width, STATE)
        later = spread(leave_ref[...], low, width) * mul(b_ref[...], end, NT)
        out_ref[:, low : low + width] = (local_ref[:, low : low + width] + later).astype(LOW)


def project_kernel(*refs, sibling):
    grads, (own, up, down), fetched, given = refs[:4], refs[4:7], refs[7:9], refs[9:11]
    _, out_ref, held_ref, total_ref, sems = refs[11:]
    columns = out_ref.shape[1]
    part = columns // 2
    here = fetches_sibling() if sibling else jnp.logical_not(fetches_sibling())

    def copies(pieces):
        return [
            pltpu.make_async_copy(piece, held_ref.at[pl.ds(at * part, part), :], sems.at[at])
            for at, piece in enumerate(pieces)
        ]

    def start(pieces):
        for copy in copies(pieces):
            copy.start()

    pl.when(here)(lambda: start(fetched))
    pl.when(jnp.logical_not(here))(lambda: start(given))
    width = 2 * LANES
    first = 0 if sibling else columns
    for low in range(0, columns, width):
        half = slice(first + low, first + low + width)
        total = mul(grads[0][...], own[half, :], NT)
        total += mul(grads[1][...], up[half, :], NT)
        total_ref[:, low : low + width] = total + mul(grads[3][...], down[half, :], NT)
    for copy in copies(fetched):
        copy.wait()
    for low in range(0, columns, width):
        to = slice(low, low + width)
        total = total_ref[:, to] + mul(grads[2][...], held_ref[to, :], NT)
        out_ref[:, to] = total.astype(out_ref.dtype)


def sum_kernel(kept_ref, received_ref, out_ref):
    out_ref[...] = (kept_ref[...] + received_ref[...].astype(FULL)).astype(LOW)


BLOCK = pl.BlockSpec(memory_space=pltpu.VMEM)
HBM = pl.BlockSpec(memory_space=pltpu.HBM)


def call(body, out_shape, specs, vmem, out_specs=BLOCK, scratch=()):
    return pl.pallas_call(
        body,
        out_shape=out_shape,
        in_specs=specs,
        out_specs=out_specs,
        scratch_shapes=scratch,
        compiler_params=pltpu.CompilerParams(vmem_limit_bytes=vmem),
        cost_estimate=pl.CostEstimate(flops=1000, bytes_accessed=1000, transcendentals=0),
    )


def along_x(value, step):
    devices = lax.axis_size("tp")
    return lax.ppermute(
        value, "tp", [(at, (at + CORES * step) % devices) for at in range(devices)]
    )


def along_y(value, step):
    pairs = []
    for at in range(lax.axis_size("seq")):
        y = at % ALONG_Y
        pairs.append((at, at - y + (y + step) % ALONG_Y))
    return lax.ppermute(value, "seq", pairs)


def per_device(inner_x, in_b, in_c, log_decay, doc_lengths, out_grad, w_b, w_c):
    tokens = inner_x.shape[0]
    devices = lax.axis_size("seq")
    rows = WIDE // devices
    columns = w_b.shape[0] // lax.axis_size("tp")
    local = (doc_lengths, log_decay, inner_x, in_b, out_grad, in_c)
    dma = pltpu.SemaphoreType.DMA
    shape = jax.ShapeDtypeStruct
    held = [pltpu.SMEM(doc_lengths.shape, doc_lengths.dtype)] + [
        pltpu.VMEM(a.shape, a.dtype) for a in local[1:]
    ]
    summary = call(
        summary_kernel,
        shape((devices, 2 * rows + 8, STATE), LOW),
        [HBM] * 6,
        LARGE_VMEM,
        BLOCK,
        held + [dma((6,))],
    )(*local)
    both = (CORES * columns, 2 * STATE)

    def stage(kernel, piece, count, after):
        return call(
            kernel,
            [shape(piece, LOW)] * 2,
            [HBM] * 3,
            LARGE_VMEM,
            [HBM] * 2,
            [pltpu.VMEM(piece, LOW)] * 2 + [dma((2 * count,)), dma((count,))],
        )(after, w_b, w_c)

    ways = (1, 3)
    far = stage(stage_far_kernel, (columns // 2, 2 * STATE), 2, summary)
    fetched = [along_x(piece, 2) for piece in far]
    given = [along_y(piece, way) for piece, way in zip(fetched, ways)]
    own = call(
        own_kernel,
        shape(both, LOW),
        [HBM] * 2,
        LARGE_VMEM,
        HBM,
        [pltpu.VMEM(both, LOW), dma((4,)), dma((2,))],
    )(w_b, w_c)
    summary = lax.all_to_all(summary, "seq", 0, 0)
    grad_x, terms, leave_cols = call(
        local_kernel,
        [
            shape((tokens, WIDE), FULL),
            shape((tokens, 2 * WIDE + 4 * STATE), LOW),
            shape((tokens, 2 * HEADS), LOW),
        ],
        [HBM] * 6,
        16 * MIB,
        [BLOCK] * 3,
        held + [dma((6,))],
    )(*local)
    near = stage(stage_near_kernel, both, 4, leave_cols)
    up, down = [along_x(piece, way) for piece, way in zip(near, ways)]
    edges = call(
        scan_kernel,
        shape((devices, 2 * rows, STATE), LOW),
        [BLOCK] + [HBM] * 3,
        4 * MIB,
    )(summary, leave_cols, *fetched)
    edges = lax.all_to_all(edges, "seq", 0, 0)
    grad_bc = call(
        grad_bc_kernel,
        shape((tokens, 2 * STATE), LOW),
        [BLOCK, BLOCK, HBM, HBM],
        8 * MIB,
    )(terms, edges, up, down)
    others = [along_x(grad_bc, step) for step in (1, 2, 3)]
    grad_x, done = call(
        grad_x_kernel,
        [shape((tokens, WIDE), LOW), shape((8, LANES), FULL)],
        [BLOCK] * 4,
        8 * MIB,
        [BLOCK] * 2,
    )(in_b, leave_cols, grad_x, edges)

    def project(sibling, kind):
        return call(
            functools.partial(project_kernel, sibling=sibling),
            shape((tokens, columns), kind),
            [BLOCK] * 7 + [HBM] * 4 + [BLOCK],
            16 * MIB,
            BLOCK,
            [
                pltpu.VMEM((columns, 2 * STATE), LOW),
                pltpu.VMEM((tokens, columns), FULL),
                dma((2,)),
            ],
        )(grad_bc, *others, own, up, down, *fetched, *given, done)

    partner = [(at, at ^ 1) for at in range(lax.axis_size("tp"))]
    received = lax.ppermute(project(True, LOW), "tp", partner)
    grad_input = call(sum_kernel, shape((tokens, columns), LOW), [BLOCK] * 2, 8 * MIB)(
        project(False, FULL), received
    )
    return grad_x, grad_input


def solution(mesh):
    placed = (
        P("seq", "tp"),
        P("seq", "tp"),
        P("seq", "tp"),
        P("tp", "seq"),
        P(),
        P("seq", "tp"),
        P(None, "tp"),
        P(None, "tp"),
    )
    return jax.shard_map(
        per_device,
        mesh=mesh,
        in_specs=placed,
        out_specs=(P("seq", "tp"), P("seq", "tp")),
        check_vma=False,
    )
```

```python
import functools

import jax
import jax.numpy as jnp
from jax import lax
from jax.experimental import pallas as pl
from jax.experimental.pallas import tpu as pltpu
from jax.sharding import PartitionSpec as P

HEAD_DIM = 64
STATE = 128
SPAN = 128
HEADS = 16
LANES = 128
WIDE = HEADS * HEAD_DIM
PAIRS = WIDE // LANES
CORES = 2
ALONG_Y = 4
LOW = jnp.bfloat16
FULL = jnp.float32
NN = (((1,), (0,)), ((), ()))
NT = (((1,), (1,)), ((), ()))
TN = (((0,), (0,)), ((), ()))
MIB = 1024 * 1024
LARGE_VMEM = 56 * MIB


def mul(a, b, dims=NN):
    return lax.dot_general(a, b, dims, preferred_element_type=FULL)


def iota(shape, axis):
    return lax.broadcasted_iota(jnp.int32, shape, axis)


def doc_of(positions, ends):
    return sum((positions >= end).astype(jnp.int32) for end in ends)


def doc_ends(lengths_ref):
    first = lengths_ref[0]
    second = first + lengths_ref[1]
    return (first, second, second + lengths_ref[2])


def token_vectors(log_ref, lengths_ref):
    tokens = log_ref.shape[1]
    first_row = lax.axis_index("seq") * tokens
    ends = doc_ends(lengths_ref)
    upper = (iota((tokens, tokens), 0) <= iota((tokens, tokens), 1)).astype(FULL)
    cumulative = lax.dot_general(
        log_ref[...], upper, NN, precision=lax.Precision.HIGHEST, preferred_element_type=FULL
    )
    docs = doc_of(first_row + iota((HEADS, tokens), 1), ends)
    prior = jnp.where(first_row > 0, doc_of(first_row - 1, ends), -1)
    last = doc_of(first_row + tokens - 1, ends)
    cum_last = cumulative[:, tokens - 1 :]
    enter = jnp.where(docs == prior, jnp.exp(cumulative), 0.0)
    leave = jnp.where(docs == last, jnp.exp(cum_last - cumulative), 0.0)
    total = jnp.where(last == prior, jnp.exp(cum_last), 0.0)
    return first_row, ends, cumulative, docs, enter, leave, total


def split_columns(rows):
    high = rows.astype(LOW).astype(FULL)
    both = jnp.concatenate([high, rows - high], axis=0)
    return both.T.astype(LOW)


def spread(columns, low, width):
    head = (low + iota((2 * HEADS, width), 1)) // HEAD_DIM
    pick = (head == iota((2 * HEADS, width), 0) % HEADS).astype(FULL).astype(LOW)
    return mul(columns, pick)


def fetch(pairs, sems):
    copies = [
        pltpu.make_async_copy(source, target, sems.at[at])
        for at, (source, target) in enumerate(pairs)
    ]
    for copy in copies:
        copy.start()
    return copies


def summary_kernel(
    lengths_hbm,
    log_hbm,
    x_hbm,
    b_hbm,
    dy_hbm,
    c_hbm,
    out_ref,
    lengths_ref,
    log_ref,
    x_ref,
    b_ref,
    dy_ref,
    c_ref,
    sems,
):
    loads = fetch(
        [
            (lengths_hbm, lengths_ref),
            (log_hbm, log_ref),
            (x_hbm, x_ref),
            (b_hbm, b_ref),
            (dy_hbm, dy_ref),
            (c_hbm, c_ref),
        ],
        sems,
    )
    slices = out_ref.shape[0]
    rows = WIDE // slices
    loads[0].wait()
    loads[1].wait()
    _, _, _, _, enter, leave, total = token_vectors(log_ref, lengths_ref)
    enter_cols = split_columns(enter)
    leave_cols = split_columns(leave)
    width = 2 * LANES
    for side, (wide_ref, narrow_ref, cols) in enumerate(
        ((x_ref, b_ref, leave_cols), (dy_ref, c_ref, enter_cols))
    ):
        loads[2 + 2 * side].wait()
        loads[3 + 2 * side].wait()
        narrow = narrow_ref[...]
        for chunk in range(WIDE // width):
            low = chunk * width
            at = slice(low // rows, (low + width) // rows)
            weighted = wide_ref[:, low : low + width].astype(FULL) * spread(cols, low, width)
            product = mul(weighted.astype(LOW), narrow, TN).astype(LOW)
            out_ref[at, side * rows : (side + 1) * rows, :] = product.reshape(
                width // rows, rows, STATE
            )
    total = jnp.broadcast_to(total, (HEADS, STATE))
    high = total.astype(LOW).astype(FULL)
    per_head = slices // HEADS
    for head in range(HEADS):
        rest = jnp.broadcast_to((total - high)[head : head + 1], (8, STATE))
        tile = jnp.where(iota((8, STATE), 0) == 0, high[head : head + 1], rest).astype(LOW)
        for part in range(per_head):
            out_ref[head * per_head + part, 2 * rows : 2 * rows + 8, :] = tile


def fetches_sibling():
    return lax.rem(lax.axis_index("seq"), 2) == 0


def pass_through(pieces, w_b_hbm, w_c_hbm, load_sems, sent_sems):
    pairs = []
    for rows, held_ref, _ in pieces:
        pairs.append((w_b_hbm.at[rows, :], held_ref.at[:, pl.ds(0, STATE)]))
        pairs.append((w_c_hbm.at[rows, :], held_ref.at[:, pl.ds(STATE, STATE)]))
    loads = fetch(pairs, load_sems)
    sends = []
    for at, (_, held_ref, sent_ref) in enumerate(pieces):
        loads[2 * at].wait()
        loads[2 * at + 1].wait()
        sends.append(pltpu.make_async_copy(held_ref, sent_ref, sent_sems.at[at]))
        sends[-1].start()
    for send in sends:
        send.wait()


def stage_far_kernel(_, w_b_hbm, w_c_hbm, sent_ref, held_ref, *sems):
    columns = sent_ref.shape[0]
    me = lax.axis_index("tp")
    core, chips = lax.rem(me, CORES), lax.axis_size("tp") // CORES
    half = lax.rem(core + 1 + lax.rem(lax.axis_index("seq"), 2), CORES)
    row = (lax.rem(me // CORES + 2, chips) * CORES + half) * columns
    from_row = pl.ds(pl.multiple_of(row, columns), columns)
    pass_through([(from_row, held_ref, sent_ref)], w_b_hbm, w_c_hbm, *sems)


def stage_near_kernel(_, w_b_hbm, w_c_hbm, *refs):
    sent_refs, held_refs, sems = refs[:2], refs[2:4], refs[4:]
    columns = sent_refs[0].shape[0] // CORES
    me = lax.axis_index("tp")
    core, chips = lax.rem(me, CORES), lax.axis_size("tp") // CORES
    pieces = []
    for step, held_ref, sent_ref in zip((1, 3), held_refs, sent_refs):
        first = lax.rem(me // CORES + step, chips) * CORES
        for which, other in enumerate((1 - core, core)):
            row = pl.multiple_of((first + other) * columns, columns)
            to = pl.ds(which * columns, columns)
            pieces.append((pl.ds(row, columns), held_ref.at[to, :], sent_ref.at[to, :]))
    pass_through(pieces, w_b_hbm, w_c_hbm, *sems)


def own_kernel(w_b_hbm, w_c_hbm, out_ref, held_ref, *sems):
    columns = out_ref.shape[0] // CORES
    me = lax.axis_index("tp")
    core = lax.rem(me, CORES)
    pieces = []
    for which, other in enumerate((1 - core, core)):
        row = pl.multiple_of((me - core + other) * columns, columns)
        to = pl.ds(which * columns, columns)
        pieces.append((pl.ds(row, columns), held_ref.at[to, :], out_ref.at[to, :]))
    pass_through(pieces, w_b_hbm, w_c_hbm, *sems)


def scan_kernel(in_ref, *refs):
    out_ref = refs[-1]
    devices, rows = out_ref.shape[0], out_ref.shape[1] // 2
    decays = []
    for at in range(devices):
        pair = in_ref[at, 2 * rows : 2 * rows + 8, :].astype(FULL)
        decays.append(pair[0:1] + pair[1:2])
    state = jnp.zeros((rows, STATE), FULL)
    for at in range(devices):
        out_ref[at, 0:rows, :] = state.astype(LOW)
        state = decays[at] * state + in_ref[at, 0:rows, :].astype(FULL)
    state = jnp.zeros((rows, STATE), FULL)
    for at in reversed(range(devices)):
        out_ref[at, rows : 2 * rows, :] = state.astype(LOW)
        state = decays[at] * state + in_ref[at, rows : 2 * rows, :].astype(FULL)


def local_kernel(
    lengths_hbm,
    log_hbm,
    x_hbm,
    b_hbm,
    dy_hbm,
    c_hbm,
    grad_x_ref,
    terms_ref,
    leave_ref,
    lengths_ref,
    log_ref,
    x_ref,
    b_ref,
    dy_ref,
    c_ref,
    sems,
):
    loads = fetch(
        [
            (lengths_hbm, lengths_ref),
            (log_hbm, log_ref),
            (x_hbm, x_ref),
            (b_hbm, b_ref),
            (dy_hbm, dy_ref),
            (c_hbm, c_ref),
        ],
        sems,
    )
    for load in loads:
        load.wait()
    first_row, ends, cumulative, docs, enter, leave, _ = token_vectors(log_ref, lengths_ref)
    enter_cols, leave_cols = split_columns(enter), split_columns(leave)
    leave_ref[...] = leave_cols
    cum_cols = cumulative.T
    middle = doc_of(first_row + SPAN - 1, ends)
    cum_middle = cumulative[:, SPAN - 1 : SPAN]
    leave_first = jnp.where(
        docs[:, :SPAN] == middle, jnp.exp(cum_middle - cumulative[:, :SPAN]), 0.0
    )
    enter_second = jnp.where(
        docs[:, SPAN:] == middle, jnp.exp(cumulative[:, SPAN:] - cum_middle), 0.0
    )
    leave_first, enter_second = split_columns(leave_first), split_columns(enter_second)
    b, c = b_ref[...], c_ref[...]
    scores = mul(b, c, NT)
    cross_scores = scores[:SPAN, SPAN:].astype(LOW)
    is_left = iota((SPAN, LANES), 1) < HEAD_DIM
    masks = []
    for number in range(2):
        base = first_row + number * SPAN
        same = doc_of(base + iota((SPAN, SPAN), 0), ends) == doc_of(
            base + iota((SPAN, SPAN), 1), ends
        )
        masks.append(same & (iota((SPAN, SPAN), 0) <= iota((SPAN, SPAN), 1)))

    def halves(value):
        zero = jnp.zeros_like(value)
        return jnp.concatenate(
            [jnp.where(is_left, value, zero), jnp.where(is_left, zero, value)], axis=0
        )

    mixed = [jnp.zeros((SPAN, SPAN), FULL), jnp.zeros((SPAN, SPAN), FULL)]
    mixed_cross = jnp.zeros((SPAN, SPAN), FULL)
    for pair in range(PAIRS):
        low = pair * LANES
        x, dy = x_ref[:, low : low + LANES], dy_ref[:, low : low + LANES]
        for side, (wide, cols) in enumerate(((x, leave_cols), (dy, enter_cols))):
            weighted = (wide.astype(FULL) * spread(cols, low, LANES)).astype(LOW)
            terms_ref[:, side * WIDE + low : side * WIDE + low + LANES] = weighted
        first_wide = spread(leave_first, low, LANES)
        x_first = (x[:SPAN].astype(FULL) * first_wide).astype(LOW)
        dy_second = (dy[SPAN:].astype(FULL) * spread(enter_second, low, LANES)).astype(LOW)
        mixed_cross += mul(x_first, dy_second, NT)
        pieces = [first_wide * mul(cross_scores, dy_second), 0.0]
        for number in range(2):
            span = slice(number * SPAN, (number + 1) * SPAN)
            inner = mul(halves(x[span]), dy[span], NT)
            low_scores = []
            for side in range(2):
                head = 2 * pair + side
                gaps = cumulative[head : head + 1, span] - cum_cols[span, head : head + 1]
                within = jnp.exp(jnp.where(masks[number], gaps, -1e30))
                mixed[number] += within * inner[side * SPAN : (side + 1) * SPAN]
                low_scores.append((within * scores[span, span]).astype(LOW))
            grad_x_ref[span, low : low + LANES] = pieces[number] + mul(
                jnp.concatenate(low_scores, axis=1), halves(dy[span])
            )
    nothing = jnp.zeros((SPAN, SPAN), FULL)
    table = jnp.concatenate(
        [
            jnp.concatenate([mixed[0], mixed_cross], axis=1),
            jnp.concatenate([nothing, mixed[1]], axis=1),
        ],
        axis=0,
    )
    for side, part in enumerate((mul(table.astype(LOW), c), mul(table.T.astype(LOW), b))):
        high = part.astype(LOW)
        low = 2 * (WIDE + side * STATE)
        terms_ref[:, low : low + STATE] = high
        terms_ref[:, low + STATE : low + 2 * STATE] = (part - high.astype(FULL)).astype(LOW)


def grad_bc_kernel(terms_ref, edge_ref, *refs):
    out_ref = refs[-1]
    rows = edge_ref.shape[1] // 2
    for side in range(2):
        which = slice(rows, 2 * rows) if side == 0 else slice(0, rows)
        edge = edge_ref[:, which, :].reshape(WIDE, STATE)
        total = mul(terms_ref[:, side * WIDE : (side + 1) * WIDE], edge)
        low = 2 * (WIDE + side * STATE)
        for part in range(2):
            total += terms_ref[:, low + part * STATE : low + (part + 1) * STATE].astype(FULL)
        out_ref[:, side * STATE : (side + 1) * STATE] = total.astype(LOW)


def grad_x_kernel(b_ref, leave_ref, local_ref, edge_ref, out_ref, done_ref):
    done_ref[...] = jnp.zeros_like(done_ref)
    rows = edge_ref.shape[1] // 2
    width = 2 * LANES
    for chunk in range(WIDE // width):
        low = chunk * width
        at = slice(low // rows, (low + width) // rows)
        end = edge_ref[at, rows : 2 * rows, :].reshape(width, STATE)
        later = spread(leave_ref[...], low, width) * mul(b_ref[...], end, NT)
        out_ref[:, low : low + width] = (local_ref[:, low : low + width] + later).astype(LOW)


def project_kernel(*refs, sibling):
    grads, (own, up, down), fetched, given = refs[:4], refs[4:7], refs[7], refs[8:10]
    _, out_ref, held_ref, total_ref, sems = refs[10:]
    columns = out_ref.shape[1]
    part = columns // 2
    here = fetches_sibling() if sibling else jnp.logical_not(fetches_sibling())

    def copies(pieces):
        return [
            pltpu.make_async_copy(piece, held_ref.at[pl.ds(at * part, part), :], sems.at[at])
            for at, piece in enumerate(pieces)
        ]

    def start(pieces):
        for copy in copies(pieces):
            copy.start()

    fetched = [fetched.at[pl.ds(at * part, part), :] for at in range(2)]
    pl.when(here)(lambda: start(fetched))
    pl.when(jnp.logical_not(here))(lambda: start(given))
    width = 2 * LANES
    first = 0 if sibling else columns
    for low in range(0, columns, width):
        half = slice(first + low, first + low + width)
        total = mul(grads[0][...], own[half, :], NT)
        total += mul(grads[1][...], up[half, :], NT)
        total_ref[:, low : low + width] = total + mul(grads[3][...], down[half, :], NT)
    for copy in copies(fetched):
        copy.wait()
    for low in range(0, columns, width):
        to = slice(low, low + width)
        total = total_ref[:, to] + mul(grads[2][...], held_ref[to, :], NT)
        out_ref[:, to] = total.astype(out_ref.dtype)


def sum_kernel(kept_ref, received_ref, out_ref):
    out_ref[...] = (kept_ref[...] + received_ref[...].astype(FULL)).astype(LOW)


BLOCK = pl.BlockSpec(memory_space=pltpu.VMEM)
HBM = pl.BlockSpec(memory_space=pltpu.HBM)


def call(body, out_shape, specs, vmem, out_specs=BLOCK, scratch=()):
    return pl.pallas_call(
        body,
        out_shape=out_shape,
        in_specs=specs,
        out_specs=out_specs,
        scratch_shapes=scratch,
        compiler_params=pltpu.CompilerParams(vmem_limit_bytes=vmem),
        cost_estimate=pl.CostEstimate(flops=1000, bytes_accessed=1000, transcendentals=0),
    )


def along_x(value, step):
    devices = lax.axis_size("tp")
    return lax.ppermute(
        value, "tp", [(at, (at + CORES * step) % devices) for at in range(devices)]
    )


def along_y(value, step):
    pairs = []
    for at in range(lax.axis_size("seq")):
        y = at % ALONG_Y
        pairs.append((at, at - y + (y + step) % ALONG_Y))
    return lax.ppermute(value, "seq", pairs)


def per_device(inner_x, in_b, in_c, log_decay, doc_lengths, out_grad, w_b, w_c):
    tokens = inner_x.shape[0]
    devices = lax.axis_size("seq")
    rows = WIDE // devices
    columns = w_b.shape[0] // lax.axis_size("tp")
    local = (doc_lengths, log_decay, inner_x, in_b, out_grad, in_c)
    dma = pltpu.SemaphoreType.DMA
    shape = jax.ShapeDtypeStruct
    held = [pltpu.SMEM(doc_lengths.shape, doc_lengths.dtype)] + [
        pltpu.VMEM(a.shape, a.dtype) for a in local[1:]
    ]
    summary = call(
        summary_kernel,
        shape((devices, 2 * rows + 8, STATE), LOW),
        [HBM] * 6,
        LARGE_VMEM,
        BLOCK,
        held + [dma((6,))],
    )(*local)
    both = (CORES * columns, 2 * STATE)

    def stage(kernel, piece, arrays, count, after):
        return call(
            kernel,
            [shape(piece, LOW)] * arrays,
            [HBM] * 3,
            LARGE_VMEM,
            [HBM] * arrays,
            [pltpu.VMEM(piece, LOW)] * arrays + [dma((2 * count,)), dma((count,))],
        )(after, w_b, w_c)

    ways = (1, 3)
    [far] = stage(stage_far_kernel, (columns, 2 * STATE), 1, 1, summary)
    fetched = along_x(far, 2)
    given = [
        along_y(piece, way)
        for piece, way in zip((fetched[: columns // 2], fetched[columns // 2 :]), ways)
    ]
    own = call(
        own_kernel,
        shape(both, LOW),
        [HBM] * 2,
        LARGE_VMEM,
        HBM,
        [pltpu.VMEM(both, LOW), dma((4,)), dma((2,))],
    )(w_b, w_c)
    summary = lax.all_to_all(summary, "seq", 0, 0)
    grad_x, terms, leave_cols = call(
        local_kernel,
        [
            shape((tokens, WIDE), FULL),
            shape((tokens, 2 * WIDE + 4 * STATE), LOW),
            shape((tokens, 2 * HEADS), LOW),
        ],
        [HBM] * 6,
        16 * MIB,
        [BLOCK] * 3,
        held + [dma((6,))],
    )(*local)
    near = stage(stage_near_kernel, both, 2, 4, leave_cols)
    up, down = [along_x(piece, way) for piece, way in zip(near, ways)]
    edges = call(
        scan_kernel,
        shape((devices, 2 * rows, STATE), LOW),
        [BLOCK] + [HBM] * 2,
        4 * MIB,
    )(summary, leave_cols, fetched)
    edges = lax.all_to_all(edges, "seq", 0, 0)
    grad_bc = call(
        grad_bc_kernel,
        shape((tokens, 2 * STATE), LOW),
        [BLOCK, BLOCK, HBM, HBM],
        8 * MIB,
    )(terms, edges, up, down)
    others = [along_x(grad_bc, step) for step in (1, 2, 3)]
    grad_x, done = call(
        grad_x_kernel,
        [shape((tokens, WIDE), LOW), shape((8, LANES), FULL)],
        [BLOCK] * 4,
        8 * MIB,
        [BLOCK] * 2,
    )(in_b, leave_cols, grad_x, edges)

    def project(sibling, kind):
        return call(
            functools.partial(project_kernel, sibling=sibling),
            shape((tokens, columns), kind),
            [BLOCK] * 7 + [HBM] * 3 + [BLOCK],
            16 * MIB,
            BLOCK,
            [
                pltpu.VMEM((columns, 2 * STATE), LOW),
                pltpu.VMEM((tokens, columns), FULL),
                dma((2,)),
            ],
        )(grad_bc, *others, own, up, down, fetched, *given, done)

    partner = [(at, at ^ 1) for at in range(lax.axis_size("tp"))]
    received = lax.ppermute(project(True, LOW), "tp", partner)
    grad_input = call(sum_kernel, shape((tokens, columns), LOW), [BLOCK] * 2, 8 * MIB)(
        project(False, FULL), received
    )
    return grad_x, grad_input


def solution(mesh):
    placed = (
        P("seq", "tp"),
        P("seq", "tp"),
        P("seq", "tp"),
        P("tp", "seq"),
        P(),
        P("seq", "tp"),
        P(None, "tp"),
        P(None, "tp"),
    )
    return jax.shard_map(
        per_device,
        mesh=mesh,
        in_specs=placed,
        out_specs=(P("seq", "tp"), P("seq", "tp")),
        check_vma=False,
    )
```

```python
import functools

import jax
import jax.numpy as jnp
from jax import lax
from jax.experimental import pallas as pl
from jax.experimental.pallas import tpu as pltpu
from jax.sharding import PartitionSpec as P

HEAD_DIM = 64
STATE = 128
SPAN = 128
HEADS = 16
LANES = 128
WIDE = HEADS * HEAD_DIM
PAIRS = WIDE // LANES
CORES = 2
ALONG_Y = 4
LOW = jnp.bfloat16
FULL = jnp.float32
NN = (((1,), (0,)), ((), ()))
NT = (((1,), (1,)), ((), ()))
TN = (((0,), (0,)), ((), ()))
MIB = 1024 * 1024
LARGE_VMEM = 56 * MIB


def mul(a, b, dims=NN):
    return lax.dot_general(a, b, dims, preferred_element_type=FULL)


def iota(shape, axis):
    return lax.broadcasted_iota(jnp.int32, shape, axis)


def doc_of(positions, ends):
    return sum((positions >= end).astype(jnp.int32) for end in ends)


def doc_ends(lengths_ref):
    first = lengths_ref[0]
    second = first + lengths_ref[1]
    return (first, second, second + lengths_ref[2])


def token_vectors(log_ref, lengths_ref):
    tokens = log_ref.shape[1]
    first_row = lax.axis_index("seq") * tokens
    ends = doc_ends(lengths_ref)
    upper = (iota((tokens, tokens), 0) <= iota((tokens, tokens), 1)).astype(FULL)
    cumulative = lax.dot_general(
        log_ref[...], upper, NN, precision=lax.Precision.HIGHEST, preferred_element_type=FULL
    )
    docs = doc_of(first_row + iota((HEADS, tokens), 1), ends)
    prior = jnp.where(first_row > 0, doc_of(first_row - 1, ends), -1)
    last = doc_of(first_row + tokens - 1, ends)
    cum_last = cumulative[:, tokens - 1 :]
    enter = jnp.where(docs == prior, jnp.exp(cumulative), 0.0)
    leave = jnp.where(docs == last, jnp.exp(cum_last - cumulative), 0.0)
    total = jnp.where(last == prior, jnp.exp(cum_last), 0.0)
    return first_row, ends, cumulative, docs, enter, leave, total


def split_columns(rows):
    high = rows.astype(LOW).astype(FULL)
    both = jnp.concatenate([high, rows - high], axis=0)
    return both.T.astype(LOW)


def spread(columns, low, width):
    head = (low + iota((2 * HEADS, width), 1)) // HEAD_DIM
    pick = (head == iota((2 * HEADS, width), 0) % HEADS).astype(FULL).astype(LOW)
    return mul(columns, pick)


def fetch(pairs, sems):
    copies = [
        pltpu.make_async_copy(source, target, sems.at[at])
        for at, (source, target) in enumerate(pairs)
    ]
    for copy in copies:
        copy.start()
    return copies


def summary_kernel(
    lengths_hbm,
    log_hbm,
    x_hbm,
    b_hbm,
    dy_hbm,
    c_hbm,
    out_ref,
    lengths_ref,
    log_ref,
    x_ref,
    b_ref,
    dy_ref,
    c_ref,
    sems,
):
    loads = fetch(
        [
            (lengths_hbm, lengths_ref),
            (log_hbm, log_ref),
            (x_hbm, x_ref),
            (b_hbm, b_ref),
            (dy_hbm, dy_ref),
            (c_hbm, c_ref),
        ],
        sems,
    )
    slices = out_ref.shape[0]
    rows = WIDE // slices
    loads[0].wait()
    loads[1].wait()
    _, _, _, _, enter, leave, total = token_vectors(log_ref, lengths_ref)
    enter_cols = split_columns(enter)
    leave_cols = split_columns(leave)
    width = 2 * LANES
    for side, (wide_ref, narrow_ref, cols) in enumerate(
        ((x_ref, b_ref, leave_cols), (dy_ref, c_ref, enter_cols))
    ):
        loads[2 + 2 * side].wait()
        loads[3 + 2 * side].wait()
        narrow = narrow_ref[...]
        for chunk in range(WIDE // width):
            low = chunk * width
            at = slice(low // rows, (low + width) // rows)
            weighted = wide_ref[:, low : low + width].astype(FULL) * spread(cols, low, width)
            product = mul(weighted.astype(LOW), narrow, TN).astype(LOW)
            out_ref[at, side * rows : (side + 1) * rows, :] = product.reshape(
                width // rows, rows, STATE
            )
    total = jnp.broadcast_to(total, (HEADS, STATE))
    high = total.astype(LOW).astype(FULL)
    per_head = slices // HEADS
    for head in range(HEADS):
        rest = jnp.broadcast_to((total - high)[head : head + 1], (8, STATE))
        tile = jnp.where(iota((8, STATE), 0) == 0, high[head : head + 1], rest).astype(LOW)
        for part in range(per_head):
            out_ref[head * per_head + part, 2 * rows : 2 * rows + 8, :] = tile


def fetches_sibling():
    return lax.rem(lax.axis_index("seq"), 2) == 0


def pass_through(pieces, w_b_hbm, w_c_hbm, load_sems, sent_sems):
    pairs = []
    for rows, held_ref, _ in pieces:
        pairs.append((w_b_hbm.at[rows, :], held_ref.at[:, pl.ds(0, STATE)]))
        pairs.append((w_c_hbm.at[rows, :], held_ref.at[:, pl.ds(STATE, STATE)]))
    loads = fetch(pairs, load_sems)
    sends = []
    for at, (_, held_ref, sent_ref) in enumerate(pieces):
        loads[2 * at].wait()
        loads[2 * at + 1].wait()
        sends.append(pltpu.make_async_copy(held_ref, sent_ref, sent_sems.at[at]))
        sends[-1].start()
    for send in sends:
        send.wait()


def stage_far_kernel(_, w_b_hbm, w_c_hbm, sent_ref, held_ref, *sems):
    columns = sent_ref.shape[0]
    me = lax.axis_index("tp")
    core, chips = lax.rem(me, CORES), lax.axis_size("tp") // CORES
    half = lax.rem(core + 1 + lax.rem(lax.axis_index("seq"), 2), CORES)
    row = (lax.rem(me // CORES + 2, chips) * CORES + half) * columns
    from_row = pl.ds(pl.multiple_of(row, columns), columns)
    pass_through([(from_row, held_ref, sent_ref)], w_b_hbm, w_c_hbm, *sems)


def stage_near_kernel(_, w_b_hbm, w_c_hbm, *refs):
    sent_refs, held_refs, sems = refs[:3], refs[3:6], refs[6:]
    columns = sent_refs[0].shape[0] // CORES
    me = lax.axis_index("tp")
    core, chips = lax.rem(me, CORES), lax.axis_size("tp") // CORES
    pieces = []
    for step, held_ref, sent_ref in zip((1, 3, 0), held_refs, sent_refs):
        first = lax.rem(me // CORES + step, chips) * CORES
        for which, other in enumerate((1 - core, core)):
            row = pl.multiple_of((first + other) * columns, columns)
            to = pl.ds(which * columns, columns)
            pieces.append((pl.ds(row, columns), held_ref.at[to, :], sent_ref.at[to, :]))
    pass_through(pieces, w_b_hbm, w_c_hbm, *sems)


def scan_kernel(in_ref, *refs):
    out_ref = refs[-1]
    devices, rows = out_ref.shape[0], out_ref.shape[1] // 2
    decays = []
    for at in range(devices):
        pair = in_ref[at, 2 * rows : 2 * rows + 8, :].astype(FULL)
        decays.append(pair[0:1] + pair[1:2])
    state = jnp.zeros((rows, STATE), FULL)
    for at in range(devices):
        out_ref[at, 0:rows, :] = state.astype(LOW)
        state = decays[at] * state + in_ref[at, 0:rows, :].astype(FULL)
    state = jnp.zeros((rows, STATE), FULL)
    for at in reversed(range(devices)):
        out_ref[at, rows : 2 * rows, :] = state.astype(LOW)
        state = decays[at] * state + in_ref[at, rows : 2 * rows, :].astype(FULL)


def local_kernel(
    lengths_hbm,
    log_hbm,
    x_hbm,
    b_hbm,
    dy_hbm,
    c_hbm,
    grad_x_ref,
    terms_ref,
    leave_ref,
    lengths_ref,
    log_ref,
    x_ref,
    b_ref,
    dy_ref,
    c_ref,
    sems,
):
    loads = fetch(
        [
            (lengths_hbm, lengths_ref),
            (log_hbm, log_ref),
            (x_hbm, x_ref),
            (b_hbm, b_ref),
            (dy_hbm, dy_ref),
            (c_hbm, c_ref),
        ],
        sems,
    )
    for load in loads:
        load.wait()
    first_row, ends, cumulative, docs, enter, leave, _ = token_vectors(log_ref, lengths_ref)
    enter_cols, leave_cols = split_columns(enter), split_columns(leave)
    leave_ref[...] = leave_cols
    cum_cols = cumulative.T
    middle = doc_of(first_row + SPAN - 1, ends)
    cum_middle = cumulative[:, SPAN - 1 : SPAN]
    leave_first = jnp.where(
        docs[:, :SPAN] == middle, jnp.exp(cum_middle - cumulative[:, :SPAN]), 0.0
    )
    enter_second = jnp.where(
        docs[:, SPAN:] == middle, jnp.exp(cumulative[:, SPAN:] - cum_middle), 0.0
    )
    leave_first, enter_second = split_columns(leave_first), split_columns(enter_second)
    b, c = b_ref[...], c_ref[...]
    scores = mul(b, c, NT)
    cross_scores = scores[:SPAN, SPAN:].astype(LOW)
    is_left = iota((SPAN, LANES), 1) < HEAD_DIM
    masks = []
    for number in range(2):
        base = first_row + number * SPAN
        same = doc_of(base + iota((SPAN, SPAN), 0), ends) == doc_of(
            base + iota((SPAN, SPAN), 1), ends
        )
        masks.append(same & (iota((SPAN, SPAN), 0) <= iota((SPAN, SPAN), 1)))

    def halves(value):
        zero = jnp.zeros_like(value)
        return jnp.concatenate(
            [jnp.where(is_left, value, zero), jnp.where(is_left, zero, value)], axis=0
        )

    mixed = [jnp.zeros((SPAN, SPAN), FULL), jnp.zeros((SPAN, SPAN), FULL)]
    mixed_cross = jnp.zeros((SPAN, SPAN), FULL)
    for pair in range(PAIRS):
        low = pair * LANES
        x, dy = x_ref[:, low : low + LANES], dy_ref[:, low : low + LANES]
        for side, (wide, cols) in enumerate(((x, leave_cols), (dy, enter_cols))):
            weighted = (wide.astype(FULL) * spread(cols, low, LANES)).astype(LOW)
            terms_ref[:, side * WIDE + low : side * WIDE + low + LANES] = weighted
        first_wide = spread(leave_first, low, LANES)
        x_first = (x[:SPAN].astype(FULL) * first_wide).astype(LOW)
        dy_second = (dy[SPAN:].astype(FULL) * spread(enter_second, low, LANES)).astype(LOW)
        mixed_cross += mul(x_first, dy_second, NT)
        pieces = [first_wide * mul(cross_scores, dy_second), 0.0]
        for number in range(2):
            span = slice(number * SPAN, (number + 1) * SPAN)
            inner = mul(halves(x[span]), dy[span], NT)
            low_scores = []
            for side in range(2):
                head = 2 * pair + side
                gaps = cumulative[head : head + 1, span] - cum_cols[span, head : head + 1]
                within = jnp.exp(jnp.where(masks[number], gaps, -1e30))
                mixed[number] += within * inner[side * SPAN : (side + 1) * SPAN]
                low_scores.append((within * scores[span, span]).astype(LOW))
            grad_x_ref[span, low : low + LANES] = pieces[number] + mul(
                jnp.concatenate(low_scores, axis=1), halves(dy[span])
            )
    nothing = jnp.zeros((SPAN, SPAN), FULL)
    table = jnp.concatenate(
        [
            jnp.concatenate([mixed[0], mixed_cross], axis=1),
            jnp.concatenate([nothing, mixed[1]], axis=1),
        ],
        axis=0,
    )
    for side, part in enumerate((mul(table.astype(LOW), c), mul(table.T.astype(LOW), b))):
        high = part.astype(LOW)
        low = 2 * (WIDE + side * STATE)
        terms_ref[:, low : low + STATE] = high
        terms_ref[:, low + STATE : low + 2 * STATE] = (part - high.astype(FULL)).astype(LOW)


def grad_bc_kernel(terms_ref, edge_ref, *refs):
    out_ref = refs[-1]
    rows = edge_ref.shape[1] // 2
    for side in range(2):
        which = slice(rows, 2 * rows) if side == 0 else slice(0, rows)
        edge = edge_ref[:, which, :].reshape(WIDE, STATE)
        total = mul(terms_ref[:, side * WIDE : (side + 1) * WIDE], edge)
        low = 2 * (WIDE + side * STATE)
        for part in range(2):
            total += terms_ref[:, low + part * STATE : low + (part + 1) * STATE].astype(FULL)
        out_ref[:, side * STATE : (side + 1) * STATE] = total.astype(LOW)


def grad_x_kernel(b_ref, leave_ref, local_ref, edge_ref, out_ref, done_ref):
    done_ref[...] = jnp.zeros_like(done_ref)
    rows = edge_ref.shape[1] // 2
    width = 2 * LANES
    for chunk in range(WIDE // width):
        low = chunk * width
        at = slice(low // rows, (low + width) // rows)
        end = edge_ref[at, rows : 2 * rows, :].reshape(width, STATE)
        later = spread(leave_ref[...], low, width) * mul(b_ref[...], end, NT)
        out_ref[:, low : low + width] = (local_ref[:, low : low + width] + later).astype(LOW)


def project_kernel(*refs, sibling):
    grads, (own, up, down), fetched, given = refs[:4], refs[4:7], refs[7], refs[8:10]
    _, out_ref, held_ref, total_ref, sems = refs[10:]
    columns = out_ref.shape[1]
    part = columns // 2
    here = fetches_sibling() if sibling else jnp.logical_not(fetches_sibling())

    def copies(pieces):
        return [
            pltpu.make_async_copy(piece, held_ref.at[pl.ds(at * part, part), :], sems.at[at])
            for at, piece in enumerate(pieces)
        ]

    def start(pieces):
        for copy in copies(pieces):
            copy.start()

    fetched = [fetched.at[pl.ds(at * part, part), :] for at in range(2)]
    pl.when(here)(lambda: start(fetched))
    pl.when(jnp.logical_not(here))(lambda: start(given))
    width = 2 * LANES
    first = 0 if sibling else columns
    for low in range(0, columns, width):
        half = slice(first + low, first + low + width)
        total = mul(grads[0][...], own[half, :], NT)
        total += mul(grads[2][...], up[half, :], NT)
        total_ref[:, low : low + width] = total + mul(grads[3][...], down[half, :], NT)
    for copy in copies(fetched):
        copy.wait()
    for low in range(0, columns, width):
        to = slice(low, low + width)
        total = total_ref[:, to] + mul(grads[1][...], held_ref[to, :], NT)
        out_ref[:, to] = total.astype(out_ref.dtype)


def sum_kernel(kept_ref, received_ref, out_ref):
    out_ref[...] = (kept_ref[...] + received_ref[...].astype(FULL)).astype(LOW)


BLOCK = pl.BlockSpec(memory_space=pltpu.VMEM)
HBM = pl.BlockSpec(memory_space=pltpu.HBM)


def call(body, out_shape, specs, vmem, out_specs=BLOCK, scratch=()):
    return pl.pallas_call(
        body,
        out_shape=out_shape,
        in_specs=specs,
        out_specs=out_specs,
        scratch_shapes=scratch,
        compiler_params=pltpu.CompilerParams(vmem_limit_bytes=vmem),
        cost_estimate=pl.CostEstimate(flops=1000, bytes_accessed=1000, transcendentals=0),
    )


def along_x(value, step):
    devices = lax.axis_size("tp")
    return lax.ppermute(
        value, "tp", [(at, (at + CORES * step) % devices) for at in range(devices)]
    )


def along_y(value, step):
    pairs = []
    for at in range(lax.axis_size("seq")):
        y = at % ALONG_Y
        pairs.append((at, at - y + (y + step) % ALONG_Y))
    return lax.ppermute(value, "seq", pairs)


def per_device(inner_x, in_b, in_c, log_decay, doc_lengths, out_grad, w_b, w_c):
    tokens = inner_x.shape[0]
    devices = lax.axis_size("seq")
    rows = WIDE // devices
    columns = w_b.shape[0] // lax.axis_size("tp")
    local = (doc_lengths, log_decay, inner_x, in_b, out_grad, in_c)
    dma = pltpu.SemaphoreType.DMA
    shape = jax.ShapeDtypeStruct
    held = [pltpu.SMEM(doc_lengths.shape, doc_lengths.dtype)] + [
        pltpu.VMEM(a.shape, a.dtype) for a in local[1:]
    ]
    summary = call(
        summary_kernel,
        shape((devices, 2 * rows + 8, STATE), LOW),
        [HBM] * 6,
        LARGE_VMEM,
        BLOCK,
        held + [dma((6,))],
    )(*local)
    both = (CORES * columns, 2 * STATE)

    def stage(kernel, piece, arrays, count, after):
        return call(
            kernel,
            [shape(piece, LOW)] * arrays,
            [HBM] * 3,
            LARGE_VMEM,
            [HBM] * arrays,
            [pltpu.VMEM(piece, LOW)] * arrays + [dma((2 * count,)), dma((count,))],
        )(after, w_b, w_c)

    ways = (1, 3)
    [far] = stage(stage_far_kernel, (columns, 2 * STATE), 1, 1, summary)
    fetched = along_x(far, 2)
    given = [
        along_y(piece, way)
        for piece, way in zip((fetched[: columns // 2], fetched[columns // 2 :]), ways)
    ]
    summary = lax.all_to_all(summary, "seq", 0, 0)
    grad_x, terms, leave_cols = call(
        local_kernel,
        [
            shape((tokens, WIDE), FULL),
            shape((tokens, 2 * WIDE + 4 * STATE), LOW),
            shape((tokens, 2 * HEADS), LOW),
        ],
        [HBM] * 6,
        16 * MIB,
        [BLOCK] * 3,
        held + [dma((6,))],
    )(*local)
    *near, own = stage(stage_near_kernel, both, 3, 6, leave_cols)
    up, down = [along_x(piece, way) for piece, way in zip(near, ways)]
    edges = call(
        scan_kernel,
        shape((devices, 2 * rows, STATE), LOW),
        [BLOCK] + [HBM] * 2,
        4 * MIB,
    )(summary, leave_cols, fetched)
    edges = lax.all_to_all(edges, "seq", 0, 0)
    grad_bc = call(
        grad_bc_kernel,
        shape((tokens, 2 * STATE), LOW),
        [BLOCK, BLOCK, HBM, HBM],
        8 * MIB,
    )(terms, edges, up, down)
    others = [along_x(grad_bc, step) for step in (2, 1, 3)]
    grad_x, done = call(
        grad_x_kernel,
        [shape((tokens, WIDE), LOW), shape((8, LANES), FULL)],
        [BLOCK] * 4,
        8 * MIB,
        [BLOCK] * 2,
    )(in_b, leave_cols, grad_x, edges)

    def project(sibling, kind):
        return call(
            functools.partial(project_kernel, sibling=sibling),
            shape((tokens, columns), kind),
            [BLOCK] * 7 + [HBM] * 3 + [BLOCK],
            16 * MIB,
            BLOCK,
            [
                pltpu.VMEM((columns, 2 * STATE), LOW),
                pltpu.VMEM((tokens, columns), FULL),
                dma((2,)),
            ],
        )(grad_bc, *others, own, up, down, fetched, *given, done)

    partner = [(at, at ^ 1) for at in range(lax.axis_size("tp"))]
    received = lax.ppermute(project(True, LOW), "tp", partner)
    grad_input = call(sum_kernel, shape((tokens, columns), LOW), [BLOCK] * 2, 8 * MIB)(
        project(False, FULL), received
    )
    return grad_x, grad_input


def solution(mesh):
    placed = (
        P("seq", "tp"),
        P("seq", "tp"),
        P("seq", "tp"),
        P("tp", "seq"),
        P(),
        P("seq", "tp"),
        P(None, "tp"),
        P(None, "tp"),
    )
    return jax.shard_map(
        per_device,
        mesh=mesh,
        in_specs=placed,
        out_specs=(P("seq", "tp"), P("seq", "tp")),
        check_vma=False,
    )
```

```python
import functools

import jax
import jax.numpy as jnp
from jax import lax
from jax.experimental import pallas as pl
from jax.experimental.pallas import tpu as pltpu
from jax.sharding import PartitionSpec as P

HEAD_DIM = 64
STATE = 128
SPAN = 128
HEADS = 16
LANES = 128
WIDE = HEADS * HEAD_DIM
PAIRS = WIDE // LANES
CORES = 2
ALONG_Y = 4
LOW = jnp.bfloat16
FULL = jnp.float32
NN = (((1,), (0,)), ((), ()))
NT = (((1,), (1,)), ((), ()))
TN = (((0,), (0,)), ((), ()))
MIB = 1024 * 1024
LARGE_VMEM = 56 * MIB


def mul(a, b, dims=NN):
    return lax.dot_general(a, b, dims, preferred_element_type=FULL)


def iota(shape, axis):
    return lax.broadcasted_iota(jnp.int32, shape, axis)


def doc_of(positions, ends):
    return sum((positions >= end).astype(jnp.int32) for end in ends)


def doc_ends(lengths_ref):
    first = lengths_ref[0]
    second = first + lengths_ref[1]
    return (first, second, second + lengths_ref[2])


def token_vectors(log_ref, lengths_ref):
    tokens = log_ref.shape[1]
    first_row = lax.axis_index("seq") * tokens
    ends = doc_ends(lengths_ref)
    upper = (iota((tokens, tokens), 0) <= iota((tokens, tokens), 1)).astype(FULL)
    cumulative = lax.dot_general(
        log_ref[...], upper, NN, precision=lax.Precision.HIGHEST, preferred_element_type=FULL
    )
    docs = doc_of(first_row + iota((HEADS, tokens), 1), ends)
    prior = jnp.where(first_row > 0, doc_of(first_row - 1, ends), -1)
    last = doc_of(first_row + tokens - 1, ends)
    cum_last = cumulative[:, tokens - 1 :]
    enter = jnp.where(docs == prior, jnp.exp(cumulative), 0.0)
    leave = jnp.where(docs == last, jnp.exp(cum_last - cumulative), 0.0)
    total = jnp.where(last == prior, jnp.exp(cum_last), 0.0)
    return first_row, ends, cumulative, docs, enter, leave, total


def split_columns(rows):
    high = rows.astype(LOW).astype(FULL)
    both = jnp.concatenate([high, rows - high], axis=0)
    return both.T.astype(LOW)


def spread(columns, low, width):
    head = (low + iota((2 * HEADS, width), 1)) // HEAD_DIM
    pick = (head == iota((2 * HEADS, width), 0) % HEADS).astype(FULL).astype(LOW)
    return mul(columns, pick)


def fetch(pairs, sems):
    copies = [
        pltpu.make_async_copy(source, target, sems.at[at])
        for at, (source, target) in enumerate(pairs)
    ]
    for copy in copies:
        copy.start()
    return copies


def summary_kernel(
    lengths_hbm,
    log_hbm,
    x_hbm,
    b_hbm,
    dy_hbm,
    c_hbm,
    out_ref,
    lengths_ref,
    log_ref,
    x_ref,
    b_ref,
    dy_ref,
    c_ref,
    sems,
):
    loads = fetch(
        [
            (lengths_hbm, lengths_ref),
            (log_hbm, log_ref),
            (x_hbm, x_ref),
            (b_hbm, b_ref),
            (dy_hbm, dy_ref),
            (c_hbm, c_ref),
        ],
        sems,
    )
    slices = out_ref.shape[0]
    rows = WIDE // slices
    loads[0].wait()
    loads[1].wait()
    _, _, _, _, enter, leave, total = token_vectors(log_ref, lengths_ref)
    enter_cols = split_columns(enter)
    leave_cols = split_columns(leave)
    width = 2 * LANES
    for side, (wide_ref, narrow_ref, cols) in enumerate(
        ((x_ref, b_ref, leave_cols), (dy_ref, c_ref, enter_cols))
    ):
        loads[2 + 2 * side].wait()
        loads[3 + 2 * side].wait()
        narrow = narrow_ref[...]
        for chunk in range(WIDE // width):
            low = chunk * width
            at = slice(low // rows, (low + width) // rows)
            weighted = wide_ref[:, low : low + width].astype(FULL) * spread(cols, low, width)
            product = mul(weighted.astype(LOW), narrow, TN).astype(LOW)
            out_ref[at, side * rows : (side + 1) * rows, :] = product.reshape(
                width // rows, rows, STATE
            )
    total = jnp.broadcast_to(total, (HEADS, STATE))
    high = total.astype(LOW).astype(FULL)
    per_head = slices // HEADS
    for head in range(HEADS):
        rest = jnp.broadcast_to((total - high)[head : head + 1], (8, STATE))
        tile = jnp.where(iota((8, STATE), 0) == 0, high[head : head + 1], rest).astype(LOW)
        for part in range(per_head):
            out_ref[head * per_head + part, 2 * rows : 2 * rows + 8, :] = tile


def fetches_sibling():
    return lax.rem(lax.axis_index("seq"), 2) == 0


def pass_through(pieces, w_b_hbm, w_c_hbm, load_sems, sent_sems):
    pairs = []
    for rows, held_ref, _ in pieces:
        pairs.append((w_b_hbm.at[rows, :], held_ref.at[:, pl.ds(0, STATE)]))
        pairs.append((w_c_hbm.at[rows, :], held_ref.at[:, pl.ds(STATE, STATE)]))
    loads = fetch(pairs, load_sems)
    sends = []
    for at, (_, held_ref, sent_ref) in enumerate(pieces):
        loads[2 * at].wait()
        loads[2 * at + 1].wait()
        sends.append(pltpu.make_async_copy(held_ref, sent_ref, sent_sems.at[at]))
        sends[-1].start()
    for send in sends:
        send.wait()


def stage_far_kernel(_, w_b_hbm, w_c_hbm, sent_ref, held_ref, *sems):
    columns = sent_ref.shape[0]
    me = lax.axis_index("tp")
    core, chips = lax.rem(me, CORES), lax.axis_size("tp") // CORES
    half = lax.rem(core + 1 + lax.rem(lax.axis_index("seq"), 2), CORES)
    row = (lax.rem(me // CORES + 2, chips) * CORES + half) * columns
    from_row = pl.ds(pl.multiple_of(row, columns), columns)
    pass_through([(from_row, held_ref, sent_ref)], w_b_hbm, w_c_hbm, *sems)


def stage_near_kernel(_, w_b_hbm, w_c_hbm, *refs):
    sent_refs, held_refs, sems = refs[:2], refs[2:4], refs[4:]
    columns = sent_refs[0].shape[0] // CORES
    me = lax.axis_index("tp")
    core, chips = lax.rem(me, CORES), lax.axis_size("tp") // CORES
    pieces = []
    for step, held_ref, sent_ref in zip((1, 3), held_refs, sent_refs):
        first = lax.rem(me // CORES + step, chips) * CORES
        for which, other in enumerate((1 - core, core)):
            row = pl.multiple_of((first + other) * columns, columns)
            to = pl.ds(which * columns, columns)
            pieces.append((pl.ds(row, columns), held_ref.at[to, :], sent_ref.at[to, :]))
    pass_through(pieces, w_b_hbm, w_c_hbm, *sems)


def own_kernel(w_b_hbm, w_c_hbm, out_ref, held_ref, *sems):
    columns = out_ref.shape[0] // CORES
    me = lax.axis_index("tp")
    core = lax.rem(me, CORES)
    pieces = []
    for which, other in enumerate((1 - core, core)):
        row = pl.multiple_of((me - core + other) * columns, columns)
        to = pl.ds(which * columns, columns)
        pieces.append((pl.ds(row, columns), held_ref.at[to, :], out_ref.at[to, :]))
    pass_through(pieces, w_b_hbm, w_c_hbm, *sems)


def scan_kernel(in_ref, *refs):
    out_ref = refs[-1]
    devices, rows = out_ref.shape[0], out_ref.shape[1] // 2
    decays = []
    for at in range(devices):
        pair = in_ref[at, 2 * rows : 2 * rows + 8, :].astype(FULL)
        decays.append(pair[0:1] + pair[1:2])
    state = jnp.zeros((rows, STATE), FULL)
    for at in range(devices):
        out_ref[at, 0:rows, :] = state.astype(LOW)
        state = decays[at] * state + in_ref[at, 0:rows, :].astype(FULL)
    state = jnp.zeros((rows, STATE), FULL)
    for at in reversed(range(devices)):
        out_ref[at, rows : 2 * rows, :] = state.astype(LOW)
        state = decays[at] * state + in_ref[at, rows : 2 * rows, :].astype(FULL)


def local_kernel(
    lengths_hbm,
    log_hbm,
    x_hbm,
    b_hbm,
    dy_hbm,
    c_hbm,
    grad_x_ref,
    terms_ref,
    leave_ref,
    lengths_ref,
    log_ref,
    x_ref,
    b_ref,
    dy_ref,
    c_ref,
    sems,
):
    loads = fetch(
        [
            (lengths_hbm, lengths_ref),
            (log_hbm, log_ref),
            (x_hbm, x_ref),
            (b_hbm, b_ref),
            (dy_hbm, dy_ref),
            (c_hbm, c_ref),
        ],
        sems,
    )
    for load in loads:
        load.wait()
    first_row, ends, cumulative, docs, enter, leave, _ = token_vectors(log_ref, lengths_ref)
    enter_cols, leave_cols = split_columns(enter), split_columns(leave)
    leave_ref[...] = leave_cols
    cum_cols = cumulative.T
    middle = doc_of(first_row + SPAN - 1, ends)
    cum_middle = cumulative[:, SPAN - 1 : SPAN]
    leave_first = jnp.where(
        docs[:, :SPAN] == middle, jnp.exp(cum_middle - cumulative[:, :SPAN]), 0.0
    )
    enter_second = jnp.where(
        docs[:, SPAN:] == middle, jnp.exp(cumulative[:, SPAN:] - cum_middle), 0.0
    )
    leave_first, enter_second = split_columns(leave_first), split_columns(enter_second)
    b, c = b_ref[...], c_ref[...]
    scores = mul(b, c, NT)
    cross_scores = scores[:SPAN, SPAN:].astype(LOW)
    is_left = iota((SPAN, LANES), 1) < HEAD_DIM
    masks = []
    for number in range(2):
        base = first_row + number * SPAN
        same = doc_of(base + iota((SPAN, SPAN), 0), ends) == doc_of(
            base + iota((SPAN, SPAN), 1), ends
        )
        masks.append(same & (iota((SPAN, SPAN), 0) <= iota((SPAN, SPAN), 1)))

    def halves(value):
        zero = jnp.zeros_like(value)
        return jnp.concatenate(
            [jnp.where(is_left, value, zero), jnp.where(is_left, zero, value)], axis=0
        )

    mixed = [jnp.zeros((SPAN, SPAN), FULL), jnp.zeros((SPAN, SPAN), FULL)]
    mixed_cross = jnp.zeros((SPAN, SPAN), FULL)
    for pair in range(PAIRS):
        low = pair * LANES
        x, dy = x_ref[:, low : low + LANES], dy_ref[:, low : low + LANES]
        for side, (wide, cols) in enumerate(((x, leave_cols), (dy, enter_cols))):
            weighted = (wide.astype(FULL) * spread(cols, low, LANES)).astype(LOW)
            terms_ref[:, side * WIDE + low : side * WIDE + low + LANES] = weighted
        first_wide = spread(leave_first, low, LANES)
        x_first = (x[:SPAN].astype(FULL) * first_wide).astype(LOW)
        dy_second = (dy[SPAN:].astype(FULL) * spread(enter_second, low, LANES)).astype(LOW)
        mixed_cross += mul(x_first, dy_second, NT)
        pieces = [first_wide * mul(cross_scores, dy_second), 0.0]
        for number in range(2):
            span = slice(number * SPAN, (number + 1) * SPAN)
            inner = mul(halves(x[span]), dy[span], NT)
            low_scores = []
            for side in range(2):
                head = 2 * pair + side
                gaps = cumulative[head : head + 1, span] - cum_cols[span, head : head + 1]
                within = jnp.exp(jnp.where(masks[number], gaps, -1e30))
                mixed[number] += within * inner[side * SPAN : (side + 1) * SPAN]
                low_scores.append((within * scores[span, span]).astype(LOW))
            grad_x_ref[span, low : low + LANES] = pieces[number] + mul(
                jnp.concatenate(low_scores, axis=1), halves(dy[span])
            )
    nothing = jnp.zeros((SPAN, SPAN), FULL)
    table = jnp.concatenate(
        [
            jnp.concatenate([mixed[0], mixed_cross], axis=1),
            jnp.concatenate([nothing, mixed[1]], axis=1),
        ],
        axis=0,
    )
    for side, part in enumerate((mul(table.astype(LOW), c), mul(table.T.astype(LOW), b))):
        high = part.astype(LOW)
        low = 2 * (WIDE + side * STATE)
        terms_ref[:, low : low + STATE] = high
        terms_ref[:, low + STATE : low + 2 * STATE] = (part - high.astype(FULL)).astype(LOW)


def grad_bc_kernel(terms_ref, edge_ref, *refs):
    out_ref = refs[-1]
    rows = edge_ref.shape[1] // 2
    for side in range(2):
        which = slice(rows, 2 * rows) if side == 0 else slice(0, rows)
        edge = edge_ref[:, which, :].reshape(WIDE, STATE)
        total = mul(terms_ref[:, side * WIDE : (side + 1) * WIDE], edge)
        low = 2 * (WIDE + side * STATE)
        for part in range(2):
            total += terms_ref[:, low + part * STATE : low + (part + 1) * STATE].astype(FULL)
        out_ref[:, side * STATE : (side + 1) * STATE] = total.astype(LOW)


def grad_x_kernel(b_ref, leave_ref, local_ref, edge_ref, out_ref, done_ref):
    done_ref[...] = jnp.zeros_like(done_ref)
    rows = edge_ref.shape[1] // 2
    width = 2 * LANES
    for chunk in range(WIDE // width):
        low = chunk * width
        at = slice(low // rows, (low + width) // rows)
        end = edge_ref[at, rows : 2 * rows, :].reshape(width, STATE)
        later = spread(leave_ref[...], low, width) * mul(b_ref[...], end, NT)
        out_ref[:, low : low + width] = (local_ref[:, low : low + width] + later).astype(LOW)


def project_kernel(*refs, sibling):
    grads, (own, up, down), fetched, given = refs[:4], refs[4:7], refs[7], refs[8:10]
    _, out_ref, held_ref, total_ref, sems = refs[10:]
    columns = out_ref.shape[1]
    part = columns // 2
    here = fetches_sibling() if sibling else jnp.logical_not(fetches_sibling())

    def copies(pieces):
        return [
            pltpu.make_async_copy(piece, held_ref.at[pl.ds(at * part, part), :], sems.at[at])
            for at, piece in enumerate(pieces)
        ]

    def start(pieces):
        for copy in copies(pieces):
            copy.start()

    fetched = [fetched.at[pl.ds(at * part, part), :] for at in range(2)]
    pl.when(here)(lambda: start(fetched))
    pl.when(jnp.logical_not(here))(lambda: start(given))
    width = 2 * LANES
    first = 0 if sibling else columns
    for low in range(0, columns, width):
        half = slice(first + low, first + low + width)
        total = mul(grads[0][...], own[half, :], NT)
        total += mul(grads[1][...], up[half, :], NT)
        total_ref[:, low : low + width] = total + mul(grads[3][...], down[half, :], NT)
    for copy in copies(fetched):
        copy.wait()
    for low in range(0, columns, width):
        to = slice(low, low + width)
        total = total_ref[:, to] + mul(grads[2][...], held_ref[to, :], NT)
        out_ref[:, to] = total.astype(out_ref.dtype)


def sum_kernel(kept_ref, received_ref, out_ref):
    out_ref[...] = (kept_ref[...] + received_ref[...].astype(FULL)).astype(LOW)


BLOCK = pl.BlockSpec(memory_space=pltpu.VMEM)
HBM = pl.BlockSpec(memory_space=pltpu.HBM)


def call(body, out_shape, specs, vmem, out_specs=BLOCK, scratch=()):
    return pl.pallas_call(
        body,
        out_shape=out_shape,
        in_specs=specs,
        out_specs=out_specs,
        scratch_shapes=scratch,
        compiler_params=pltpu.CompilerParams(vmem_limit_bytes=vmem),
        cost_estimate=pl.CostEstimate(flops=1000, bytes_accessed=1000, transcendentals=0),
    )


def along_x(value, step):
    devices = lax.axis_size("tp")
    return lax.ppermute(
        value, "tp", [(at, (at + CORES * step) % devices) for at in range(devices)]
    )


def along_y(value, step):
    pairs = []
    for at in range(lax.axis_size("seq")):
        y = at % ALONG_Y
        pairs.append((at, at - y + (y + step) % ALONG_Y))
    return lax.ppermute(value, "seq", pairs)


def per_device(inner_x, in_b, in_c, log_decay, doc_lengths, out_grad, w_b, w_c):
    tokens = inner_x.shape[0]
    devices = lax.axis_size("seq")
    rows = WIDE // devices
    columns = w_b.shape[0] // lax.axis_size("tp")
    local = (doc_lengths, log_decay, inner_x, in_b, out_grad, in_c)
    dma = pltpu.SemaphoreType.DMA
    shape = jax.ShapeDtypeStruct
    held = [pltpu.SMEM(doc_lengths.shape, doc_lengths.dtype)] + [
        pltpu.VMEM(a.shape, a.dtype) for a in local[1:]
    ]
    summary = call(
        summary_kernel,
        shape((devices, 2 * rows + 8, STATE), LOW),
        [HBM] * 6,
        LARGE_VMEM,
        BLOCK,
        held + [dma((6,))],
    )(*local)
    both = (CORES * columns, 2 * STATE)

    def stage(kernel, piece, arrays, count, after):
        return call(
            kernel,
            [shape(piece, LOW)] * arrays,
            [HBM] * 3,
            LARGE_VMEM,
            [HBM] * arrays,
            [pltpu.VMEM(piece, LOW)] * arrays + [dma((2 * count,)), dma((count,))],
        )(after, w_b, w_c)

    ways = (1, 3)
    [far] = stage(stage_far_kernel, (columns, 2 * STATE), 1, 1, summary)
    fetched = along_x(far, 2)
    given = [
        along_y(piece, way)
        for piece, way in zip((fetched[: columns // 2], fetched[columns // 2 :]), ways)
    ]
    own = call(
        own_kernel,
        shape(both, LOW),
        [HBM] * 2,
        LARGE_VMEM,
        HBM,
        [pltpu.VMEM(both, LOW), dma((4,)), dma((2,))],
    )(w_b, w_c)
    sent = summary
    summary = lax.all_to_all(summary, "seq", 0, 0)
    grad_x, terms, leave_cols = call(
        local_kernel,
        [
            shape((tokens, WIDE), FULL),
            shape((tokens, 2 * WIDE + 4 * STATE), LOW),
            shape((tokens, 2 * HEADS), LOW),
        ],
        [HBM] * 6,
        16 * MIB,
        [BLOCK] * 3,
        held + [dma((6,))],
    )(*local)
    near = stage(stage_near_kernel, both, 2, 4, sent)
    up, down = [along_x(piece, way) for piece, way in zip(near, ways)]
    edges = call(
        scan_kernel,
        shape((devices, 2 * rows, STATE), LOW),
        [BLOCK] + [HBM] * 2,
        4 * MIB,
    )(summary, leave_cols, fetched)
    edges = lax.all_to_all(edges, "seq", 0, 0)
    grad_bc = call(
        grad_bc_kernel,
        shape((tokens, 2 * STATE), LOW),
        [BLOCK, BLOCK, HBM, HBM],
        8 * MIB,
    )(terms, edges, up, down)
    others = [along_x(grad_bc, step) for step in (1, 2, 3)]
    grad_x, done = call(
        grad_x_kernel,
        [shape((tokens, WIDE), LOW), shape((8, LANES), FULL)],
        [BLOCK] * 4,
        8 * MIB,
        [BLOCK] * 2,
    )(in_b, leave_cols, grad_x, edges)

    def project(sibling, kind):
        return call(
            functools.partial(project_kernel, sibling=sibling),
            shape((tokens, columns), kind),
            [BLOCK] * 7 + [HBM] * 3 + [BLOCK],
            16 * MIB,
            BLOCK,
            [
                pltpu.VMEM((columns, 2 * STATE), LOW),
                pltpu.VMEM((tokens, columns), FULL),
                dma((2,)),
            ],
        )(grad_bc, *others, own, up, down, fetched, *given, done)

    partner = [(at, at ^ 1) for at in range(lax.axis_size("tp"))]
    received = lax.ppermute(project(True, LOW), "tp", partner)
    grad_input = call(sum_kernel, shape((tokens, columns), LOW), [BLOCK] * 2, 8 * MIB)(
        project(False, FULL), received
    )
    return grad_x, grad_input


def solution(mesh):
    placed = (
        P("seq", "tp"),
        P("seq", "tp"),
        P("seq", "tp"),
        P("tp", "seq"),
        P(),
        P("seq", "tp"),
        P(None, "tp"),
        P(None, "tp"),
    )
    return jax.shard_map(
        per_device,
        mesh=mesh,
        in_specs=placed,
        out_specs=(P("seq", "tp"), P("seq", "tp")),
        check_vma=False,
    )
```
